32 devices in a mesh: dp: 8 (over y, x, core), head: 4 (over z).
Axes of the slice: x: 2, y: 2, z: 4, core: 2. Of those that a mesh axis runs over, the one named last changes fastest.
Arguments:
- tokens: bfloat16 [8, 2048, 2048], P('dp', 'head'), may hold values from -6 to 6
- lengths: int32 [8], P('dp'), may hold values from 1024 to 2048, as said below
- gain_attn: float32 [2048], replicated, may hold values from 0.5 to 1.5
- w_query: bfloat16 [2048, 2048], P('dp', 'head'), may hold values from -0.125 to 0.125
- w_key: bfloat16 [2048, 2048], P('dp', 'head'), may hold values from -0.125 to 0.125
- w_value: bfloat16 [2048, 4096], P('dp', 'head'), may hold values from -0.125 to 0.125
- w_decay: bfloat16 [2048, 16], P('dp', 'head'), may hold values from -0.125 to 0.125
- w_beta: bfloat16 [2048, 16], P('dp', 'head'), may hold values from -0.125 to 0.125
- w_gate_out: bfloat16 [2048, 4096], P('dp', 'head'), may hold values from -0.125 to 0.125
- conv_query: float32 [4, 2048], replicated, may hold values from -3 to 3
- conv_key: float32 [4, 2048], replicated, may hold values from -3 to 3
- conv_value: float32 [4, 4096], replicated, may hold values from -3 to 3
- decay_log: float32 [16], replicated, may hold values from -6.9 to -3
- decay_bias: float32 [16], replicated, may hold values from -2 to 1
- gain_head: float32 [256], replicated, may hold values from 0.5 to 1.5
- w_out: bfloat16 [2048, 4096], P('dp', 'head'), may hold values from -0.1875 to 0.1875
- gain_mlp: float32 [2048], replicated, may hold values from 0.5 to 1.5
- w_gate: bfloat16 [2048, 5632], P('dp', 'head'), may hold values from -0.125 to 0.125
- w_up: bfloat16 [2048, 5632], P('dp', 'head'), may hold values from -0.125 to 0.125
- w_down: bfloat16 [2048, 5632], P('dp', 'head'), may hold values from -0.078125 to 0.078125
- cotangent: bfloat16 [8, 2048, 2048], P('dp', 'head'), may hold values from -6 to 6
Outputs:
- mixed_rows: bfloat16 [8, 2048, 2048], P('dp', 'head')
- tokens_grad: bfloat16 [8, 2048, 2048], P('dp', 'head')
- grad_gain_attn: float32 [2048], replicated
- grad_w_query: float32 [2048, 2048], P('dp', 'head')
- grad_w_key: float32 [2048, 2048], P('dp', 'head')
- grad_w_value: float32 [2048, 4096], P('dp', 'head')
- grad_w_decay: float32 [2048, 16], P('dp', 'head')
- grad_w_beta: float32 [2048, 16], P('dp', 'head')
- grad_w_gate_out: float32 [2048, 4096], P('dp', 'head')
- grad_conv_query: float32 [4, 2048], replicated
- grad_conv_key: float32 [4, 2048], replicated
- grad_conv_value: float32 [4, 4096], replicated
- grad_decay_log: float32 [16], replicated
- grad_decay_bias: float32 [16], replicated
- grad_gain_head: float32 [256], replicated
- grad_w_out: float32 [2048, 4096], P('dp', 'head')
- grad_gain_mlp: float32 [2048], replicated
- grad_w_gate: float32 [2048, 5632], P('dp', 'head')
- grad_w_up: float32 [2048, 5632], P('dp', 'head')
- grad_w_down: float32 [2048, 5632], P('dp', 'head')
The draws below stay inside these ranges and needn't reach their ends.
Inputs may be any that keep to these rules, and one draw needn't show every extreme that they name: `lengths`: in every aligned pair of rows (rows 0 and 1, 2 and 3, and so on) one row has all 2048 positions valid.
All inputs are finite; a program needn't handle non-finite values.
Results may differ from the reference program's by a relative error of at most 0.02.
Values may be sent and summed in bfloat16 or wider, within the bound.
No kernel may reach another device: no remote copies, remote signals or barrier semaphores. Data moves between devices by JAX's collectives and lax.ppermute only.
A program may use at most 448 MiB of HBM per device.

```python
import jax
import jax.numpy as jnp
from jax import lax

D = 2048
HEADS = 16
DK = 128
DV = 256
FF = 5632
CONV = 4
SPAN = 64
ROWS_G = 1
L = 2048
ROWS = 8


def draw_lengths(key, part):
    key = jax.random.fold_in(key, 7)
    first_key, second_key = jax.random.split(key)
    base = jax.random.randint(first_key, (ROWS,), L // 2, L + 1, dtype=jnp.int32)
    chosen = jax.random.randint(second_key, (ROWS // 2,), 0, 2, dtype=jnp.int32)
    slot_index = jnp.arange(ROWS, dtype=jnp.int32) % 2
    is_full = slot_index == jnp.repeat(chosen, 2)
    return jnp.where(is_full, L, base).astype(jnp.int32)


def steps_of(stream_key, dims, cuts, smallest, largest):
    gain = 1.0
    for axis_at, blocks in cuts:
        heights = jax.random.uniform(jax.random.fold_in(jax.random.fold_in(stream_key, 6), axis_at), (blocks,), jnp.float32, smallest / len(cuts), largest / len(cuts))
        gain = gain * jnp.repeat(jnp.exp(heights), dims[axis_at] // blocks).reshape((-1,) + (1,) * (len(dims) - 1 - axis_at))
    return gain


def scatter_about(own_key, shape, width, bound, shards=(), kind=jnp.bfloat16):
    factor_of = steps_of(own_key, shape, shards, -0.22, 0.18) if shards else 1.0
    entries = jax.random.normal(own_key, shape, jnp.float32) * width * factor_of
    return jnp.minimum(jnp.maximum(entries, -bound), bound).astype(kind)


def setup_inputs(seed: int = 0) -> dict:
    streams_of = jax.random.split(jax.random.key(seed), 22)
    tokens = scatter_about(streams_of[0], (ROWS, L, D), 1.0, 6.0, ((0, 8), (1, 4)))
    lengths = draw_lengths(jax.random.fold_in(streams_of[21], 71), 0)
    gain_attn = jnp.clip(1.0 + 0.1 * jax.random.normal(streams_of[2], (D,), jnp.float32), 0.5, 1.5)
    w_query = scatter_about(streams_of[3], (D, HEADS * DK), D ** -0.5, 0.125, ((0, 8), (1, 4)))
    w_key = scatter_about(streams_of[4], (D, HEADS * DK), D ** -0.5, 0.125, ((0, 8), (1, 4)))
    w_value = scatter_about(streams_of[5], (D, HEADS * DV), D ** -0.5, 0.125, ((0, 8), (1, 4)))
    w_decay = scatter_about(streams_of[6], (D, HEADS), D ** -0.5, 0.125, ((0, 8), (1, 4)))
    w_beta = scatter_about(streams_of[7], (D, HEADS), D ** -0.5, 0.125, ((0, 8), (1, 4)))
    w_gate_out = scatter_about(streams_of[8], (D, HEADS * DV), D ** -0.5, 0.125, ((0, 8), (1, 4)))
    conv_query = scatter_about(streams_of[9], (CONV, HEADS * DK), CONV ** -0.5, 3.0, (), jnp.float32)
    conv_key = scatter_about(streams_of[10], (CONV, HEADS * DK), CONV ** -0.5, 3.0, (), jnp.float32)
    conv_value = scatter_about(streams_of[11], (CONV, HEADS * DV), CONV ** -0.5, 3.0, (), jnp.float32)
    decay_log = jnp.clip(jax.random.uniform(streams_of[12], (HEADS,), jnp.float32, -6.9, -3.0), -6.9, -3.0)
    decay_bias = jnp.clip(jax.random.uniform(streams_of[13], (HEADS,), jnp.float32, -2.0, 1.0), -2.0, 1.0)
    gain_head = jnp.clip(1.0 + 0.1 * jax.random.normal(streams_of[14], (DV,), jnp.float32), 0.5, 1.5)
    w_out = scatter_about(streams_of[15], (D, HEADS * DV), (HEADS * DV // 4) ** -0.5, 0.1875, ((0, 8), (1, 4)))
    gain_mlp = jnp.clip(1.0 + 0.1 * jax.random.normal(streams_of[16], (D,), jnp.float32), 0.5, 1.5)
    w_gate = scatter_about(streams_of[17], (D, FF), D ** -0.5, 0.125, ((0, 8), (1, 4)))
    w_up = scatter_about(streams_of[18], (D, FF), D ** -0.5, 0.125, ((0, 8), (1, 4)))
    w_down = scatter_about(streams_of[19], (D, FF), FF ** -0.5, 0.078125, ((0, 8), (1, 4)))
    cotangent = scatter_about(streams_of[20], (ROWS, L, D), 1.0, 6.0, ((0, 8), (1, 4)))
    return {"tokens": tokens, "lengths": lengths, "gain_attn": gain_attn, "w_query": w_query, "w_key": w_key, "w_value": w_value, "w_decay": w_decay, "w_beta": w_beta, "w_gate_out": w_gate_out, "conv_query": conv_query, "conv_key": conv_key, "conv_value": conv_value, "decay_log": decay_log, "decay_bias": decay_bias, "gain_head": gain_head, "w_out": w_out, "gain_mlp": gain_mlp, "w_gate": w_gate, "w_up": w_up, "w_down": w_down, "cotangent": cotangent}


NORM_EPS = 1e-06

@jax.custom_vjp
def low(v):
    return lax.optimization_barrier(v.astype(jnp.bfloat16)).astype(jnp.float32)

@jax.custom_vjp
def low_back(v):
    return v

def low_keep(v):
    return (low(v), None)

def low_pass(kept, grad):
    return (grad,)

def back_keep(v):
    return (v, None)

def back_low(kept, grad):
    return (low(grad),)
low.defvjp(low_keep, low_pass)
low_back.defvjp(back_keep, back_low)

def rms_norm(values_in, gain_vec):
    return values_in * lax.rsqrt(lax.optimization_barrier(jnp.mean(values_in * values_in, axis=-1, keepdims=True)) + NORM_EPS) * gain_vec

def causal_conv(signal, kernel):
    tap_count = kernel.shape[0]
    length = signal.shape[1]
    padded = jnp.pad(signal, ((0, 0), (tap_count - 1, 0), (0, 0)))
    result = jnp.zeros_like(signal)
    for offset in range(tap_count):
        result = result + kernel[offset] * padded[:, offset:offset + length]
    return result

def unit_lower_inverse(system):
    highest = lax.Precision.HIGHEST
    lead = system.shape[:-2]
    order = system.shape[-1]
    blocks = jnp.ones(lead + (order, 1, 1), jnp.float32)
    size = 1
    while size < order:
        count = order // (2 * size)
        tiles = system.reshape(lead + (count, 2 * size, count, 2 * size))
        tiles = jnp.moveaxis(jnp.diagonal(tiles, axis1=-4, axis2=-2), -1, -3)
        lower_left = tiles[..., size:, :size]
        upper = blocks[..., 0::2, :, :]
        bottom = blocks[..., 1::2, :, :]
        corner = -jnp.matmul(jnp.matmul(bottom, lower_left, precision=highest), upper, precision=highest)
        zeros = jnp.zeros_like(corner)
        top_row = jnp.concatenate([upper, zeros], axis=-1)
        bottom_row = jnp.concatenate([corner, bottom], axis=-1)
        blocks = jnp.concatenate([top_row, bottom_row], axis=-2)
        size = size * 2
    return blocks.reshape(lead + (order, order))

def span_step(states, block_in):
    queries, keys_in, values, decays, betas = block_in
    highest = lax.Precision.HIGHEST
    cumulative = jnp.cumsum(decays, axis=0).T
    q_head = queries.transpose(1, 0, 2)
    k_head = keys_in.transpose(1, 0, 2)
    v_head = values.transpose(1, 0, 2)
    positions = jnp.arange(SPAN)
    inclusive = positions[:, None] >= positions[None, :]
    strictly = positions[:, None] > positions[None, :]
    spread = cumulative[:, :, None] - cumulative[:, None, :]
    within = jnp.where(inclusive, jnp.exp(jnp.where(inclusive, spread, 0.0)), 0.0)
    below = jnp.where(strictly, within, 0.0)
    key_gram = jnp.einsum('hid,hjd->hij', k_head, k_head, precision=highest)
    beta_head = betas.T
    system = jnp.eye(SPAN, dtype=jnp.float32) + beta_head[:, :, None] * key_gram * below
    leading = jnp.exp(cumulative)
    right_side = jnp.concatenate([(beta_head * leading)[:, :, None] * k_head, beta_head[:, :, None] * v_head], axis=2)
    inverse = unit_lower_inverse(system)
    solved = jnp.einsum('hij,hje->hie', inverse, right_side, precision=highest)
    w_part = solved[:, :, :DK]
    u_part = solved[:, :, DK:]
    fresh = u_part - jnp.einsum('hcd,hde->hce', w_part, states, precision=highest)
    scores = jnp.einsum('hid,hjd->hij', q_head, k_head, precision=highest) * within
    outputs = jnp.einsum('hcd,hde->hce', q_head * leading[:, :, None], states, precision=highest)
    outputs = outputs + jnp.einsum('hij,hje->hie', scores, fresh, precision=highest)
    outputs = outputs * DK ** (-0.5)
    remaining = jnp.exp(cumulative[:, -1:] - cumulative)
    states = leading[:, -1][:, None, None] * states + jnp.einsum('hcd,hce->hde', k_head * remaining[:, :, None], fresh, precision=highest)
    return (states, outputs.transpose(1, 0, 2))

def gdn_row(queries, keys_in, values, decays, betas):
    length = queries.shape[0]
    head_count = queries.shape[1]
    block_count = length // SPAN
    blocks_all = (queries.reshape(block_count, SPAN, head_count, DK), keys_in.reshape(block_count, SPAN, head_count, DK), values.reshape(block_count, SPAN, head_count, DV), decays.reshape(block_count, SPAN, head_count), betas.reshape(block_count, SPAN, head_count))
    states = jnp.zeros((head_count, DK, DV), jnp.float32)
    _, outputs = lax.scan(jax.checkpoint(span_step), states, blocks_all)
    return outputs.reshape(length, head_count, DV)

def mixer(pre_query, pre_key, pre_value, pre_decay, pre_beta, pre_gate, conv_q, conv_k, conv_v, log_rates, rate_bias, gain_vec):
    row_count, length, head_count = pre_decay.shape
    queries = jax.nn.silu(causal_conv(pre_query, conv_q)).reshape(row_count, length, head_count, DK)
    queries = queries * lax.rsqrt(lax.optimization_barrier(jnp.sum(queries * queries, axis=-1, keepdims=True)) + NORM_EPS)
    keys_in = jax.nn.silu(causal_conv(pre_key, conv_k)).reshape(row_count, length, head_count, DK)
    keys_in = keys_in * lax.rsqrt(lax.optimization_barrier(jnp.sum(keys_in * keys_in, axis=-1, keepdims=True)) + NORM_EPS)
    values = jax.nn.silu(causal_conv(pre_value, conv_v)).reshape(row_count, length, head_count, DV)
    betas = jax.nn.sigmoid(pre_beta)
    decays = -jnp.exp(log_rates) * jax.nn.softplus(pre_decay + rate_bias)
    recurrent = jax.vmap(gdn_row)(queries, keys_in, values, decays, betas)
    gated = rms_norm(recurrent, gain_vec) * jax.nn.silu(pre_gate.reshape(row_count, length, head_count, DV))
    return gated.reshape(row_count, length, head_count * DV)

def layer(params, inputs, mask_rows):
    gain_attn, w_query, w_key, w_value, w_decay, w_beta, w_gate_out, conv_query, conv_key, conv_value, decay_log, decay_bias, gain_head, w_out, gain_mlp, w_gate, w_up, w_down = params
    highest = lax.Precision.HIGHEST
    normed = low(rms_norm(inputs, gain_attn))

    def project(weight):
        return low_back(jnp.dot(normed, weight, precision=highest))
    mixed = low(mixer(project(w_query), project(w_key), project(w_value), project(w_decay), project(w_beta), project(w_gate_out), conv_query, conv_key, conv_value, decay_log, decay_bias, gain_head))
    attended = low_back(jnp.dot(mixed, w_out.T, precision=highest))
    middle = inputs + mask_rows * attended
    normed_two = low(rms_norm(middle, gain_mlp))
    gate_vals = low_back(jnp.dot(normed_two, w_gate, precision=highest))
    up_vals = low_back(jnp.dot(normed_two, w_up, precision=highest))
    hidden = low(jax.nn.silu(gate_vals) * up_vals)
    mlp_out = low_back(jnp.dot(hidden, w_down.T, precision=highest))
    return middle + mask_rows * mlp_out

def reference(tokens, lengths, gain_attn, w_query, w_key, w_value, w_decay, w_beta, w_gate_out, conv_query, conv_key, conv_value, decay_log, decay_bias, gain_head, w_out, gain_mlp, w_gate, w_up, w_down, cotangent):
    params = tuple((item.astype(jnp.float32) for item in (gain_attn, w_query, w_key, w_value, w_decay, w_beta, w_gate_out, conv_query, conv_key, conv_value, decay_log, decay_bias, gain_head, w_out, gain_mlp, w_gate, w_up, w_down)))
    groups = ROWS // ROWS_G
    inputs_all = tokens.astype(jnp.float32).reshape(groups, ROWS_G, L, D)
    cot_all = cotangent.astype(jnp.float32).reshape(groups, ROWS_G, L, D)
    positions = jnp.arange(L, dtype=jnp.int32)
    masks = (positions[None, :] < lengths.astype(jnp.int32)[:, None]).astype(jnp.float32).reshape(groups, ROWS_G, L, 1)

    def one_group(totals, batch_in):
        inputs, mask_rows, cot_rows = batch_in

        def forward(weights_in, inputs_in):
            return layer(weights_in, inputs_in, mask_rows)
        result, backward = jax.vjp(forward, params, inputs)
        grad_params, grad_inputs = backward(cot_rows)
        totals = jax.tree.map(jnp.add, totals, grad_params)
        return (totals, (result, grad_inputs))
    zeros = jax.tree.map(jnp.zeros_like, params)
    totals, (results, grad_inputs) = lax.scan(one_group, zeros, (inputs_all, masks, cot_all))
    mixed_rows = results.reshape(ROWS, L, D).astype(jnp.bfloat16)
    tokens_grad = grad_inputs.reshape(ROWS, L, D).astype(jnp.bfloat16)
    return (mixed_rows, tokens_grad, totals[0], totals[1], totals[2], totals[3], totals[4], totals[5], totals[6], totals[7], totals[8], totals[9], totals[10], totals[11], totals[12], totals[13], totals[14], totals[15], totals[16], totals[17])
```

```python
import functools

import jax
import jax.numpy as jnp
from jax import lax
from jax.experimental import pallas as pl
from jax.experimental.pallas import tpu as pltpu
from jax.sharding import PartitionSpec as P

DK = 128
DV = 256
CHUNK = 128
NORM_EPS = 1e-06
BF = jnp.bfloat16
F32 = jnp.float32
NN = (((1,), (0,)), ((), ()))
NT = (((1,), (1,)), ((), ()))
TN = (((0,), (0,)), ((), ()))


def mm(a, b, dims=NN):
    return lax.dot_general(a.astype(BF), b.astype(BF), dims, preferred_element_type=F32)


def split(a):
    high = a.astype(BF)
    return high, (a - high.astype(F32)).astype(BF)


def mm3(a, b, dims=NN):
    ah, al = split(a)
    bh, bl = split(b)
    return mm(ah, bh, dims) + mm(ah, bl, dims) + mm(al, bh, dims)


def exact(a, b, dims=NN):
    return lax.dot_general(a, b, dims, precision=lax.Precision.HIGHEST, preferred_element_type=F32)


def iotas(n):
    return (
        lax.broadcasted_iota(jnp.int32, (n, n), 0),
        lax.broadcasted_iota(jnp.int32, (n, n), 1),
    )


def lower_inverses(lowers):
    n = lowers[0].shape[0]
    row, col = iotas(n)
    eye = (row == col).astype(F32)
    pair = (row // 2 == col // 2).astype(F32)
    inverses = [eye - low * pair for low in lowers]
    size = 2
    while size < n:
        corner = ((row // (2 * size)) == (col // (2 * size))) & ((row // size) != (col // size))
        corner = corner.astype(F32)
        half = [x.astype(BF) for x in inverses]
        inner = [mm(x, low * corner) for x, low in zip(half, lowers)]
        inverses = [x - mm(i, h) for x, i, h in zip(inverses, inner, half)]
        size = size * 2
    residual = [eye - x - mm3(low, x) for low, x in zip(lowers, inverses)]
    return [x + mm(x, r) for x, r in zip(inverses, residual)]


def sigmoid(x):
    return 1.0 / (1.0 + jnp.exp(-x))


def conv_of(buf, taps, sl):
    total = taps[0:1, sl] * buf[5 : 5 + CHUNK, sl]
    for i in range(1, 4):
        total = total + taps[i : i + 1, sl] * buf[5 + i : 5 + i + CHUNK, sl]
    return total


def softplus(x):
    return jnp.maximum(x, 0.0) + jnp.log1p(jnp.exp(-jnp.abs(x)))


def unit(a):
    r = lax.rsqrt(jnp.sum(a * a, axis=-1, keepdims=True) + NORM_EPS)
    return a * r, r


def mixer_forward_kernel(
    heads, pq, pk, pv, pg, ps, cq, ck, cv, rates, bias, gain,
    mixed, t_out, s_out, f_out, bq, bk, bv, state,
):
    step = pl.program_id(1)

    @pl.when(step == 0)
    def _():
        state[...] = jnp.zeros_like(state)
        for b in (bq, bk, bv):
            b[0:8, :] = jnp.zeros((8, b.shape[1]), F32)

    @pl.when(step > 0)
    def _():
        for b in (bq, bk, bv):
            b[0:8, :] = b[CHUNK : CHUNK + 8, :]

    for b, p in ((bq, pq), (bk, pk), (bv, pv)):
        b[8 : CHUNK + 8, :] = p[0].astype(F32)
    row, col = iotas(CHUNK)
    small = ps[0]
    g = rates[...] * softplus(small + bias[...])
    beta_all = sigmoid(small)
    cum = exact((row >= col).astype(F32), g)
    cum_t = cum.T
    hs = range(heads)
    ks = [slice(h * DK, (h + 1) * DK) for h in hs]
    vs = [slice(h * DV, (h + 1) * DV) for h in hs]
    q, k, v, within, kbeta, gamma, rem, last = [], [], [], [], [], [], [], []
    for h in hs:
        a = conv_of(bq, cq, ks[h])
        q.append(unit(a * sigmoid(a))[0])
        a = conv_of(bk, ck, ks[h])
        k.append(unit(a * sigmoid(a))[0])
        a = conv_of(bv, cv, vs[h])
        v.append(a * sigmoid(a))
        gc = cum[:, h : h + 1]
        within.append(jnp.exp(jnp.where(row >= col, gc - cum_t[h : h + 1, :], -1e30)))
        kbeta.append(beta_all[:, heads + h : heads + h + 1])
        gamma.append(jnp.exp(gc))
        tail = cum[CHUNK - 1 : CHUNK, h : h + 1]
        rem.append(jnp.exp(tail - gc))
        last.append(jnp.exp(tail))
    kb = [x.astype(BF) for x in k]
    lowers = [
        jnp.where(row > col, kbeta[h] * (mm(kb[h], kb[h], NT) * within[h]), 0.0) for h in hs
    ]
    scores = [mm(q[h], kb[h], NT) * within[h] for h in hs]
    inv = lower_inverses(lowers)
    states = [state[h] for h in hs]
    sb = [s.astype(BF) for s in states]
    both = [
        mm(jnp.concatenate([gamma[h] * k[h], gamma[h] * q[h]], axis=0), sb[h]) for h in hs
    ]
    fresh = [mm(inv[h], kbeta[h] * (v[h] - both[h][:CHUNK])) for h in hs]
    fb = [x.astype(BF) for x in fresh]
    out = [(both[h][CHUNK:] + mm(scores[h], fb[h])) * DK**-0.5 for h in hs]
    for h in hs:
        state[h] = last[h] * states[h] + mm(rem[h] * k[h], fb[h], TN)
        t_out[0, 0, h] = inv[h].astype(t_out.dtype)
        s_out[0, 0, h] = sb[h]
        f_out[0, :, vs[h]] = fb[h]
        o = out[h]
        r = lax.rsqrt(jnp.mean(o * o, axis=-1, keepdims=True) + NORM_EPS)
        pgh = pg[0, :, vs[h]].astype(F32)
        mixed[0, :, vs[h]] = (o * r * gain[...] * (pgh * sigmoid(pgh))).astype(mixed.dtype)


def mixer_backward_kernel(
    heads, dm, pq, pk, pv, pg, ps, tq, tk, tv, cq, ck, cv, rates, bias, gain, t_in, s_in, f_in,
    gqks, gvg, dcq, dck, dcv, dsm, dgain,
    bq, bk, bv, eq, ek, ev, dstate,
):
    row_at = pl.program_id(0)
    step = pl.program_id(1)
    chunk = pl.num_programs(1) - 1 - step

    @pl.when((row_at == 0) & (step == 0))
    def _():
        for r in (dcq, dck, dcv, dsm, dgain):
            r[...] = jnp.zeros_like(r)

    @pl.when(step == 0)
    def _():
        dstate[...] = jnp.zeros_like(dstate)
        for b in (eq, ek, ev):
            b[CHUNK : CHUNK + 8, :] = jnp.zeros((8, b.shape[1]), F32)

    @pl.when(step > 0)
    def _():
        for b in (eq, ek, ev):
            b[CHUNK : CHUNK + 8, :] = b[0:8, :]

    has_before = (chunk > 0).astype(F32)
    for b, p, t in ((bq, pq, tq), (bk, pk, tk), (bv, pv, tv)):
        b[0:8, :] = t[0].astype(F32) * has_before
        b[8 : CHUNK + 8, :] = p[0].astype(F32)
    row, col = iotas(CHUNK)
    lane = col
    small = ps[0]
    shifted = small + bias[...]
    g = rates[...] * softplus(shifted)
    beta_all = sigmoid(small)
    cum = exact((row >= col).astype(F32), g)
    cum_t = cum.T
    hs = range(heads)
    ks = [slice(h * DK, (h + 1) * DK) for h in hs]
    vs = [slice(h * DV, (h + 1) * DV) for h in hs]
    scale = DK**-0.5
    dcum = jnp.zeros((CHUNK, CHUNK), F32)
    dcum_rows = jnp.zeros((CHUNK, CHUNK), F32)
    dbeta = jnp.zeros((CHUNK, CHUNK), F32)
    head_dgain = jnp.zeros((1, DV), F32)
    q, k, v, rq, rk, kbeta, gamma, rem, last, within = [], [], [], [], [], [], [], [], [], []
    for h in hs:
        a = conv_of(bq, cq, ks[h])
        x, r = unit(a * sigmoid(a))
        q.append(x)
        rq.append(r)
        a = conv_of(bk, ck, ks[h])
        x, r = unit(a * sigmoid(a))
        k.append(x)
        rk.append(r)
        a = conv_of(bv, cv, vs[h])
        v.append(a * sigmoid(a))
        gc = cum[:, h : h + 1]
        within.append(jnp.exp(jnp.where(row >= col, gc - cum_t[h : h + 1, :], -1e30)))
        kbeta.append(beta_all[:, heads + h : heads + h + 1])
        gamma.append(jnp.exp(gc))
        tail = cum[CHUNK - 1 : CHUNK, h : h + 1]
        rem.append(jnp.exp(tail - gc))
        last.append(jnp.exp(tail))
    qb = [x.astype(BF) for x in q]
    kb = [x.astype(BF) for x in k]
    sb = [s_in[0, 0, h] for h in hs]
    fb = [f_in[0, :, vs[h]] for h in hs]
    tb = [t_in[0, 0, h].astype(BF) for h in hs]
    gram = [mm(kb[h], kb[h], NT) * within[h] for h in hs]
    scores = [mm(qb[h], kb[h], NT) * within[h] for h in hs]
    gk_gq = [
        jnp.concatenate([gamma[h] * k[h], gamma[h] * q[h]], axis=0) for h in hs
    ]
    both = [mm(gk_gq[h], sb[h]) for h in hs]
    x_in = [v[h] - both[h][:CHUNK] for h in hs]
    out = [(both[h][CHUNK:] + mm(scores[h], fb[h])) * scale for h in hs]
    dout = []
    for h in hs:
        o = out[h]
        r = lax.rsqrt(jnp.mean(o * o, axis=-1, keepdims=True) + NORM_EPS)
        n = o * r
        p = pg[0, :, vs[h]].astype(F32)
        s = sigmoid(p)
        d = dm[0, :, vs[h]].astype(F32)
        y = n * gain[...]
        at = heads * DV + h * DV
        gvg[0, :, at : at + DV] = (d * y * (s * (1.0 + p * (1.0 - s)))).astype(BF)
        dy = d * (p * s)
        head_dgain = head_dgain + jnp.sum(dy * n, axis=0, keepdims=True)
        dn = dy * gain[...]
        dout.append(scale * r * (dn - n * jnp.mean(n * dn, axis=-1, keepdims=True)))
    dob = [x.astype(BF) for x in dout]
    ds_next = [dstate[h] for h in hs]
    dsb = [x.astype(BF) for x in ds_next]
    krem = [rem[h] * k[h] for h in hs]
    dfresh = [mm(scores[h], dob[h], TN) + mm(krem[h], dsb[h]) for h in hs]
    dr = [mm(tb[h], dfresh[h], TN) for h in hs]
    drb = [x.astype(BF) for x in dr]
    dx = [kbeta[h] * dr[h] for h in hs]
    dx_do = [jnp.concatenate([-dx[h], dout[h]], axis=0).astype(BF) for h in hs]
    for h in hs:
        dstate[h] = last[h] * ds_next[h] + mm(gk_gq[h], dx_do[h], TN)
    dgk_gq = [mm(dx_do[h], sb[h], NT) for h in hs]
    dkrem = [mm(fb[h], dsb[h], NT) for h in hs]
    dscore = [mm(dob[h], fb[h], NT) for h in hs]
    dlow = [jnp.where(row > col, -mm(drb[h], fb[h], NT), 0.0) for h in hs]
    for h in hs:
        m = dscore[h] * within[h]
        dgram = kbeta[h] * (dlow[h] * within[h])
        lg = dlow[h] * gram[h]
        e = dscore[h] * scores[h] + kbeta[h] * lg
        dq = gamma[h] * dgk_gq[h][CHUNK:] + mm(m, kb[h])
        mk = jnp.concatenate([m, dgram], axis=0)
        dk = (
            gamma[h] * dgk_gq[h][:CHUNK]
            + rem[h] * dkrem[h]
            + mm(mk, jnp.concatenate([qb[h], kb[h]], axis=0), TN)
            + mm(dgram, kb[h])
        )
        rem_part = jnp.sum(dkrem[h] * krem[h], axis=-1, keepdims=True)
        head_dcum = (
            jnp.sum(e, axis=-1, keepdims=True)
            + jnp.sum(
                dgk_gq[h][:CHUNK] * gk_gq[h][:CHUNK] + dgk_gq[h][CHUNK:] * gk_gq[h][CHUNK:],
                axis=-1, keepdims=True,
            )
            - rem_part
        )
        state_part = jnp.sum(
            jnp.sum(ds_next[h] * sb[h].astype(F32), axis=0, keepdims=True), axis=1, keepdims=True
        )
        end_part = jnp.sum(rem_part, axis=0, keepdims=True) + last[h] * state_part
        head_dcum = head_dcum + jnp.where(row[:, 0:1] == CHUNK - 1, end_part, 0.0)
        dcum = dcum + jnp.where(lane == h, head_dcum, 0.0)
        dcum_rows = dcum_rows + jnp.where(row == h, jnp.sum(e, axis=0, keepdims=True), 0.0)
        head_dbeta = jnp.sum(dr[h] * x_in[h], axis=-1, keepdims=True) + jnp.sum(
            lg, axis=-1, keepdims=True
        )
        dbeta = dbeta + jnp.where(lane == heads + h, head_dbeta, 0.0)
        a = conv_of(bq, cq, ks[h])
        s = sigmoid(a)
        da = rq[h] * (dq - q[h] * jnp.sum(q[h] * dq, axis=-1, keepdims=True))
        eq[0:CHUNK, ks[h]] = da * (s * (1.0 + a * (1.0 - s)))
        a = conv_of(bk, ck, ks[h])
        s = sigmoid(a)
        da = rk[h] * (dk - k[h] * jnp.sum(k[h] * dk, axis=-1, keepdims=True))
        ek[0:CHUNK, ks[h]] = da * (s * (1.0 + a * (1.0 - s)))
        a = conv_of(bv, cv, vs[h])
        s = sigmoid(a)
        ev[0:CHUNK, vs[h]] = dx[h] * (s * (1.0 + a * (1.0 - s)))
    dgain[0:1, :] += head_dgain
    dcum = dcum - dcum_rows.T
    dg = exact((row >= col).astype(F32), dcum, TN)
    dshift = dg * rates[...] * sigmoid(shifted)
    dsm[0:1, :] += jnp.sum(dg * g, axis=0, keepdims=True)
    dsm[1:2, :] += jnp.sum(dshift, axis=0, keepdims=True)
    gqks[0, :, 2 * heads * DK :] = (
        jnp.where(lane < heads, dshift, 0.0) + dbeta * beta_all * (1.0 - beta_all)
    ).astype(BF)
    for b, e, taps, dtaps, out_ref, start in (
        (bq, eq, cq, dcq, gqks, 0), (bk, ek, ck, dck, gqks, heads * DK), (bv, ev, cv, dcv, gvg, 0),
    ):
        for at in range(0, b.shape[1], DK):
            sl = slice(at, at + DK)
            own = e[0:CHUNK, sl]
            total = taps[3:4, sl] * own
            for i in range(3):
                total = total + taps[i : i + 1, sl] * e[3 - i : 3 - i + CHUNK, sl]
            out_ref[0, :, start + at : start + at + DK] = total.astype(BF)
            for i in range(4):
                dtaps[i : i + 1, sl] += jnp.sum(
                    own * b[5 + i : 5 + i + CHUNK, sl], axis=0, keepdims=True
                )


def whole_spec(shape):
    return pl.BlockSpec(shape, lambda r, c: (0,) * len(shape))


def lane_pad(vec, at):
    return jnp.zeros((1, 128), F32).at[0, at : at + vec.shape[0]].set(vec)


def mixer_forward(pqks, pvg, cq, ck, cv, log_rates, rate_bias, gain):
    rows, length, value_width = pvg.shape
    value_width = value_width // 2
    key_width = value_width * DK // DV
    heads = key_width // DK
    chunks = length // CHUNK
    seq = lambda width, at=0: pl.BlockSpec((1, CHUNK, width), lambda r, c: (r, c, at))
    per = lambda a, b: pl.BlockSpec((1, 1, heads, a, b), lambda r, c: (r, c, 0, 0, 0))
    return pl.pallas_call(
        functools.partial(mixer_forward_kernel, heads),
        grid=(rows, chunks),
        in_specs=[seq(key_width), seq(key_width, 1), seq(value_width), seq(value_width, 1),
                  seq(128, 2 * heads),
                  whole_spec((4, key_width)), whole_spec((4, key_width)), whole_spec((4, value_width)),
                  whole_spec((1, 128)), whole_spec((1, 128)), whole_spec((1, DV))],
        out_specs=[seq(value_width), per(CHUNK, CHUNK), per(DK, DV), seq(value_width)],
        out_shape=[
            jax.ShapeDtypeStruct((rows, length, value_width), BF),
            jax.ShapeDtypeStruct((rows, chunks, heads, CHUNK, CHUNK), BF),
            jax.ShapeDtypeStruct((rows, chunks, heads, DK, DV), BF),
            jax.ShapeDtypeStruct((rows, length, value_width), BF),
        ],
        scratch_shapes=[
            pltpu.VMEM((CHUNK + 8, key_width), F32),
            pltpu.VMEM((CHUNK + 8, key_width), F32),
            pltpu.VMEM((CHUNK + 8, value_width), F32),
            pltpu.VMEM((heads, DK, DV), F32),
        ],
        compiler_params=pltpu.CompilerParams(
            dimension_semantics=("arbitrary", "arbitrary"), vmem_limit_bytes=40 << 20
        ),
        name="mixer_forward",
    )(pqks, pqks, pvg, pvg, pqks, cq, ck, cv, lane_pad(-jnp.exp(log_rates), 0),
      lane_pad(rate_bias, 0), gain.reshape(1, DV))


def mixer_backward(dm, pqks, pvg, cq, ck, cv, log_rates, rate_bias, gain, t_in, s_in, f_in):
    rows, length, value_width = dm.shape
    key_width = value_width * DK // DV
    heads = key_width // DK
    chunks = length // CHUNK
    seq = lambda width, at=0: pl.BlockSpec(
        (1, CHUNK, width), lambda r, c: (r, chunks - 1 - c, at)
    )
    before = lambda width, at=0: pl.BlockSpec(
        (1, 8, width),
        lambda r, c: (r, jnp.maximum((chunks - 1 - c) * (CHUNK // 8) - 1, 0), at),
    )
    per = lambda a, b: pl.BlockSpec(
        (1, 1, heads, a, b), lambda r, c: (r, chunks - 1 - c, 0, 0, 0)
    )
    seq_shape = lambda width: jax.ShapeDtypeStruct((rows, length, width), BF)
    return pl.pallas_call(
        functools.partial(mixer_backward_kernel, heads),
        grid=(rows, chunks),
        in_specs=[seq(value_width), seq(key_width), seq(key_width, 1), seq(value_width),
                  seq(value_width, 1), seq(128, 2 * heads),
                  before(key_width), before(key_width, 1), before(value_width),
                  whole_spec((4, key_width)), whole_spec((4, key_width)), whole_spec((4, value_width)),
                  whole_spec((1, 128)), whole_spec((1, 128)), whole_spec((1, DV)),
                  per(CHUNK, CHUNK), per(DK, DV), seq(value_width)],
        out_specs=[seq(2 * key_width + 128), seq(2 * value_width),
                   whole_spec((8, key_width)), whole_spec((8, key_width)), whole_spec((8, value_width)),
                   whole_spec((8, 128)), whole_spec((8, DV))],
        out_shape=[seq_shape(2 * key_width + 128), seq_shape(2 * value_width),
                   jax.ShapeDtypeStruct((8, key_width), F32),
                   jax.ShapeDtypeStruct((8, key_width), F32),
                   jax.ShapeDtypeStruct((8, value_width), F32),
                   jax.ShapeDtypeStruct((8, 128), F32),
                   jax.ShapeDtypeStruct((8, DV), F32)],
        scratch_shapes=[
            pltpu.VMEM((CHUNK + 8, key_width), F32),
            pltpu.VMEM((CHUNK + 8, key_width), F32),
            pltpu.VMEM((CHUNK + 8, value_width), F32),
            pltpu.VMEM((CHUNK + 8, key_width), F32),
            pltpu.VMEM((CHUNK + 8, key_width), F32),
            pltpu.VMEM((CHUNK + 8, value_width), F32),
            pltpu.VMEM((heads, DK, DV), F32),
        ],
        compiler_params=pltpu.CompilerParams(
            dimension_semantics=("arbitrary", "arbitrary"), vmem_limit_bytes=48 << 20
        ),
        name="mixer_backward",
    )(dm, pqks, pqks, pvg, pvg, pqks, pqks, pqks, pvg, cq, ck, cv, lane_pad(-jnp.exp(log_rates), 0),
      lane_pad(rate_bias, 0), gain.reshape(1, DV), t_in, s_in, f_in)


GROUP = 0


def ring(size, group):
    return [(i, i // group * group + (i + 1) % group) for i in range(size)]


def swap(size, bit):
    return [(i, i ^ bit) for i in range(size)]


def matmul(a, b, dims=NN):
    return lax.dot_general(a, b, dims, preferred_element_type=F32)


def gather_ring(piece, size, group):
    pieces = [piece]
    for _ in range(group - 1):
        pieces.append(lax.ppermute(pieces[-1], "head", ring(size, group)))
    return pieces


def scatter_ring(part_of, size, group):
    total = part_of(1 % group)
    for s in range(2, group + 1):
        moved = lax.ppermute(total.astype(BF), "head", ring(size, group))
        total = part_of(s % group) + moved.astype(F32)
    return total


def norm_parts(x):
    r = lax.rsqrt(jnp.mean(x * x, axis=-1, keepdims=True) + NORM_EPS)
    return x * r, r


def norm_back(n, r, gain, grad):
    inner = gain * grad
    return r * (inner - n * jnp.mean(n * inner, axis=-1, keepdims=True))


def sum_small(flat, sizes):
    for axis in ("dp", "head"):
        bit = 1
        while bit < sizes[axis]:
            flat = flat + lax.ppermute(flat, axis, swap(sizes[axis], bit))
            bit = bit * 2
    return flat


def per_device(
    tokens,
    lengths,
    gain_attn,
    w_query,
    w_key,
    w_value,
    w_decay,
    w_beta,
    w_gate_out,
    conv_query,
    conv_key,
    conv_value,
    decay_log,
    decay_bias,
    gain_head,
    w_out,
    gain_mlp,
    w_gate,
    w_up,
    w_down,
    cotangent,
):
    rows, piece, width = tokens.shape
    size = lax.axis_size("head")
    me = lax.axis_index("head")
    length = piece * size
    heads = w_decay.shape[1]
    flat_piece = rows * piece
    positions = me * piece + jnp.arange(piece, dtype=jnp.int32)
    mask = (positions[None, :] < lengths[:, None]).astype(F32)[:, :, None]

    def owner(s):
        return lax.rem(me + size - s, size)

    def put(whole, part, s):
        return lax.dynamic_update_slice_in_dim(whole, part, owner(s) * piece, 1)

    def take(whole, s):
        return lax.dynamic_slice_in_dim(whole, owner(s) * piece, piece, 1)

    def gather_weight(w):
        return lax.all_gather(w, "dp", axis=0, tiled=True)

    small_pad = jnp.zeros((w_decay.shape[0], 128 - 2 * heads), BF)
    w_qks = gather_weight(jnp.concatenate([w_query, w_key, w_decay, w_beta, small_pad], axis=1))
    w_vg = gather_weight(jnp.concatenate([w_value, w_gate_out], axis=1))
    wo_full = gather_weight(w_out)
    wgate_full = gather_weight(w_gate)
    wup_full = gather_weight(w_up)
    wdown_full = gather_weight(w_down)

    inputs32 = tokens.astype(F32)
    n_one, r_one = norm_parts(inputs32)
    normed = (n_one * gain_attn).astype(BF)
    normed_pieces = gather_ring(normed, size, size)
    normed_all = jnp.zeros((rows, length, width), BF)
    pqks = jnp.zeros((rows, length, w_qks.shape[1]), F32)
    pvg = jnp.zeros((rows, length, w_vg.shape[1]), F32)
    batch_nn = (((2,), (0,)), ((), ()))
    batch_nt = (((2,), (1,)), ((), ()))
    for s, item in enumerate(normed_pieces):
        pqks = put(pqks, matmul(item, w_qks, batch_nn), s)
        pvg = put(pvg, matmul(item, w_vg, batch_nn), s)
        normed_all = put(normed_all, item, s)

    cq = lax.dynamic_slice_in_dim(conv_query, me * heads * DK, heads * DK, 1)
    ck = lax.dynamic_slice_in_dim(conv_key, me * heads * DK, heads * DK, 1)
    cv = lax.dynamic_slice_in_dim(conv_value, me * heads * DV, heads * DV, 1)
    log_local = lax.dynamic_slice_in_dim(decay_log, me * heads, heads, 0)
    bias_local = lax.dynamic_slice_in_dim(decay_bias, me * heads, heads, 0)
    mixed, t_kept, s_kept, f_kept = mixer_forward(
        pqks, pvg, cq, ck, cv, log_local, bias_local, gain_head
    )
    attended = scatter_ring(
        lambda s: matmul(take(mixed, s), wo_full, batch_nt), size, size
    )
    middle = inputs32 + mask * attended
    n_two, r_two = norm_parts(middle)
    normed_two = (n_two * gain_mlp).astype(BF)
    cot32 = cotangent.astype(F32)
    grad_mlp = (mask * cot32).astype(BF)

    group = GROUP or size
    second = [x.reshape(flat_piece, width) for x in gather_ring(normed_two, size, group)]
    grad_out = [x.reshape(flat_piece, width) for x in gather_ring(grad_mlp, size, group)]
    hidden, grad_gate, grad_up = [], [], []
    for x, g in zip(second, grad_out):
        gate = matmul(x, wgate_full)
        up = matmul(x, wup_full)
        sig = jax.nn.sigmoid(gate)
        act = gate * sig
        hidden.append((act * up).astype(BF))
        back = matmul(g, wdown_full)
        grad_gate.append((back * up * sig * (1.0 + gate * (1.0 - sig))).astype(BF))
        grad_up.append((back * act).astype(BF))
    shape3 = (rows, piece, width)
    grad_normed_two = scatter_ring(
        lambda s: matmul(grad_gate[s], wgate_full, NT) + matmul(grad_up[s], wup_full, NT),
        size, group,
    ).reshape(shape3)
    grad_gain_mlp = jnp.sum(grad_normed_two * n_two, axis=(0, 1))
    grad_middle = cot32 + norm_back(n_two, r_two, gain_mlp, grad_normed_two)
    grad_attn = (mask * grad_middle).astype(BF)
    grad_attn_pieces = gather_ring(grad_attn, size, size)
    grad_mixed = jnp.zeros((rows, length, heads * DV), F32)
    grad_attn_all = jnp.zeros((rows, length, width), BF)
    for s, item in enumerate(grad_attn_pieces):
        grad_mixed = put(grad_mixed, matmul(item, wo_full, batch_nn), s)
        grad_attn_all = put(grad_attn_all, item, s)

    mlp_out = scatter_ring(
        lambda s: matmul(hidden[s], wdown_full, NT), size, group
    ).reshape(shape3)
    mixed_rows = (middle + mask * mlp_out).astype(BF)
    second_all = jnp.concatenate(second, axis=0)
    grad_wdown = matmul(jnp.concatenate(grad_out, axis=0), jnp.concatenate(hidden, axis=0), TN)
    grad_wgate = matmul(second_all, jnp.concatenate(grad_gate, axis=0), TN)
    grad_wup = matmul(second_all, jnp.concatenate(grad_up, axis=0), TN)

    def scatter_weight(g):
        return lax.psum_scatter(g.astype(BF), "dp", scatter_dimension=0, tiled=True).astype(F32)

    out_wdown = scatter_weight(grad_wdown)
    out_wgate = scatter_weight(grad_wgate)
    out_wup = scatter_weight(grad_wup)
    flat = lambda x: x.reshape(rows * length, x.shape[2])
    out_wout = scatter_weight(matmul(flat(grad_attn_all), flat(mixed), TN))

    gqks, gvg, dcq, dck, dcv, dsm, dgain = mixer_backward(
        grad_mixed, pqks, pvg, cq, ck, cv, log_local, bias_local, gain_head,
        t_kept, s_kept, f_kept,
    )
    gain_sums = []

    def part_one(s):
        part = matmul(take(gqks, s), w_qks, batch_nt) + matmul(take(gvg, s), w_vg, batch_nt)
        gain_sums.append(jnp.sum(part * take(normed_all, s).astype(F32), axis=(0, 1)))
        return part

    grad_normed = scatter_ring(part_one, size, size)
    out_qks = scatter_weight(matmul(flat(normed_all), flat(gqks), TN))
    out_vg = scatter_weight(matmul(flat(normed_all), flat(gvg), TN))
    tokens_grad = (grad_middle + norm_back(n_one, r_one, gain_attn, grad_normed)).astype(BF)

    def spread(part, axis):
        shape = part.shape[:axis] + (size,) + part.shape[axis:]
        whole = jnp.zeros(shape, F32)
        whole = lax.dynamic_update_slice_in_dim(whole, jnp.expand_dims(part, axis), me, axis)
        return whole.reshape(part.shape[:axis] + (size * part.shape[axis],) + part.shape[axis + 1 :])

    small = (
        sum(gain_sums) / gain_attn,
        grad_gain_mlp,
        dgain[0],
        spread(dcq[:4], 1),
        spread(dck[:4], 1),
        spread(dcv[:4], 1),
        spread(dsm[0, :heads], 0),
        spread(dsm[1, :heads], 0),
    )
    lane_sizes = [x.size for x in small]
    total = sum(lane_sizes)
    padded = -(-total // 1024) * 1024
    packed = jnp.concatenate(
        [x.reshape(-1) for x in small] + [jnp.zeros((padded - total,), F32)]
    ).reshape(padded // 128, 128)
    packed = sum_small(packed, {"dp": lax.axis_size("dp"), "head": size}).reshape(-1)
    sums = []
    at = 0
    for x in small:
        sums.append(packed[at : at + x.size].reshape(x.shape))
        at = at + x.size
    key_width = heads * DK
    value_width = heads * DV
    return (
        mixed_rows,
        tokens_grad,
        sums[0],
        out_qks[:, :key_width],
        out_qks[:, key_width : 2 * key_width],
        out_vg[:, :value_width],
        out_qks[:, 2 * key_width : 2 * key_width + heads],
        out_qks[:, 2 * key_width + heads : 2 * key_width + 2 * heads],
        out_vg[:, value_width:],
        sums[3],
        sums[4],
        sums[5],
        sums[6],
        sums[7],
        sums[2],
        out_wout,
        sums[1],
        out_wgate,
        out_wup,
        out_wdown,
    )


def solution(mesh):
    rows = P("dp", "head", None)
    weight = P("dp", "head")
    same = P()
    return jax.shard_map(
        per_device,
        mesh=mesh,
        in_specs=(
            rows, P("dp"), same, weight, weight, weight, weight, weight, weight, same, same, same,
            same, same, same, weight, same, weight, weight, weight, rows,
        ),
        out_specs=(
            rows, rows, same, weight, weight, weight, weight, weight, weight, same, same, same,
            same, same, same, weight, same, weight, weight, weight,
        ),
        check_vma=False,
    )
```

```python
import functools

import jax
import jax.numpy as jnp
from jax import lax
from jax.experimental import pallas as pl
from jax.experimental.pallas import tpu as pltpu
from jax.sharding import PartitionSpec as P

DK = 128
DV = 256
CHUNK = 128
NORM_EPS = 1e-06
BF = jnp.bfloat16
F32 = jnp.float32
NN = (((1,), (0,)), ((), ()))
NT = (((1,), (1,)), ((), ()))
TN = (((0,), (0,)), ((), ()))


def mm(a, b, dims=NN):
    return lax.dot_general(a.astype(BF), b.astype(BF), dims, preferred_element_type=F32)


def split(a):
    high = a.astype(BF)
    return high, (a - high.astype(F32)).astype(BF)


def mm3(a, b, dims=NN):
    ah, al = split(a)
    bh, bl = split(b)
    return mm(ah, bh, dims) + mm(ah, bl, dims) + mm(al, bh, dims)


def exact(a, b, dims=NN):
    return lax.dot_general(a, b, dims, precision=lax.Precision.HIGHEST, preferred_element_type=F32)


def iotas(n):
    return (
        lax.broadcasted_iota(jnp.int32, (n, n), 0),
        lax.broadcasted_iota(jnp.int32, (n, n), 1),
    )


def lower_inverses(lowers):
    n = lowers[0].shape[0]
    row, col = iotas(n)
    eye = (row == col).astype(F32)
    pair = (row // 2 == col // 2).astype(F32)
    inverses = [eye - low * pair for low in lowers]
    size = 2
    while size < n:
        corner = ((row // (2 * size)) == (col // (2 * size))) & ((row // size) != (col // size))
        corner = corner.astype(F32)
        half = [x.astype(BF) for x in inverses]
        inner = [mm(x, low * corner) for x, low in zip(half, lowers)]
        inverses = [x - mm(i, h) for x, i, h in zip(inverses, inner, half)]
        size = size * 2
    residual = [eye - x - mm3(low, x) for low, x in zip(lowers, inverses)]
    return [x + mm(x, r) for x, r in zip(inverses, residual)]


def sigmoid(x):
    return 1.0 / (1.0 + jnp.exp(-x))


def conv_of(buf, taps, sl):
    total = taps[0:1, sl] * buf[5 : 5 + CHUNK, sl]
    for i in range(1, 4):
        total = total + taps[i : i + 1, sl] * buf[5 + i : 5 + i + CHUNK, sl]
    return total


def softplus(x):
    return jnp.maximum(x, 0.0) + jnp.log1p(jnp.exp(-jnp.abs(x)))


def unit(a):
    r = lax.rsqrt(jnp.sum(a * a, axis=-1, keepdims=True) + NORM_EPS)
    return a * r, r


def mixer_forward_kernel(
    heads, pq, pk, pv, pg, ps, cq, ck, cv, rates, bias, gain,
    mixed, t_out, s_out, f_out, bq, bk, bv, state,
):
    step = pl.program_id(1)

    @pl.when(step == 0)
    def _():
        state[...] = jnp.zeros_like(state)
        for b in (bq, bk, bv):
            b[0:8, :] = jnp.zeros((8, b.shape[1]), F32)

    @pl.when(step > 0)
    def _():
        for b in (bq, bk, bv):
            b[0:8, :] = b[CHUNK : CHUNK + 8, :]

    for b, p in ((bq, pq), (bk, pk), (bv, pv)):
        b[8 : CHUNK + 8, :] = p[0].astype(F32)
    row, col = iotas(CHUNK)
    small = ps[0]
    g = rates[...] * softplus(small + bias[...])
    beta_all = sigmoid(small)
    cum = exact((row >= col).astype(F32), g)
    cum_t = cum.T
    hs = range(heads)
    ks = [slice(h * DK, (h + 1) * DK) for h in hs]
    vs = [slice(h * DV, (h + 1) * DV) for h in hs]
    q, k, v, within, kbeta, gamma, rem, last = [], [], [], [], [], [], [], []
    for h in hs:
        a = conv_of(bq, cq, ks[h])
        q.append(unit(a * sigmoid(a))[0])
        a = conv_of(bk, ck, ks[h])
        k.append(unit(a * sigmoid(a))[0])
        a = conv_of(bv, cv, vs[h])
        v.append(a * sigmoid(a))
        gc = cum[:, h : h + 1]
        within.append(jnp.exp(jnp.where(row >= col, gc - cum_t[h : h + 1, :], -1e30)))
        kbeta.append(beta_all[:, heads + h : heads + h + 1])
        gamma.append(jnp.exp(gc))
        tail = cum[CHUNK - 1 : CHUNK, h : h + 1]
        rem.append(jnp.exp(tail - gc))
        last.append(jnp.exp(tail))
    kb = [x.astype(BF) for x in k]
    lowers = [
        jnp.where(row > col, kbeta[h] * (mm(kb[h], kb[h], NT) * within[h]), 0.0) for h in hs
    ]
    scores = [mm(q[h], kb[h], NT) * within[h] for h in hs]
    inv = lower_inverses(lowers)
    states = [state[h] for h in hs]
    sb = [s.astype(BF) for s in states]
    both = [
        mm(jnp.concatenate([gamma[h] * k[h], gamma[h] * q[h]], axis=0), sb[h]) for h in hs
    ]
    fresh = [mm(inv[h], kbeta[h] * (v[h] - both[h][:CHUNK])) for h in hs]
    fb = [x.astype(BF) for x in fresh]
    out = [(both[h][CHUNK:] + mm(scores[h], fb[h])) * DK**-0.5 for h in hs]
    for h in hs:
        state[h] = last[h] * states[h] + mm(rem[h] * k[h], fb[h], TN)
        t_out[0, 0, h] = inv[h].astype(t_out.dtype)
        s_out[0, 0, h] = sb[h]
        f_out[0, :, vs[h]] = fb[h]
        o = out[h]
        r = lax.rsqrt(jnp.mean(o * o, axis=-1, keepdims=True) + NORM_EPS)
        pgh = pg[0, :, vs[h]].astype(F32)
        mixed[0, :, vs[h]] = (o * r * gain[...] * (pgh * sigmoid(pgh))).astype(mixed.dtype)


def mixer_backward_kernel(
    heads, dm, pq, pk, pv, pg, ps, tq, tk, tv, cq, ck, cv, rates, bias, gain, t_in, s_in, f_in,
    gqks, gvg, dcq, dck, dcv, dsm, dgain,
    bq, bk, bv, eq, ek, ev, dstate,
):
    row_at = pl.program_id(0)
    step = pl.program_id(1)
    chunk = pl.num_programs(1) - 1 - step

    @pl.when((row_at == 0) & (step == 0))
    def _():
        for r in (dcq, dck, dcv, dsm, dgain):
            r[...] = jnp.zeros_like(r)

    @pl.when(step == 0)
    def _():
        dstate[...] = jnp.zeros_like(dstate)
        for b in (eq, ek, ev):
            b[CHUNK : CHUNK + 8, :] = jnp.zeros((8, b.shape[1]), F32)

    @pl.when(step > 0)
    def _():
        for b in (eq, ek, ev):
            b[CHUNK : CHUNK + 8, :] = b[0:8, :]

    has_before = (chunk > 0).astype(F32)
    for b, p, t in ((bq, pq, tq), (bk, pk, tk), (bv, pv, tv)):
        b[0:8, :] = t[0].astype(F32) * has_before
        b[8 : CHUNK + 8, :] = p[0].astype(F32)
    row, col = iotas(CHUNK)
    lane = col
    small = ps[0]
    shifted = small + bias[...]
    g = rates[...] * softplus(shifted)
    beta_all = sigmoid(small)
    cum = exact((row >= col).astype(F32), g)
    cum_t = cum.T
    hs = range(heads)
    ks = [slice(h * DK, (h + 1) * DK) for h in hs]
    vs = [slice(h * DV, (h + 1) * DV) for h in hs]
    scale = DK**-0.5
    dcum = jnp.zeros((CHUNK, CHUNK), F32)
    dcum_rows = jnp.zeros((CHUNK, CHUNK), F32)
    dbeta = jnp.zeros((CHUNK, CHUNK), F32)
    head_dgain = jnp.zeros((1, DV), F32)
    q, k, v, rq, rk, kbeta, gamma, rem, last, within = [], [], [], [], [], [], [], [], [], []
    for h in hs:
        a = conv_of(bq, cq, ks[h])
        x, r = unit(a * sigmoid(a))
        q.append(x)
        rq.append(r)
        a = conv_of(bk, ck, ks[h])
        x, r = unit(a * sigmoid(a))
        k.append(x)
        rk.append(r)
        a = conv_of(bv, cv, vs[h])
        v.append(a * sigmoid(a))
        gc = cum[:, h : h + 1]
        within.append(jnp.exp(jnp.where(row >= col, gc - cum_t[h : h + 1, :], -1e30)))
        kbeta.append(beta_all[:, heads + h : heads + h + 1])
        gamma.append(jnp.exp(gc))
        tail = cum[CHUNK - 1 : CHUNK, h : h + 1]
        rem.append(jnp.exp(tail - gc))
        last.append(jnp.exp(tail))
    qb = [x.astype(BF) for x in q]
    kb = [x.astype(BF) for x in k]
    sb = [s_in[0, 0, h] for h in hs]
    fb = [f_in[0, :, vs[h]] for h in hs]
    tb = [t_in[0, 0, h].astype(BF) for h in hs]
    gram = [mm(kb[h], kb[h], NT) * within[h] for h in hs]
    scores = [mm(qb[h], kb[h], NT) * within[h] for h in hs]
    gk_gq = [
        jnp.concatenate([gamma[h] * k[h], gamma[h] * q[h]], axis=0) for h in hs
    ]
    both = [mm(gk_gq[h], sb[h]) for h in hs]
    x_in = [v[h] - both[h][:CHUNK] for h in hs]
    out = [(both[h][CHUNK:] + mm(scores[h], fb[h])) * scale for h in hs]
    dout = []
    for h in hs:
        o = out[h]
        r = lax.rsqrt(jnp.mean(o * o, axis=-1, keepdims=True) + NORM_EPS)
        n = o * r
        p = pg[0, :, vs[h]].astype(F32)
        s = sigmoid(p)
        d = dm[0, :, vs[h]].astype(F32)
        y = n * gain[...]
        at = heads * DV + h * DV
        gvg[0, :, at : at + DV] = (d * y * (s * (1.0 + p * (1.0 - s)))).astype(BF)
        dy = d * (p * s)
        head_dgain = head_dgain + jnp.sum(dy * n, axis=0, keepdims=True)
        dn = dy * gain[...]
        dout.append(scale * r * (dn - n * jnp.mean(n * dn, axis=-1, keepdims=True)))
    dob = [x.astype(BF) for x in dout]
    ds_next = [dstate[h] for h in hs]
    dsb = [x.astype(BF) for x in ds_next]
    krem = [rem[h] * k[h] for h in hs]
    dfresh = [mm(scores[h], dob[h], TN) + mm(krem[h], dsb[h]) for h in hs]
    dr = [mm(tb[h], dfresh[h], TN) for h in hs]
    drb = [x.astype(BF) for x in dr]
    dx = [kbeta[h] * dr[h] for h in hs]
    dx_do = [jnp.concatenate([-dx[h], dout[h]], axis=0).astype(BF) for h in hs]
    for h in hs:
        dstate[h] = last[h] * ds_next[h] + mm(gk_gq[h], dx_do[h], TN)
    dgk_gq = [mm(dx_do[h], sb[h], NT) for h in hs]
    dkrem = [mm(fb[h], dsb[h], NT) for h in hs]
    dscore = [mm(dob[h], fb[h], NT) for h in hs]
    dlow = [jnp.where(row > col, -mm(drb[h], fb[h], NT), 0.0) for h in hs]
    for h in hs:
        m = dscore[h] * within[h]
        dgram = kbeta[h] * (dlow[h] * within[h])
        lg = dlow[h] * gram[h]
        e = dscore[h] * scores[h] + kbeta[h] * lg
        dq = gamma[h] * dgk_gq[h][CHUNK:] + mm(m, kb[h])
        mk = jnp.concatenate([m, dgram], axis=0)
        dk = (
            gamma[h] * dgk_gq[h][:CHUNK]
            + rem[h] * dkrem[h]
            + mm(mk, jnp.concatenate([qb[h], kb[h]], axis=0), TN)
            + mm(dgram, kb[h])
        )
        rem_part = jnp.sum(dkrem[h] * krem[h], axis=-1, keepdims=True)
        head_dcum = (
            jnp.sum(e, axis=-1, keepdims=True)
            + jnp.sum(
                dgk_gq[h][:CHUNK] * gk_gq[h][:CHUNK] + dgk_gq[h][CHUNK:] * gk_gq[h][CHUNK:],
                axis=-1, keepdims=True,
            )
            - rem_part
        )
        state_part = jnp.sum(
            jnp.sum(ds_next[h] * sb[h].astype(F32), axis=0, keepdims=True), axis=1, keepdims=True
        )
        end_part = jnp.sum(rem_part, axis=0, keepdims=True) + last[h] * state_part
        head_dcum = head_dcum + jnp.where(row[:, 0:1] == CHUNK - 1, end_part, 0.0)
        dcum = dcum + jnp.where(lane == h, head_dcum, 0.0)
        dcum_rows = dcum_rows + jnp.where(row == h, jnp.sum(e, axis=0, keepdims=True), 0.0)
        head_dbeta = jnp.sum(dr[h] * x_in[h], axis=-1, keepdims=True) + jnp.sum(
            lg, axis=-1, keepdims=True
        )
        dbeta = dbeta + jnp.where(lane == heads + h, head_dbeta, 0.0)
        a = conv_of(bq, cq, ks[h])
        s = sigmoid(a)
        da = rq[h] * (dq - q[h] * jnp.sum(q[h] * dq, axis=-1, keepdims=True))
        eq[0:CHUNK, ks[h]] = da * (s * (1.0 + a * (1.0 - s)))
        a = conv_of(bk, ck, ks[h])
        s = sigmoid(a)
        da = rk[h] * (dk - k[h] * jnp.sum(k[h] * dk, axis=-1, keepdims=True))
        ek[0:CHUNK, ks[h]] = da * (s * (1.0 + a * (1.0 - s)))
        a = conv_of(bv, cv, vs[h])
        s = sigmoid(a)
        ev[0:CHUNK, vs[h]] = dx[h] * (s * (1.0 + a * (1.0 - s)))
    dgain[0:1, :] += head_dgain
    dcum = dcum - dcum_rows.T
    dg = exact((row >= col).astype(F32), dcum, TN)
    dshift = dg * rates[...] * sigmoid(shifted)
    dsm[0:1, :] += jnp.sum(dg * g, axis=0, keepdims=True)
    dsm[1:2, :] += jnp.sum(dshift, axis=0, keepdims=True)
    gqks[0, :, 2 * heads * DK :] = (
        jnp.where(lane < heads, dshift, 0.0) + dbeta * beta_all * (1.0 - beta_all)
    ).astype(BF)
    for b, e, taps, dtaps, out_ref, start in (
        (bq, eq, cq, dcq, gqks, 0), (bk, ek, ck, dck, gqks, heads * DK), (bv, ev, cv, dcv, gvg, 0),
    ):
        for at in range(0, b.shape[1], DK):
            sl = slice(at, at + DK)
            own = e[0:CHUNK, sl]
            total = taps[3:4, sl] * own
            for i in range(3):
                total = total + taps[i : i + 1, sl] * e[3 - i : 3 - i + CHUNK, sl]
            out_ref[0, :, start + at : start + at + DK] = total.astype(BF)
            for i in range(4):
                dtaps[i : i + 1, sl] += jnp.sum(
                    own * b[5 + i : 5 + i + CHUNK, sl], axis=0, keepdims=True
                )


def whole_spec(shape):
    return pl.BlockSpec(shape, lambda r, c: (0,) * len(shape))


def lane_pad(vec, at):
    return jnp.zeros((1, 128), F32).at[0, at : at + vec.shape[0]].set(vec)


def mixer_forward(pqks, pvg, cq, ck, cv, log_rates, rate_bias, gain):
    rows, length, value_width = pvg.shape
    value_width = value_width // 2
    key_width = value_width * DK // DV
    heads = key_width // DK
    chunks = length // CHUNK
    seq = lambda width, at=0: pl.BlockSpec((1, CHUNK, width), lambda r, c: (r, c, at))
    per = lambda a, b: pl.BlockSpec((1, 1, heads, a, b), lambda r, c: (r, c, 0, 0, 0))
    return pl.pallas_call(
        functools.partial(mixer_forward_kernel, heads),
        grid=(rows, chunks),
        in_specs=[seq(key_width), seq(key_width, 1), seq(value_width), seq(value_width, 1),
                  seq(128, 2 * heads),
                  whole_spec((4, key_width)), whole_spec((4, key_width)), whole_spec((4, value_width)),
                  whole_spec((1, 128)), whole_spec((1, 128)), whole_spec((1, DV))],
        out_specs=[seq(value_width), per(CHUNK, CHUNK), per(DK, DV), seq(value_width)],
        out_shape=[
            jax.ShapeDtypeStruct((rows, length, value_width), BF),
            jax.ShapeDtypeStruct((rows, chunks, heads, CHUNK, CHUNK), BF),
            jax.ShapeDtypeStruct((rows, chunks, heads, DK, DV), BF),
            jax.ShapeDtypeStruct((rows, length, value_width), BF),
        ],
        scratch_shapes=[
            pltpu.VMEM((CHUNK + 8, key_width), F32),
            pltpu.VMEM((CHUNK + 8, key_width), F32),
            pltpu.VMEM((CHUNK + 8, value_width), F32),
            pltpu.VMEM((heads, DK, DV), F32),
        ],
        compiler_params=pltpu.CompilerParams(
            dimension_semantics=("arbitrary", "arbitrary"), vmem_limit_bytes=40 << 20
        ),
        cost_estimate=pl.CostEstimate(flops=0, bytes_accessed=int(rows * chunks * heads * 3500000.0), transcendentals=0),
        name="mixer_forward",
    )(pqks, pqks, pvg, pvg, pqks, cq, ck, cv, lane_pad(-jnp.exp(log_rates), 0),
      lane_pad(rate_bias, 0), gain.reshape(1, DV))


def mixer_backward(dm, pqks, pvg, cq, ck, cv, log_rates, rate_bias, gain, t_in, s_in, f_in):
    rows, length, value_width = dm.shape
    key_width = value_width * DK // DV
    heads = key_width // DK
    chunks = length // CHUNK
    seq = lambda width, at=0: pl.BlockSpec(
        (1, CHUNK, width), lambda r, c: (r, chunks - 1 - c, at)
    )
    before = lambda width, at=0: pl.BlockSpec(
        (1, 8, width),
        lambda r, c: (r, jnp.maximum((chunks - 1 - c) * (CHUNK // 8) - 1, 0), at),
    )
    per = lambda a, b: pl.BlockSpec(
        (1, 1, heads, a, b), lambda r, c: (r, chunks - 1 - c, 0, 0, 0)
    )
    seq_shape = lambda width: jax.ShapeDtypeStruct((rows, length, width), BF)
    return pl.pallas_call(
        functools.partial(mixer_backward_kernel, heads),
        grid=(rows, chunks),
        in_specs=[seq(value_width), seq(key_width), seq(key_width, 1), seq(value_width),
                  seq(value_width, 1), seq(128, 2 * heads),
                  before(key_width), before(key_width, 1), before(value_width),
                  whole_spec((4, key_width)), whole_spec((4, key_width)), whole_spec((4, value_width)),
                  whole_spec((1, 128)), whole_spec((1, 128)), whole_spec((1, DV)),
                  per(CHUNK, CHUNK), per(DK, DV), seq(value_width)],
        out_specs=[seq(2 * key_width + 128), seq(2 * value_width),
                   whole_spec((8, key_width)), whole_spec((8, key_width)), whole_spec((8, value_width)),
                   whole_spec((8, 128)), whole_spec((8, DV))],
        out_shape=[seq_shape(2 * key_width + 128), seq_shape(2 * value_width),
                   jax.ShapeDtypeStruct((8, key_width), F32),
                   jax.ShapeDtypeStruct((8, key_width), F32),
                   jax.ShapeDtypeStruct((8, value_width), F32),
                   jax.ShapeDtypeStruct((8, 128), F32),
                   jax.ShapeDtypeStruct((8, DV), F32)],
        scratch_shapes=[
            pltpu.VMEM((CHUNK + 8, key_width), F32),
            pltpu.VMEM((CHUNK + 8, key_width), F32),
            pltpu.VMEM((CHUNK + 8, value_width), F32),
            pltpu.VMEM((CHUNK + 8, key_width), F32),
            pltpu.VMEM((CHUNK + 8, key_width), F32),
            pltpu.VMEM((CHUNK + 8, value_width), F32),
            pltpu.VMEM((heads, DK, DV), F32),
        ],
        compiler_params=pltpu.CompilerParams(
            dimension_semantics=("arbitrary", "arbitrary"), vmem_limit_bytes=48 << 20
        ),
        cost_estimate=pl.CostEstimate(flops=0, bytes_accessed=int(rows * chunks * heads * 5304687.5), transcendentals=0),
        name="mixer_backward",
    )(dm, pqks, pqks, pvg, pvg, pqks, pqks, pqks, pvg, cq, ck, cv, lane_pad(-jnp.exp(log_rates), 0),
      lane_pad(rate_bias, 0), gain.reshape(1, DV), t_in, s_in, f_in)


FREE = pl.CostEstimate(flops=0, bytes_accessed=0, transcendentals=0)
VMEM_LIMIT = 44 << 20


def rows_kernel(count, nt, has_weigh, at, *refs):
    out = refs[-2] if has_weigh else refs[-1]
    total = None
    for i in range(count):
        part = lax.dot_general(
            refs[2 * i][0], refs[2 * i + 1][...], NT if nt else NN, preferred_element_type=F32
        )
        total = part if total is None else total + part
    if has_weigh:
        refs[-1][0, 0:1, :] = jnp.sum(
            total * refs[2 * count][0].astype(F32), axis=0, keepdims=True
        )
    out[0] = total.astype(out.dtype)


def rows_matmul(pairs, piece, nt=False, tile=512, take=0, weigh=None, into=None, put=0, dtype=BF):
    rows = pairs[0][0].shape[0]
    width = pairs[0][1].shape[0 if nt else 1]
    tile = min(tile, width)
    at = jnp.stack([jnp.int32(take), jnp.int32(put)])
    specs, args = [], []
    for a, w in pairs:
        depth = a.shape[2]
        specs.append(pl.BlockSpec((1, piece, depth), lambda r, n, at: (r, at[0], 0)))
        if nt:
            specs.append(pl.BlockSpec((tile, depth), lambda r, n, at: (n, 0)))
        else:
            specs.append(pl.BlockSpec((depth, tile), lambda r, n, at: (0, n)))
        args.extend((a, w))
    if weigh is not None:
        specs.append(pl.BlockSpec((1, piece, tile), lambda r, n, at: (r, 0, n)))
        args.append(weigh)
    aliases = {}
    shape = (rows, piece, width)
    if into is not None:
        shape = into.shape
        dtype = into.dtype
        if not isinstance(into, jax.ShapeDtypeStruct):
            specs.append(pl.BlockSpec(memory_space=pl.ANY))
            args.append(into)
            aliases = {len(args): 0}
    out_specs = [pl.BlockSpec((1, piece, tile), lambda r, n, at: (r, at[1], n))]
    out_shape = [jax.ShapeDtypeStruct(shape, dtype)]
    if weigh is not None:
        out_specs.append(pl.BlockSpec((1, 8, tile), lambda r, n, at: (r, 0, n)))
        out_shape.append(jax.ShapeDtypeStruct((rows, 8, width), F32))
    out = pl.pallas_call(
        functools.partial(rows_kernel, len(pairs), nt, weigh is not None),
        grid_spec=pltpu.PrefetchScalarGridSpec(
            num_scalar_prefetch=1,
            grid=(rows, pl.cdiv(width, tile)),
            in_specs=specs,
            out_specs=out_specs,
        ),
        out_shape=out_shape,
        input_output_aliases=aliases,
        compiler_params=pltpu.CompilerParams(
            dimension_semantics=("arbitrary", "arbitrary"), vmem_limit_bytes=VMEM_LIMIT
        ),
        cost_estimate=FREE,
        name="rows_matmul",
    )(at, *args)
    return out[0] if weigh is None else (out[0], jnp.sum(out[1][:, 0], axis=0))


def outer_kernel(count, blocks, at, *refs):
    xs, gs = refs[:count], refs[count : 2 * count]
    out, flipped = refs[-2:]
    rows, piece, width = xs[0].shape
    depth = rows * piece
    block = flipped.shape[0] // blocks

    @pl.when(pl.program_id(0) == 0)
    def _():
        for i, x in enumerate(xs):
            for k in range(blocks):
                start = pl.multiple_of((2 * k + at[0]) * block, block)
                part = x[:, :, pl.ds(start, block)].reshape(depth, block)
                flipped[k * block : (k + 1) * block, i * depth : (i + 1) * depth] = part.T

    total = None
    for i, g in enumerate(gs):
        part = lax.dot_general(
            flipped[:, i * depth : (i + 1) * depth],
            g[...].reshape(depth, g.shape[2]),
            NN,
            preferred_element_type=F32,
        )
        total = part if total is None else total + part
    for extra in refs[2 * count : -2]:
        total = total + extra[...].astype(F32)
    out[...] = total.astype(out.dtype)


def outer_sum(xs, gs, places, core, data, tile=512, adds=(), dtype=BF):
    rows, piece, width = xs[0].shape
    columns = gs[0].shape[2]
    tile = min(tile, columns)
    at = jnp.stack([jnp.int32(core)] + [jnp.int32(x) for x in places])
    specs = [pl.BlockSpec((rows, piece, width), lambda n, at: (0, 0, 0))] * len(xs)
    for i in range(len(gs)):
        specs.append(
            pl.BlockSpec((rows, piece, tile), lambda n, at, i=i: (0, at[1 + i], n))
        )
    args = [*xs, *gs]
    out_spec = pl.BlockSpec((width // 2, tile), lambda n, at: (0, n))
    for extra in adds:
        specs.append(out_spec)
        args.append(extra)
    return pl.pallas_call(
        functools.partial(outer_kernel, len(xs), data // 2),
        grid_spec=pltpu.PrefetchScalarGridSpec(
            num_scalar_prefetch=1,
            grid=(columns // tile,),
            in_specs=specs,
            out_specs=out_spec,
            scratch_shapes=[pltpu.VMEM((width // 2, len(xs) * rows * piece), BF)],
        ),
        out_shape=jax.ShapeDtypeStruct((width // 2, columns), dtype),
        compiler_params=pltpu.CompilerParams(
            dimension_semantics=("arbitrary",), vmem_limit_bytes=VMEM_LIMIT
        ),
        cost_estimate=FREE,
        name="outer_sum",
    )(at, *args)


UNITS = 256


def lanes_of(units):
    return 128 if units % 128 == 0 else 64


def mlp_kernel(lanes, x, wgu, g, wd, hidden, grads):
    mlp_finish(lanes, lax.dot_general(x[...], wgu[...], NN, preferred_element_type=F32), g, wd, hidden, grads)


def mlp_finish(lanes, both, g, wd, hidden, grads):
    back = lax.dot_general(g[...], wd[...], NN, preferred_element_type=F32)
    for at in range(0, UNITS, lanes):
        first, second = 2 * at, 2 * at + lanes
        gate = both[:, first : first + lanes]
        up = both[:, second : second + lanes]
        own = back[:, at : at + lanes]
        sig = sigmoid(gate)
        act = gate * sig
        hidden[:, at : at + lanes] = (act * up).astype(BF)
        own_gate = own * up * (sig * (1.0 + gate * (1.0 - sig)))
        grads[:, first : first + lanes] = own_gate.astype(BF)
        grads[:, second : second + lanes] = (own * act).astype(BF)


def mlp_block(g, wd, x=None, wgu=None, both=None):
    piece, width = g.shape
    units = wd.shape[1]
    whole = pl.BlockSpec((piece, width), lambda n: (0, 0))
    part = lambda depth, size: pl.BlockSpec((depth, size), lambda n: (0, n))
    if both is None:
        kernel, args = mlp_kernel, (x, wgu, g, wd)
        specs = [whole, part(width, 2 * UNITS), whole, part(width, UNITS)]
    else:
        kernel, args = mlp_finish, (both, g, wd)
        specs = [part(piece, 2 * UNITS), whole, part(width, UNITS)]
    return pl.pallas_call(
        functools.partial(kernel, lanes_of(units)),
        grid=(pl.cdiv(units, UNITS),),
        in_specs=specs,
        out_specs=[part(piece, UNITS), part(piece, 2 * UNITS)],
        out_shape=[
            jax.ShapeDtypeStruct((piece, units), BF),
            jax.ShapeDtypeStruct((piece, 2 * units), BF),
        ],
        compiler_params=pltpu.CompilerParams(
            dimension_semantics=("arbitrary",), vmem_limit_bytes=VMEM_LIMIT
        ),
        cost_estimate=FREE,
        name="mlp_block",
    )(*args)


NORM_ROWS = 128


def row_stats(x):
    r = lax.rsqrt(jnp.mean(x * x, axis=-1, keepdims=True) + NORM_EPS)
    return x * r, r


def norm_grad(n, r, inner):
    return r * (inner - n * jnp.mean(n * inner, axis=-1, keepdims=True))


def valid_rows(at):
    start = at[0] + pl.program_id(1) * NORM_ROWS
    positions = start + lax.broadcasted_iota(jnp.int32, (NORM_ROWS, 1), 0)
    return (positions < at[1 + pl.program_id(0)]).astype(F32)


def enter_kernel(at, tokens, gain, normed):
    normed[0] = (row_stats(tokens[0].astype(F32))[0] * gain[...]).astype(BF)


def middle_kernel(at, own, moved, tokens, gain, middle, normed):
    total = own[0] + moved[0].astype(F32)
    x = tokens[0].astype(F32) + valid_rows(at) * total
    middle[0] = x
    normed[0] = (row_stats(x)[0] * gain[...]).astype(BF)


def middle_back_kernel(at, own, moved, middle, cot, gain, grad_middle, grad_attn, dgain):
    @pl.when((pl.program_id(0) == 0) & (pl.program_id(1) == 0))
    def _():
        dgain[...] = jnp.zeros_like(dgain)

    grad = own[0] + moved[0].astype(F32)
    n, r = row_stats(middle[0])
    dgain[0:1, :] += jnp.sum(grad * n, axis=0, keepdims=True)
    total = cot[0].astype(F32) + norm_grad(n, r, gain[...] * grad)
    grad_middle[0] = total
    grad_attn[0] = (valid_rows(at) * total).astype(BF)


def leave_kernel(at, own, moved, tokens, grad_middle, gain, out):
    grad = own[0] + moved[0].astype(F32)
    n, r = row_stats(tokens[0].astype(F32))
    out[0] = (grad_middle[0] + norm_grad(n, r, gain[...] * grad)).astype(BF)


def result_kernel(at, own, moved, middle, out):
    total = own[0] + moved[0].astype(F32)
    out[0] = (middle[0] + valid_rows(at) * total).astype(BF)


def by_rows(kernel, at, arrays, gain, out_types, with_sum=False):
    rows, piece, width = arrays[0].shape
    block = pl.BlockSpec((1, NORM_ROWS, width), lambda r, t, at: (r, t, 0))
    out_shape = [jax.ShapeDtypeStruct((rows, piece, width), x) for x in out_types]
    out_specs = [block] * len(out_types)
    specs = [block] * len(arrays)
    args = list(arrays)
    if gain is not None:
        specs.append(pl.BlockSpec((1, width), lambda r, t, at: (0, 0)))
        args.append(gain.reshape(1, width))
    if with_sum:
        out_shape.append(jax.ShapeDtypeStruct((8, width), F32))
        out_specs.append(pl.BlockSpec((8, width), lambda r, t, at: (0, 0)))
    return pl.pallas_call(
        kernel,
        grid_spec=pltpu.PrefetchScalarGridSpec(
            num_scalar_prefetch=1,
            grid=(rows, piece // NORM_ROWS),
            in_specs=specs,
            out_specs=out_specs,
        ),
        out_shape=out_shape,
        compiler_params=pltpu.CompilerParams(
            dimension_semantics=("arbitrary", "arbitrary"), vmem_limit_bytes=VMEM_LIMIT
        ),
        cost_estimate=FREE,
        name=kernel.__name__,
    )(at, *args)


def ring(size, group):
    return [(i, i // group * group + (i + 1) % group) for i in range(size)]


def across(size):
    return [(i, (i + size // 2) % size) for i in range(size)]


def swap(size, bit):
    return [(i, i ^ bit) for i in range(size)]


def tie(*values):
    return lax.optimization_barrier(values)


def matmul(a, b):
    return lax.dot_general(a, b, NN, preferred_element_type=F32)


def sum_small(flat, sizes):
    for axis in ("dp", "head"):
        bit = 1
        while bit < sizes[axis]:
            flat = flat + lax.ppermute(flat, axis, swap(sizes[axis], bit))
            bit = bit * 2
    return flat


def alternate(gate, up):
    rows, units = gate.shape
    lanes = lanes_of(units)
    parts = [x.reshape(rows, units // lanes, lanes) for x in (gate, up)]
    pair = jnp.stack(parts, axis=2)
    return pair.reshape(rows, 2 * units)


def apart(both):
    rows, units = both.shape[0], both.shape[1] // 2
    lanes = lanes_of(units)
    pair = both.reshape(rows, units // lanes, 2, lanes)
    return pair[:, :, 0].reshape(rows, units), pair[:, :, 1].reshape(rows, units)


def per_device(
    tokens,
    lengths,
    gain_attn,
    w_query,
    w_key,
    w_value,
    w_decay,
    w_beta,
    w_gate_out,
    conv_query,
    conv_key,
    conv_value,
    decay_log,
    decay_bias,
    gain_head,
    w_out,
    gain_mlp,
    w_gate,
    w_up,
    w_down,
    cotangent,
):
    rows, piece, width = tokens.shape
    size = lax.axis_size("head")
    data = lax.axis_size("dp")
    me = lax.axis_index("head")
    core = lax.rem(lax.axis_index("dp"), 2)
    length = piece * size
    heads = w_decay.shape[1]
    key_width, value_width = heads * DK, heads * DV
    shape3 = (rows, piece, width)
    flat_piece = rows * piece
    group = size // 2
    at = jnp.concatenate([(me * piece).astype(jnp.int32)[None], lengths])
    positions = me * piece + jnp.arange(piece, dtype=jnp.int32)
    mask = (positions[None, :] < lengths[:, None]).astype(F32)[:, :, None]

    def owner(s):
        return lax.rem(me + size - s, size)

    def step(x, group):
        return lax.ppermute(x, "head", ring(size, group))

    def opposite(x):
        return lax.ppermute(x, "head", across(size))

    def gather_weight(w):
        return lax.all_gather(w, "dp", axis=0, tiled=True)

    def outer_halves(xs, gs, places, tile=512):
        away = outer_sum(xs, gs, places, 1 - core, data, tile)
        moved = lax.ppermute(away, "dp", swap(data, 1))
        return outer_sum(xs, gs, places, core, data, tile, (moved,))

    def scatter_weight(total):
        places = [[i + c for i in range(0, data, 2)] for c in range(2)]
        return lax.psum_scatter(
            total, "dp", scatter_dimension=0, tiled=True, axis_index_groups=places
        )

    normed = by_rows(enter_kernel, at, [tokens], gain_attn, [BF])[0]
    small_pad = jnp.zeros((w_decay.shape[0], 128 - 2 * heads), BF)
    w_qks = gather_weight(jnp.concatenate([w_query, w_key, w_decay, w_beta, small_pad], axis=1))
    w_vg = gather_weight(jnp.concatenate([w_value, w_gate_out], axis=1))
    wo_full = gather_weight(w_out)

    qks_buffer = jax.ShapeDtypeStruct((rows, length, 2 * key_width + 128), F32)
    vg_buffer = jax.ShapeDtypeStruct((rows, length, 2 * value_width), F32)
    def project_qks(item, s, into):
        return rows_matmul([(item, w_qks)], piece, tile=into.shape[2], into=into, put=owner(s))

    def project_vg(item, s, into):
        return rows_matmul([(item, w_vg)], piece, into=into, put=owner(s))

    pqks = project_qks(normed, 0, qks_buffer)
    pvg = vg_buffer
    pieces = [normed]
    for s in range(1, size):
        send = pieces[-1]
        if s == 1:
            send, w_gate, w_up, cotangent = tie(send, w_gate, w_up, cotangent)
        item = step(send, size)
        if s == 1:
            w_gu = alternate(w_gate, w_up)
            grad_mlp = (mask * cotangent.astype(F32)).astype(BF)
            item, w_gu, grad_mlp = tie(item, w_gu, grad_mlp)
        if s == size - 1:
            for place, early in enumerate(pieces):
                pvg = project_vg(early, place, pvg)
            item, pqks, pvg, w_gu, w_down = tie(item, pqks, pvg, w_gu, w_down)
        elif s > 1:
            item, pqks = tie(item, pqks)
        pqks = project_qks(item, s, pqks)
        pieces.append(item)
    normed_pieces = pieces
    w_gu_other = opposite(w_gu)
    w_down_other = opposite(w_down)
    pvg = project_vg(item, size - 1, pvg)

    cq = lax.dynamic_slice_in_dim(conv_query, me * key_width, key_width, 1)
    ck = lax.dynamic_slice_in_dim(conv_key, me * key_width, key_width, 1)
    cv = lax.dynamic_slice_in_dim(conv_value, me * value_width, value_width, 1)
    log_local = lax.dynamic_slice_in_dim(decay_log, me * heads, heads, 0)
    bias_local = lax.dynamic_slice_in_dim(decay_bias, me * heads, heads, 0)
    mixed, t_kept, s_kept, f_kept = mixer_forward(
        pqks, pvg, cq, ck, cv, log_local, bias_local, gain_head
    )
    mixed, w_gu_other, w_down_other = tie(mixed, w_gu_other, w_down_other)
    wgu_full = [gather_weight(w_gu), gather_weight(w_gu_other)]
    wdown_full = [gather_weight(w_down), gather_weight(w_down_other)]

    def attn_part(s, dtype=F32):
        return rows_matmul([(mixed, wo_full)], piece, nt=True, take=owner(s), dtype=dtype)

    total = attn_part(1, BF)
    for s in range(2, size + 1):
        moved = step(total, size)
        own = attn_part(s % size)
        moved, own = tie(moved, own)
        total = (own + moved.astype(F32)).astype(BF)
    middle, normed_two = by_rows(middle_kernel, at, [own, moved, tokens], gain_mlp, [F32, BF])
    flat2 = lambda x: x.reshape(flat_piece, width)
    second, grad_out = [normed_two], [grad_mlp]
    hidden, grad_gu = [[], []], [[], []]

    def keep_block(b, block):
        hidden[b].append(block[0].reshape(rows, piece, -1))
        grad_gu[b].append(block[1].reshape(rows, piece, -1))

    def mlp_part(s, dtype=F32):
        pairs = [(hidden[b][s], wdown_full[b]) for b in range(2)]
        return rows_matmul(pairs, piece, nt=True, dtype=dtype)

    def two_part(s, dtype=F32):
        pairs = [(grad_gu[b][s], wgu_full[b]) for b in range(2)]
        return rows_matmul(pairs, piece, nt=True, dtype=dtype)

    send, own_x, own_g = tie(normed_two, normed_two, grad_mlp)
    for s in range(1, group):
        moved = step(send, group)
        if s == 1:
            for b in range(2):
                keep_block(b, mlp_block(flat2(own_g), wdown_full[b], flat2(own_x), wgu_full[b]))
            moved, *held = tie(moved, *hidden[0], *hidden[1], *grad_gu[0], *grad_gu[1])
            hidden, grad_gu = [held[:1], held[1:2]], [held[2:3], held[3:]]
        second.append(moved)
        send = moved
    send, *second = tie(grad_mlp, *second)
    for s in range(1, group):
        moved = step(send, group)
        if s == 1:
            own_two = two_part(0)
            begun = [
                [matmul(flat2(x), wgu_full[b]) for b in range(2)] for x in second[1:]
            ]
            begun = [x for pair in begun for x in pair]
            moved, own_two, *begun = tie(moved, own_two, *begun)
        grad_out.append(moved)
        send = moved
    for s in range(1, group):
        for b in range(2):
            both = begun[2 * (s - 1) + b]
            keep_block(b, mlp_block(flat2(grad_out[s]), wdown_full[b], both=both))
    total, hidden[0][1], hidden[1][1] = tie(two_part(1, BF), hidden[0][1], hidden[1][1])
    for s in range(2, group + 1):
        moved = step(total, group)
        if s == group:
            own = own_two
            own_mlp, send_mlp = mlp_part(0), mlp_part(1, BF)
            moved, own_mlp, send_mlp = tie(moved, own_mlp, send_mlp)
        else:
            own = two_part(s)
            total = (own + moved.astype(F32)).astype(BF)
    grad_middle, grad_attn, dgain_mlp = by_rows(
        middle_back_kernel, at, [own, moved, middle, cotangent], gain_mlp, [F32, BF], True
    )

    pair_gu, pair_down = [None, None], [None, None]
    first = [0] * group
    mixed_buffer = jax.ShapeDtypeStruct((rows, length, value_width), F32)
    grad_mixed = mixed_buffer
    attn_pieces = [grad_attn]
    for s in range(1, size):
        send = attn_pieces[-1]
        if s < 3:
            b = 2 - s
            send, *held = tie(send, *hidden[b], *grad_gu[b])
            hidden[b], grad_gu[b] = held[:group], held[group:]
        item = step(send, size)
        if s < 3:
            pair_down[b] = outer_halves(grad_out, hidden[b], first, hidden[b][0].shape[2])
            pair_gu[b] = outer_halves(second, grad_gu[b], first, 1408)
            item, pair_gu[b], pair_down[b] = tie(item, pair_gu[b], pair_down[b])
        if s == size - 1:
            for place, early in enumerate(attn_pieces):
                grad_mixed = rows_matmul(
                    [(early, wo_full)], piece, into=grad_mixed, put=owner(place)
                )
            wout_parts = [
                outer_sum(
                    attn_pieces, [mixed] * s, [owner(x) for x in range(s)], side, data, dtype=F32
                )
                for side in (1 - core, core)
            ]
            item, grad_mixed, *wout_parts = tie(item, grad_mixed, *wout_parts)
        attn_pieces.append(item)
    grad_mixed = rows_matmul([(item, wo_full)], piece, into=grad_mixed, put=owner(size - 1))
    sums_gu = [None, scatter_weight(pair_gu[1])]
    sums_down = [None, scatter_weight(pair_down[1])]
    sums_gu[0] = scatter_weight(pair_gu[0])
    sums_down[0] = scatter_weight(pair_down[0])

    grad_mixed, send_mlp, send_gu, send_down = tie(grad_mixed, send_mlp, sums_gu[1], sums_down[1])
    moved = step(send_mlp, group)
    moved_gu, moved_down = opposite(send_gu), opposite(send_down)
    done = mixer_backward(
        grad_mixed, pqks, pvg, cq, ck, cv, log_local, bias_local, gain_head, t_kept, s_kept, f_kept
    )
    moved, moved_gu, moved_down, gqks, gvg, dcq, dck, dcv, dsm, dgain = tie(
        moved, moved_gu, moved_down, *done
    )
    for s in range(2, group):
        moved = step((mlp_part(s) + moved.astype(F32)).astype(BF), group)
    mixed_rows = by_rows(result_kernel, at, [own_mlp, moved, middle], None, [BF])[0]

    def one_part(s, dtype=F32):
        return rows_matmul(
            [(gqks, w_qks), (gvg, w_vg)], piece, nt=True, take=owner(s),
            weigh=normed_pieces[s], dtype=dtype,
        )

    places = [owner(s) for s in range(size)]
    total, gain_sum = one_part(1, BF)
    for s in range(2, size + 1):
        if s == 2:
            total, gvg = tie(total, gvg)
        elif s == 3:
            total, gqks, *last = tie(total, gqks, sums_down[0], sums_gu[0], attn_pieces[-1])
            sums_down[0], sums_gu[0], attn_last = last
        moved = step(total, size)
        own, gain_part = one_part(s % size)
        if s == 2:
            pair_vg = outer_halves(normed_pieces, [gvg] * size, places)
            moved, own, gain_part, pair_vg = tie(moved, own, gain_part, pair_vg)
        elif s == 3:
            pair_qks = outer_halves(normed_pieces, [gqks] * size, places, gqks.shape[2])
            moved, own, gain_part, pair_qks = tie(moved, own, gain_part, pair_qks)
        else:
            moved, own, gain_part = tie(moved, own, gain_part)
        gain_sum = gain_sum + gain_part
        if s < size:
            total = (own + moved.astype(F32)).astype(BF)
    away = outer_sum([attn_last], [mixed], places[-1:], 1 - core, data, 512, wout_parts[:1])
    crossed = lax.ppermute(away, "dp", swap(data, 1))
    pair_wout = outer_sum(
        [attn_last], [mixed], places[-1:], core, data, 512, (wout_parts[1], crossed)
    )
    pair_wout, own, moved = tie(pair_wout, own, moved)
    tokens_grad = by_rows(
        leave_kernel, at, [own, moved, tokens, grad_middle], gain_attn, [BF]
    )[0]
    out_vg = scatter_weight(pair_vg).astype(F32)
    out_wout = scatter_weight(pair_wout).astype(F32)
    out_qks = scatter_weight(pair_qks).astype(F32)
    out_wgate, out_wup = apart(sums_gu[0].astype(F32) + moved_gu.astype(F32))
    out_wdown = sums_down[0].astype(F32) + moved_down.astype(F32)

    def spread(part, axis):
        shape = part.shape[:axis] + (size,) + part.shape[axis:]
        whole = jnp.zeros(shape, F32)
        whole = lax.dynamic_update_slice_in_dim(whole, jnp.expand_dims(part, axis), me, axis)
        return whole.reshape(part.shape[:axis] + (size * part.shape[axis],) + part.shape[axis + 1 :])

    small = (
        gain_sum / gain_attn,
        dgain_mlp[0],
        dgain[0],
        spread(dcq[:4], 1),
        spread(dck[:4], 1),
        spread(dcv[:4], 1),
        spread(dsm[0, :heads], 0),
        spread(dsm[1, :heads], 0),
    )
    total = sum(x.size for x in small)
    padded = -(-total // 1024) * 1024
    packed = jnp.concatenate(
        [x.reshape(-1) for x in small] + [jnp.zeros((padded - total,), F32)]
    ).reshape(padded // 128, 128)
    packed = sum_small(packed, {"dp": data, "head": size}).reshape(-1)
    sums = []
    start = 0
    for x in small:
        sums.append(packed[start : start + x.size].reshape(x.shape))
        start = start + x.size
    return (
        mixed_rows,
        tokens_grad,
        sums[0],
        out_qks[:, :key_width],
        out_qks[:, key_width : 2 * key_width],
        out_vg[:, :value_width],
        out_qks[:, 2 * key_width : 2 * key_width + heads],
        out_qks[:, 2 * key_width + heads : 2 * key_width + 2 * heads],
        out_vg[:, value_width:],
        sums[3],
        sums[4],
        sums[5],
        sums[6],
        sums[7],
        sums[2],
        out_wout,
        sums[1],
        out_wgate,
        out_wup,
        out_wdown,
    )

def solution(mesh):
    rows = P("dp", "head", None)
    weight = P("dp", "head")
    same = P()
    return jax.shard_map(
        per_device,
        mesh=mesh,
        in_specs=(
            rows, P("dp"), same, weight, weight, weight, weight, weight, weight, same, same, same,
            same, same, same, weight, same, weight, weight, weight, rows,
        ),
        out_specs=(
            rows, rows, same, weight, weight, weight, weight, weight, weight, same, same, same,
            same, same, same, weight, same, weight, weight, weight,
        ),
        check_vma=False,
    )
```

```python
import functools

import jax
import jax.numpy as jnp
from jax import lax
from jax.experimental import pallas as pl
from jax.experimental.pallas import tpu as pltpu
from jax.sharding import PartitionSpec as P

DK = 128
DV = 256
CHUNK = 128
STEP = 4
BACK_STEP = 2
NORM_EPS = 1e-06
BF = jnp.bfloat16
F32 = jnp.float32
NN = (((1,), (0,)), ((), ()))
NT = (((1,), (1,)), ((), ()))
TN = (((0,), (0,)), ((), ()))


def mm(a, b, dims=NN):
    return lax.dot_general(a.astype(BF), b.astype(BF), dims, preferred_element_type=F32)


def split(a):
    high = a.astype(BF)
    return high, (a - high.astype(F32)).astype(BF)


def mm3(a, b, dims=NN):
    ah, al = split(a)
    bh, bl = split(b)
    return mm(ah, bh, dims) + mm(ah, bl, dims) + mm(al, bh, dims)


def exact(a, b, dims=NN):
    return lax.dot_general(a, b, dims, precision=lax.Precision.HIGHEST, preferred_element_type=F32)


def iotas(n):
    return (
        lax.broadcasted_iota(jnp.int32, (n, n), 0),
        lax.broadcasted_iota(jnp.int32, (n, n), 1),
    )


def lower_inverses(lowers):
    n = lowers[0].shape[0]
    row, col = iotas(n)
    eye = (row == col).astype(F32)
    pair = (row // 2 == col // 2).astype(F32)
    inverses = [eye - low * pair for low in lowers]
    size = 2
    while size < n:
        corner = ((row // (2 * size)) == (col // (2 * size))) & ((row // size) != (col // size))
        corner = corner.astype(F32)
        half = [x.astype(BF) for x in inverses]
        inner = [mm(x, low * corner) for x, low in zip(half, lowers)]
        inverses = [x - mm(i, h) for x, i, h in zip(inverses, inner, half)]
        size = size * 2
    residual = [eye - x - mm3(low, x) for low, x in zip(lowers, inverses)]
    return [x + mm(x, r) for x, r in zip(inverses, residual)]


def sigmoid(x):
    return 1.0 / (1.0 + jnp.exp(-x))


def conv_of(buf, taps, sl, start=0):
    total = taps[0:1, sl] * buf[start + 5 : start + 5 + CHUNK, sl]
    for i in range(1, 4):
        total = total + taps[i : i + 1, sl] * buf[start + 5 + i : start + 5 + i + CHUNK, sl]
    return total


def softplus(x):
    return jnp.maximum(x, 0.0) + jnp.log1p(jnp.exp(-jnp.abs(x)))


def silu_slope(a):
    s = sigmoid(a)
    value = a * s
    return value, s + value * (1.0 - s)


def unit(a):
    r = lax.rsqrt(jnp.sum(a * a, axis=-1, keepdims=True) + NORM_EPS)
    return a * r, r


def mixer_forward_kernel(
    heads, pq, pk, pv, pg, ps, cq, ck, cv, rates, bias, gain,
    mixed, t_out, s_out, f_out, bq, bk, bv, state,
):
    step = pl.program_id(1)
    span = STEP * CHUNK

    @pl.when(step == 0)
    def _():
        state[...] = jnp.zeros_like(state)
        for b in (bq, bk, bv):
            b[0:8, :] = jnp.zeros((8, b.shape[1]), F32)

    @pl.when(step > 0)
    def _():
        for b in (bq, bk, bv):
            b[0:8, :] = b[span : span + 8, :]

    for b, p in ((bq, pq), (bk, pk), (bv, pv)):
        b[8 : span + 8, :] = p[0].astype(F32)
    row, col = iotas(CHUNK)
    hs = range(heads)
    both_at = [(j, h) for j in range(STEP) for h in hs]
    ks = [slice(h * DK, (h + 1) * DK) for h in hs]
    vs = [slice(h * DV, (h + 1) * DV) for h in hs]
    lines = [slice(j * CHUNK, (j + 1) * CHUNK) for j in range(STEP)]
    cum, cum_t, betas = [], [], []
    for j in range(STEP):
        small = ps[0, lines[j], :]
        g = rates[...] * softplus(small + bias[...])
        betas.append(sigmoid(small))
        cum.append(exact((row >= col).astype(F32), g))
        cum_t.append(cum[j].T)
    q, k, v, within, kbeta, gamma, rem, last = {}, {}, {}, {}, {}, {}, {}, {}
    for x in both_at:
        j, h = x
        a = conv_of(bq, cq, ks[h], j * CHUNK)
        q[x] = unit(a * sigmoid(a))[0]
        a = conv_of(bk, ck, ks[h], j * CHUNK)
        k[x] = unit(a * sigmoid(a))[0]
        a = conv_of(bv, cv, vs[h], j * CHUNK)
        v[x] = a * sigmoid(a)
        gc = cum[j][:, h : h + 1]
        within[x] = jnp.exp(jnp.where(row >= col, gc - cum_t[j][h : h + 1, :], -1e30))
        kbeta[x] = betas[j][:, heads + h : heads + h + 1]
        gamma[x] = jnp.exp(gc)
        tail = cum[j][CHUNK - 1 : CHUNK, h : h + 1]
        rem[x] = jnp.exp(tail - gc)
        last[x] = jnp.exp(tail)
    kb = {x: k[x].astype(BF) for x in both_at}
    lowers = [
        jnp.where(row > col, kbeta[x] * (mm(kb[x], kb[x], NT) * within[x]), 0.0) for x in both_at
    ]
    scores = {x: mm(q[x], kb[x], NT) * within[x] for x in both_at}
    inv = dict(zip(both_at, lower_inverses(lowers)))
    states = [state[h] for h in hs]
    for j in range(STEP):
        sb = [s.astype(BF) for s in states]
        both = [
            mm(jnp.concatenate([gamma[j, h] * k[j, h], gamma[j, h] * q[j, h]], axis=0), sb[h])
            for h in hs
        ]
        fb = [
            mm(inv[j, h], kbeta[j, h] * (v[j, h] - both[h][:CHUNK])).astype(BF) for h in hs
        ]
        out = [(both[h][CHUNK:] + mm(scores[j, h], fb[h])) * DK**-0.5 for h in hs]
        states = [
            last[j, h] * states[h] + mm(rem[j, h] * k[j, h], fb[h], TN) for h in hs
        ]
        for h in hs:
            t_out[0, j, h] = inv[j, h].astype(t_out.dtype)
            s_out[0, j, h] = sb[h]
            f_out[0, lines[j], vs[h]] = fb[h]
            o = out[h]
            r = lax.rsqrt(jnp.mean(o * o, axis=-1, keepdims=True) + NORM_EPS)
            p = pg[0, lines[j], vs[h]].astype(F32)
            mixed[0, lines[j], vs[h]] = (o * r * gain[...] * (p * sigmoid(p))).astype(BF)
    for h in hs:
        state[h] = states[h]


def mixer_backward_kernel(
    heads, dm, pq, pk, pv, pg, ps, tq, tk, tv, cq, ck, cv, rates, bias, gain, t_in, s_in, f_in,
    gqks, gvg, dcq, dck, dcv, dsm, dgain,
    bq, bk, bv, eq, ek, ev, dstate,
):
    row_at = pl.program_id(0)
    step = pl.program_id(1)
    chunk = pl.num_programs(1) - 1 - step
    span = BACK_STEP * CHUNK

    @pl.when((row_at == 0) & (step == 0))
    def _():
        for r in (dcq, dck, dcv, dsm, dgain):
            r[...] = jnp.zeros_like(r)

    @pl.when(step == 0)
    def _():
        dstate[...] = jnp.zeros_like(dstate)
        for b in (eq, ek, ev):
            b[span : span + 8, :] = jnp.zeros((8, b.shape[1]), F32)

    @pl.when(step > 0)
    def _():
        for b in (eq, ek, ev):
            b[span : span + 8, :] = b[0:8, :]

    has_before = (chunk > 0).astype(F32)
    for b, p, t in ((bq, pq, tq), (bk, pk, tk), (bv, pv, tv)):
        b[0:8, :] = t[0].astype(F32) * has_before
        b[8 : span + 8, :] = p[0].astype(F32)
    row, col = iotas(CHUNK)
    lane = col
    hs = range(heads)
    at = [(j, h) for j in range(BACK_STEP) for h in hs]
    ks = [slice(h * DK, (h + 1) * DK) for h in hs]
    vs = [slice(h * DV, (h + 1) * DV) for h in hs]
    lines = [slice(j * CHUNK, (j + 1) * CHUNK) for j in range(BACK_STEP)]
    scale = DK**-0.5
    small, shifted, g, betas, cum, cum_t = [], [], [], [], [], []
    for j in range(BACK_STEP):
        small.append(ps[0, lines[j], :])
        shifted.append(small[j] + bias[...])
        g.append(rates[...] * softplus(shifted[j]))
        betas.append(sigmoid(small[j]))
        cum.append(exact((row >= col).astype(F32), g[j]))
        cum_t.append(cum[j].T)
    q, k, v, rq, rk, kbeta, gamma, rem, last, within = {}, {}, {}, {}, {}, {}, {}, {}, {}, {}
    sq, sk, sv = {}, {}, {}
    for x in at:
        j, h = x
        a, sq[x] = silu_slope(conv_of(bq, cq, ks[h], j * CHUNK))
        q[x], rq[x] = unit(a)
        a, sk[x] = silu_slope(conv_of(bk, ck, ks[h], j * CHUNK))
        k[x], rk[x] = unit(a)
        v[x], sv[x] = silu_slope(conv_of(bv, cv, vs[h], j * CHUNK))
        gc = cum[j][:, h : h + 1]
        within[x] = jnp.exp(jnp.where(row >= col, gc - cum_t[j][h : h + 1, :], -1e30))
        kbeta[x] = betas[j][:, heads + h : heads + h + 1]
        gamma[x] = jnp.exp(gc)
        tail = cum[j][CHUNK - 1 : CHUNK, h : h + 1]
        rem[x] = jnp.exp(tail - gc)
        last[x] = jnp.exp(tail)
    qb = {x: q[x].astype(BF) for x in at}
    kb = {x: k[x].astype(BF) for x in at}
    sb = {x: s_in[0, x[0], x[1]] for x in at}
    fb = {x: f_in[0, lines[x[0]], vs[x[1]]] for x in at}
    tb = {x: t_in[0, x[0], x[1]] for x in at}
    gram = {x: mm(kb[x], kb[x], NT) * within[x] for x in at}
    scores = {x: mm(qb[x], kb[x], NT) * within[x] for x in at}
    gk_gq = {x: jnp.concatenate([gamma[x] * k[x], gamma[x] * q[x]], axis=0) for x in at}
    both = {x: mm(gk_gq[x], sb[x]) for x in at}
    x_in = {x: v[x] - both[x][:CHUNK] for x in at}
    out = {x: (both[x][CHUNK:] + mm(scores[x], fb[x])) * scale for x in at}
    head_dgain = jnp.zeros((1, DV), F32)
    dout = {}
    for x in at:
        j, h = x
        o = out[x]
        r = lax.rsqrt(jnp.mean(o * o, axis=-1, keepdims=True) + NORM_EPS)
        n = o * r
        p = pg[0, lines[j], vs[h]].astype(F32)
        s = sigmoid(p)
        d = dm[0, lines[j], vs[h]].astype(F32)
        y = n * gain[...]
        start = heads * DV + h * DV
        gvg[0, lines[j], start : start + DV] = (d * y * (s * (1.0 + p * (1.0 - s)))).astype(BF)
        dy = d * (p * s)
        head_dgain = head_dgain + jnp.sum(dy * n, axis=0, keepdims=True)
        dn = dy * gain[...]
        dout[x] = scale * r * (dn - n * jnp.mean(n * dn, axis=-1, keepdims=True))
    dgain[0:1, :] += head_dgain
    dob = {x: dout[x].astype(BF) for x in at}
    krem = {x: rem[x] * k[x] for x in at}
    dfresh_own = {x: mm(scores[x], dob[x], TN) for x in at}
    dscore = {x: mm(dob[x], fb[x], NT) for x in at}
    ds_next, dsb, dr, dx, dx_do = {}, {}, {}, {}, {}
    ds = [dstate[h] for h in hs]
    for j in reversed(range(BACK_STEP)):
        for h in hs:
            ds_next[j, h] = ds[h]
            dsb[j, h] = ds[h].astype(BF)
        dfresh = [dfresh_own[j, h] + mm(krem[j, h], dsb[j, h]) for h in hs]
        for h in hs:
            dr[j, h] = mm(tb[j, h], dfresh[h], TN)
        for h in hs:
            dx[j, h] = kbeta[j, h] * dr[j, h]
            dx_do[j, h] = jnp.concatenate([-dx[j, h], dout[j, h]], axis=0).astype(BF)
        ds = [last[j, h] * ds[h] + mm(gk_gq[j, h], dx_do[j, h], TN) for h in hs]
    for h in hs:
        dstate[h] = ds[h]
    dgk_gq = {x: mm(dx_do[x], sb[x], NT) for x in at}
    dkrem = {x: mm(fb[x], dsb[x], NT) for x in at}
    dlow = {x: jnp.where(row > col, -mm(dr[x], fb[x], NT), 0.0) for x in at}
    dcum = [jnp.zeros((CHUNK, CHUNK), F32) for _ in range(BACK_STEP)]
    dcum_rows = [jnp.zeros((CHUNK, CHUNK), F32) for _ in range(BACK_STEP)]
    dbeta = [jnp.zeros((CHUNK, CHUNK), F32) for _ in range(BACK_STEP)]
    for x in at:
        j, h = x
        m = dscore[x] * within[x]
        dgram = kbeta[x] * (dlow[x] * within[x])
        lg = dlow[x] * gram[x]
        e = dscore[x] * scores[x] + kbeta[x] * lg
        dq = gamma[x] * dgk_gq[x][CHUNK:] + mm(m, kb[x])
        mk = jnp.concatenate([m, dgram], axis=0)
        dk = (
            gamma[x] * dgk_gq[x][:CHUNK]
            + rem[x] * dkrem[x]
            + mm(mk, jnp.concatenate([qb[x], kb[x]], axis=0), TN)
            + mm(dgram, kb[x])
        )
        rem_part = jnp.sum(dkrem[x] * krem[x], axis=-1, keepdims=True)
        head_dcum = (
            jnp.sum(e, axis=-1, keepdims=True)
            + jnp.sum(
                dgk_gq[x][:CHUNK] * gk_gq[x][:CHUNK] + dgk_gq[x][CHUNK:] * gk_gq[x][CHUNK:],
                axis=-1, keepdims=True,
            )
            - rem_part
        )
        state_part = jnp.sum(
            jnp.sum(ds_next[x] * sb[x].astype(F32), axis=0, keepdims=True), axis=1, keepdims=True
        )
        end_part = jnp.sum(rem_part, axis=0, keepdims=True) + last[x] * state_part
        head_dcum = head_dcum + jnp.where(row[:, 0:1] == CHUNK - 1, end_part, 0.0)
        dcum[j] = dcum[j] + jnp.where(lane == h, head_dcum, 0.0)
        dcum_rows[j] = dcum_rows[j] + jnp.where(
            row == h, jnp.sum(e, axis=0, keepdims=True), 0.0
        )
        head_dbeta = jnp.sum(dr[x] * x_in[x], axis=-1, keepdims=True) + jnp.sum(
            lg, axis=-1, keepdims=True
        )
        dbeta[j] = dbeta[j] + jnp.where(lane == heads + h, head_dbeta, 0.0)
        da = rq[x] * (dq - q[x] * jnp.sum(q[x] * dq, axis=-1, keepdims=True))
        eq[lines[j], ks[h]] = da * sq[x]
        da = rk[x] * (dk - k[x] * jnp.sum(k[x] * dk, axis=-1, keepdims=True))
        ek[lines[j], ks[h]] = da * sk[x]
        ev[lines[j], vs[h]] = dx[x] * sv[x]
    for j in range(BACK_STEP):
        dg = exact((row >= col).astype(F32), dcum[j] - dcum_rows[j].T, TN)
        dshift = dg * rates[...] * sigmoid(shifted[j])
        dsm[0:1, :] += jnp.sum(dg * g[j], axis=0, keepdims=True)
        dsm[1:2, :] += jnp.sum(dshift, axis=0, keepdims=True)
        gqks[0, lines[j], 2 * heads * DK :] = (
            jnp.where(lane < heads, dshift, 0.0) + dbeta[j] * betas[j] * (1.0 - betas[j])
        ).astype(BF)
    for b, e, taps, dtaps, out_ref, start in (
        (bq, eq, cq, dcq, gqks, 0), (bk, ek, ck, dck, gqks, heads * DK), (bv, ev, cv, dcv, gvg, 0),
    ):
        for first in range(0, b.shape[1], DK):
            sl = slice(first, first + DK)
            own = e[0:span, sl]
            total = taps[3:4, sl] * own
            for i in range(3):
                total = total + taps[i : i + 1, sl] * e[3 - i : 3 - i + span, sl]
            out_ref[0, :, start + first : start + first + DK] = total.astype(BF)
            for i in range(4):
                dtaps[i : i + 1, sl] += jnp.sum(
                    own * b[5 + i : 5 + i + span, sl], axis=0, keepdims=True
                )


def whole_spec(shape):
    return pl.BlockSpec(shape, lambda r, c: (0,) * len(shape))


def lane_pad(vec, at):
    return jnp.zeros((1, 128), F32).at[0, at : at + vec.shape[0]].set(vec)


def mixer_forward(pqks, pvg, cq, ck, cv, log_rates, rate_bias, gain):
    rows, length, value_width = pvg.shape
    value_width = value_width // 2
    key_width = value_width * DK // DV
    heads = key_width // DK
    chunks = length // CHUNK
    span = STEP * CHUNK
    seq = lambda width, at=0: pl.BlockSpec((1, span, width), lambda r, c: (r, c, at))
    per = lambda a, b: pl.BlockSpec((1, STEP, heads, a, b), lambda r, c: (r, c, 0, 0, 0))
    return pl.pallas_call(
        functools.partial(mixer_forward_kernel, heads),
        grid=(rows, chunks // STEP),
        in_specs=[seq(key_width), seq(key_width, 1), seq(value_width), seq(value_width, 1),
                  seq(128, 2 * heads),
                  whole_spec((4, key_width)), whole_spec((4, key_width)), whole_spec((4, value_width)),
                  whole_spec((1, 128)), whole_spec((1, 128)), whole_spec((1, DV))],
        out_specs=[seq(value_width), per(CHUNK, CHUNK), per(DK, DV), seq(value_width)],
        out_shape=[
            jax.ShapeDtypeStruct((rows, length, value_width), BF),
            jax.ShapeDtypeStruct((rows, chunks, heads, CHUNK, CHUNK), BF),
            jax.ShapeDtypeStruct((rows, chunks, heads, DK, DV), BF),
            jax.ShapeDtypeStruct((rows, length, value_width), BF),
        ],
        scratch_shapes=[
            pltpu.VMEM((span + 8, key_width), F32),
            pltpu.VMEM((span + 8, key_width), F32),
            pltpu.VMEM((span + 8, value_width), F32),
            pltpu.VMEM((heads, DK, DV), F32),
        ],
        compiler_params=pltpu.CompilerParams(
            dimension_semantics=("arbitrary", "arbitrary"), vmem_limit_bytes=40 << 20
        ),
        cost_estimate=pl.CostEstimate(flops=0, bytes_accessed=int(rows * chunks * heads * 3007812.5), transcendentals=0),
        name="mixer_forward",
    )(pqks, pqks, pvg, pvg, pqks, cq, ck, cv, lane_pad(-jnp.exp(log_rates), 0),
      lane_pad(rate_bias, 0), gain.reshape(1, DV))


def mixer_backward(dm, pqks, pvg, cq, ck, cv, log_rates, rate_bias, gain, t_in, s_in, f_in):
    rows, length, value_width = dm.shape
    key_width = value_width * DK // DV
    heads = key_width // DK
    chunks = length // CHUNK
    span = BACK_STEP * CHUNK
    steps = chunks // BACK_STEP
    seq = lambda width, at=0: pl.BlockSpec(
        (1, span, width), lambda r, c: (r, steps - 1 - c, at)
    )
    before = lambda width, at=0: pl.BlockSpec(
        (1, 8, width),
        lambda r, c: (r, jnp.maximum((steps - 1 - c) * (span // 8) - 1, 0), at),
    )
    per = lambda a, b: pl.BlockSpec(
        (1, BACK_STEP, heads, a, b), lambda r, c: (r, steps - 1 - c, 0, 0, 0)
    )
    seq_shape = lambda width: jax.ShapeDtypeStruct((rows, length, width), BF)
    return pl.pallas_call(
        functools.partial(mixer_backward_kernel, heads),
        grid=(rows, steps),
        in_specs=[seq(value_width), seq(key_width), seq(key_width, 1), seq(value_width),
                  seq(value_width, 1), seq(128, 2 * heads),
                  before(key_width), before(key_width, 1), before(value_width),
                  whole_spec((4, key_width)), whole_spec((4, key_width)), whole_spec((4, value_width)),
                  whole_spec((1, 128)), whole_spec((1, 128)), whole_spec((1, DV)),
                  per(CHUNK, CHUNK), per(DK, DV), seq(value_width)],
        out_specs=[seq(2 * key_width + 128), seq(2 * value_width),
                   whole_spec((8, key_width)), whole_spec((8, key_width)), whole_spec((8, value_width)),
                   whole_spec((8, 128)), whole_spec((8, DV))],
        out_shape=[seq_shape(2 * key_width + 128), seq_shape(2 * value_width),
                   jax.ShapeDtypeStruct((8, key_width), F32),
                   jax.ShapeDtypeStruct((8, key_width), F32),
                   jax.ShapeDtypeStruct((8, value_width), F32),
                   jax.ShapeDtypeStruct((8, 128), F32),
                   jax.ShapeDtypeStruct((8, DV), F32)],
        scratch_shapes=[
            pltpu.VMEM((span + 8, key_width), F32),
            pltpu.VMEM((span + 8, key_width), F32),
            pltpu.VMEM((span + 8, value_width), F32),
            pltpu.VMEM((span + 8, key_width), F32),
            pltpu.VMEM((span + 8, key_width), F32),
            pltpu.VMEM((span + 8, value_width), F32),
            pltpu.VMEM((heads, DK, DV), F32),
        ],
        compiler_params=pltpu.CompilerParams(
            dimension_semantics=("arbitrary", "arbitrary"), vmem_limit_bytes=48 << 20
        ),
        cost_estimate=pl.CostEstimate(flops=0, bytes_accessed=int(rows * chunks * heads * 4921875.0), transcendentals=0),
        name="mixer_backward",
    )(dm, pqks, pqks, pvg, pvg, pqks, pqks, pqks, pvg, cq, ck, cv, lane_pad(-jnp.exp(log_rates), 0),
      lane_pad(rate_bias, 0), gain.reshape(1, DV), t_in, s_in, f_in)


FREE = pl.CostEstimate(flops=0, bytes_accessed=0, transcendentals=0)
VMEM_LIMIT = 44 << 20
WIDE_LIMIT = 58 << 20
SMALL_LIMIT = 16 << 20


def rows_kernel(count, nt, has_weigh, at, *refs):
    out = refs[-2] if has_weigh else refs[-1]
    total = None
    for i in range(count):
        part = lax.dot_general(
            refs[2 * i][0], refs[2 * i + 1][...], NT if nt else NN, preferred_element_type=F32
        )
        total = part if total is None else total + part
    if has_weigh:
        refs[-1][0, 0:1, :] = jnp.sum(
            total * refs[2 * count][0].astype(F32), axis=0, keepdims=True
        )
    out[0] = total.astype(out.dtype)


def rows_matmul(
    pairs, piece, nt=False, tile=512, take=0, weigh=None, into=None, put=0, dtype=BF, limit=WIDE_LIMIT
):
    rows = pairs[0][0].shape[0]
    width = pairs[0][1].shape[0 if nt else 1]
    tile = min(tile, width)
    at = jnp.stack([jnp.int32(take), jnp.int32(put)])
    specs, args = [], []
    for a, w in pairs:
        depth = a.shape[2]
        specs.append(pl.BlockSpec((1, piece, depth), lambda r, n, at: (r, at[0], 0)))
        if nt:
            specs.append(pl.BlockSpec((tile, depth), lambda r, n, at: (n, 0)))
        else:
            specs.append(pl.BlockSpec((depth, tile), lambda r, n, at: (0, n)))
        args.extend((a, w))
    if weigh is not None:
        specs.append(pl.BlockSpec((1, piece, tile), lambda r, n, at: (r, 0, n)))
        args.append(weigh)
    aliases = {}
    shape = (rows, piece, width)
    if into is not None:
        shape = into.shape
        dtype = into.dtype
        if not isinstance(into, jax.ShapeDtypeStruct):
            specs.append(pl.BlockSpec(memory_space=pl.ANY))
            args.append(into)
            aliases = {len(args): 0}
    out_specs = [pl.BlockSpec((1, piece, tile), lambda r, n, at: (r, at[1], n))]
    out_shape = [jax.ShapeDtypeStruct(shape, dtype)]
    if weigh is not None:
        out_specs.append(pl.BlockSpec((1, 8, tile), lambda r, n, at: (r, 0, n)))
        out_shape.append(jax.ShapeDtypeStruct((rows, 8, width), F32))
    out = pl.pallas_call(
        functools.partial(rows_kernel, len(pairs), nt, weigh is not None),
        grid_spec=pltpu.PrefetchScalarGridSpec(
            num_scalar_prefetch=1,
            grid=(rows, pl.cdiv(width, tile)),
            in_specs=specs,
            out_specs=out_specs,
        ),
        out_shape=out_shape,
        input_output_aliases=aliases,
        compiler_params=pltpu.CompilerParams(
            dimension_semantics=("arbitrary", "arbitrary"), vmem_limit_bytes=limit
        ),
        cost_estimate=FREE,
        name="rows_matmul",
    )(at, *args)
    return out[0] if weigh is None else (out[0], jnp.sum(out[1][:, 0:1], axis=0))


def outer_kernel(count, blocks, groups, parts, at, *refs):
    xs, gs = refs[:count], refs[count : 2 * count]
    extras = list(refs[2 * count : -1 - parts])
    outs, flipped = refs[-1 - parts : -1], refs[-1]
    rows, piece, width = xs[0].shape
    depth = rows * piece
    block = flipped.shape[0] // blocks

    @pl.when(pl.program_id(0) == 0)
    def _():
        for i, x in enumerate(xs):
            for k in range(blocks):
                start = pl.multiple_of((2 * k + at[0]) * block, block)
                part = x[:, :, pl.ds(start, block)].reshape(depth, block)
                flipped[k * block : (k + 1) * block, i * depth : (i + 1) * depth] = part.T

    total = None
    for i, g in enumerate(gs):
        part = lax.dot_general(
            flipped[:, i * depth : (i + 1) * depth],
            g[...].reshape(depth, g.shape[2]),
            NN,
            preferred_element_type=F32,
        )
        total = part if total is None else total + part
    for size in groups:
        held, extras = extras[:size], extras[size:]
        total = total + jnp.concatenate([x[...].astype(F32) for x in held], axis=0)
    lines = total.shape[0] // parts
    for i, out in enumerate(outs):
        out[...] = total[i * lines : (i + 1) * lines].astype(out.dtype)


def outer_sum(xs, gs, places, core, data, tile=512, adds=(), dtype=BF, parts=1):
    rows, piece, width = xs[0].shape
    columns = gs[0].shape[2]
    tile = min(tile, columns)
    at = jnp.stack([jnp.int32(core)] + [jnp.int32(x) for x in places])
    whole = pl.BlockSpec(
        (rows, piece, width), lambda n, at: (0, 0, 0), pipeline_mode=pl.Buffered(1)
    )
    specs = [whole] * len(xs)
    for i in range(len(gs)):
        specs.append(
            pl.BlockSpec((rows, piece, tile), lambda n, at, i=i: (0, at[1 + i], n))
        )
    args = [*xs, *gs]
    lines = lambda count: pl.BlockSpec((width // 2 // count, tile), lambda n, at: (0, n))
    for group in adds:
        specs.extend([lines(len(group))] * len(group))
        args.extend(group)
    return pl.pallas_call(
        functools.partial(outer_kernel, len(xs), data // 2, [len(x) for x in adds], parts),
        grid_spec=pltpu.PrefetchScalarGridSpec(
            num_scalar_prefetch=1,
            grid=(columns // tile,),
            in_specs=specs,
            out_specs=[lines(parts)] * parts,
            scratch_shapes=[pltpu.VMEM((width // 2, len(xs) * rows * piece), BF)],
        ),
        out_shape=[jax.ShapeDtypeStruct((width // 2 // parts, columns), dtype)] * parts,
        compiler_params=pltpu.CompilerParams(
            dimension_semantics=("arbitrary",), vmem_limit_bytes=VMEM_LIMIT
        ),
        cost_estimate=FREE,
        name="outer_sum",
    )(at, *args)


UNITS = 256


def lanes_of(units):
    return 128 if units % 128 == 0 else 64


def mlp_kernel(lanes, x, wgu, g, wd, hidden, grads):
    mlp_finish(lanes, lax.dot_general(x[...], wgu[...], NN, preferred_element_type=F32), g, wd, hidden, grads)


def mlp_finish(lanes, both, g, wd, hidden, grads):
    back = lax.dot_general(g[...], wd[...], NN, preferred_element_type=F32)
    for at in range(0, UNITS, lanes):
        first, second = 2 * at, 2 * at + lanes
        gate = both[:, first : first + lanes]
        up = both[:, second : second + lanes]
        own = back[:, at : at + lanes]
        sig = sigmoid(gate)
        act = gate * sig
        hidden[:, at : at + lanes] = (act * up).astype(BF)
        own_gate = own * up * (sig * (1.0 + gate * (1.0 - sig)))
        grads[:, first : first + lanes] = own_gate.astype(BF)
        grads[:, second : second + lanes] = (own * act).astype(BF)


def mlp_block(g, wd, x=None, wgu=None, both=None):
    piece, width = g.shape
    units = wd.shape[1]
    whole = pl.BlockSpec((piece, width), lambda n: (0, 0))
    part = lambda depth, size: pl.BlockSpec((depth, size), lambda n: (0, n))
    if both is None:
        kernel, args = mlp_kernel, (x, wgu, g, wd)
        specs = [whole, part(width, 2 * UNITS), whole, part(width, UNITS)]
    else:
        kernel, args = mlp_finish, (both, g, wd)
        specs = [part(piece, 2 * UNITS), whole, part(width, UNITS)]
    return pl.pallas_call(
        functools.partial(kernel, lanes_of(units)),
        grid=(pl.cdiv(units, UNITS),),
        in_specs=specs,
        out_specs=[part(piece, UNITS), part(piece, 2 * UNITS)],
        out_shape=[
            jax.ShapeDtypeStruct((piece, units), BF),
            jax.ShapeDtypeStruct((piece, 2 * units), BF),
        ],
        compiler_params=pltpu.CompilerParams(
            dimension_semantics=("arbitrary",), vmem_limit_bytes=WIDE_LIMIT
        ),
        cost_estimate=FREE,
        name="mlp_block",
    )(*args)


NORM_ROWS = 128


def row_stats(x):
    r = lax.rsqrt(jnp.mean(x * x, axis=-1, keepdims=True) + NORM_EPS)
    return x * r, r


def norm_grad(n, r, inner):
    return r * (inner - n * jnp.mean(n * inner, axis=-1, keepdims=True))


def valid_rows(at):
    start = at[0] + pl.program_id(1) * NORM_ROWS
    positions = start + lax.broadcasted_iota(jnp.int32, (NORM_ROWS, 1), 0)
    return (positions < at[1 + pl.program_id(0)]).astype(F32)


def enter_kernel(at, tokens, gain, normed):
    normed[0] = (row_stats(tokens[0].astype(F32))[0] * gain[...]).astype(BF)


def middle_kernel(at, own, moved, tokens, gain, middle, normed):
    total = own[0] + moved[0].astype(F32)
    x = tokens[0].astype(F32) + valid_rows(at) * total
    middle[0] = x
    normed[0] = (row_stats(x)[0] * gain[...]).astype(BF)


def middle_back_kernel(at, own, moved, middle, cot, gain, grad_middle, grad_attn, dgain):
    @pl.when((pl.program_id(0) == 0) & (pl.program_id(1) == 0))
    def _():
        dgain[...] = jnp.zeros_like(dgain)

    grad = own[0] + moved[0].astype(F32)
    n, r = row_stats(middle[0])
    dgain[0:1, :] += jnp.sum(grad * n, axis=0, keepdims=True)
    total = cot[0].astype(F32) + norm_grad(n, r, gain[...] * grad)
    grad_middle[0] = total
    grad_attn[0] = (valid_rows(at) * total).astype(BF)


def leave_kernel(at, own, moved, tokens, grad_middle, gain, out):
    grad = own[0] + moved[0].astype(F32)
    n, r = row_stats(tokens[0].astype(F32))
    out[0] = (grad_middle[0] + norm_grad(n, r, gain[...] * grad)).astype(BF)


def result_kernel(at, own, moved, middle, out):
    total = own[0] + moved[0].astype(F32)
    out[0] = (middle[0] + valid_rows(at) * total).astype(BF)


def by_rows(kernel, at, arrays, gain, out_types, with_sum=False):
    rows, piece, width = arrays[0].shape
    block = pl.BlockSpec((1, NORM_ROWS, width), lambda r, t, at: (r, t, 0))
    out_shape = [jax.ShapeDtypeStruct((rows, piece, width), x) for x in out_types]
    out_specs = [block] * len(out_types)
    specs = [block] * len(arrays)
    args = list(arrays)
    if gain is not None:
        specs.append(pl.BlockSpec((1, width), lambda r, t, at: (0, 0)))
        args.append(gain.reshape(1, width))
    if with_sum:
        out_shape.append(jax.ShapeDtypeStruct((8, width), F32))
        out_specs.append(pl.BlockSpec((8, width), lambda r, t, at: (0, 0)))
    return pl.pallas_call(
        kernel,
        grid_spec=pltpu.PrefetchScalarGridSpec(
            num_scalar_prefetch=1,
            grid=(rows, piece // NORM_ROWS),
            in_specs=specs,
            out_specs=out_specs,
        ),
        out_shape=out_shape,
        compiler_params=pltpu.CompilerParams(
            dimension_semantics=("arbitrary", "arbitrary"), vmem_limit_bytes=SMALL_LIMIT
        ),
        cost_estimate=FREE,
        name=kernel.__name__,
    )(at, *args)


def ring(size, group):
    return [(i, i // group * group + (i + 1) % group) for i in range(size)]


def across(size):
    return [(i, (i + size // 2) % size) for i in range(size)]


def swap(size, bit):
    return [(i, i ^ bit) for i in range(size)]


def tie(*values):
    return lax.optimization_barrier(values)


def matmul(a, b):
    return lax.dot_general(a, b, NN, preferred_element_type=F32)


def sum_over(x, axis, size):
    bit = 1
    while bit < size:
        x = x + lax.ppermute(x, axis, swap(size, bit))
        bit = bit * 2
    return x


def alternate(gate, up):
    units = gate.shape[1]
    lanes = lanes_of(units)
    parts = [x[:, at : at + lanes] for at in range(0, units, lanes) for x in (gate, up)]
    return jnp.concatenate(parts, axis=1)


def apart(both):
    units = both.shape[1] // 2
    lanes = lanes_of(units)
    parts = [both[:, at : at + lanes] for at in range(0, 2 * units, lanes)]
    return jnp.concatenate(parts[0::2], axis=1), jnp.concatenate(parts[1::2], axis=1)


def per_device(
    tokens,
    lengths,
    gain_attn,
    w_query,
    w_key,
    w_value,
    w_decay,
    w_beta,
    w_gate_out,
    conv_query,
    conv_key,
    conv_value,
    decay_log,
    decay_bias,
    gain_head,
    w_out,
    gain_mlp,
    w_gate,
    w_up,
    w_down,
    cotangent,
):
    rows, piece, width = tokens.shape
    size = lax.axis_size("head")
    data = lax.axis_size("dp")
    me = lax.axis_index("head")
    core = lax.rem(lax.axis_index("dp"), 2)
    length = piece * size
    heads = w_decay.shape[1]
    key_width, value_width = heads * DK, heads * DV
    shape3 = (rows, piece, width)
    flat_piece = rows * piece
    group = size // 2
    at = jnp.concatenate([(me * piece).astype(jnp.int32)[None], lengths])
    positions = me * piece + jnp.arange(piece, dtype=jnp.int32)
    mask = (positions[None, :] < lengths[:, None]).astype(F32)[:, :, None]

    def owner(s):
        return lax.rem(me + size - s, size)

    def step(x, group):
        return lax.ppermute(x, "head", ring(size, group))

    def opposite(x):
        return lax.ppermute(x, "head", across(size))

    def gather_weight(w):
        return lax.all_gather(w, "dp", axis=0, tiled=True)

    def cross(parts):
        return [lax.ppermute(x, "dp", swap(data, 1)) for x in parts]

    def outer_halves(xs, gs, places, tile=512, parts=2, away=(), near=()):
        away = outer_sum(xs, gs, places, 1 - core, data, tile, away, parts=parts)
        return outer_sum(xs, gs, places, core, data, tile, [cross(away), *near])[0]

    def scatter_weight(total):
        places = [[i + c for i in range(0, data, 2)] for c in range(2)]
        return lax.psum_scatter(
            total, "dp", scatter_dimension=0, tiled=True, axis_index_groups=places
        )

    normed = by_rows(enter_kernel, at, [tokens], gain_attn, [BF])[0]
    small_pad = jnp.zeros((w_decay.shape[0], 128 - 2 * heads), BF)
    w_qks = gather_weight(jnp.concatenate([w_query, w_key, w_decay, w_beta, small_pad], axis=1))
    w_vg = gather_weight(jnp.concatenate([w_value, w_gate_out], axis=1))
    wo_full = gather_weight(w_out)

    qks_buffer = jax.ShapeDtypeStruct((rows, length, 2 * key_width + 128), F32)
    vg_buffer = jax.ShapeDtypeStruct((rows, length, 2 * value_width), F32)
    def project_qks(item, s, into):
        return rows_matmul([(item, w_qks)], piece, tile=into.shape[2], into=into, put=owner(s))

    def project_vg(item, s, into):
        return rows_matmul([(item, w_vg)], piece, into=into, put=owner(s))

    pqks = project_qks(normed, 0, qks_buffer)
    pvg = vg_buffer
    pieces = [normed]
    for s in range(1, size):
        send = pieces[-1]
        if s == 1:
            send, w_gate, w_up, cotangent = tie(send, w_gate, w_up, cotangent)
        item = step(send, size)
        if s == 1:
            w_gu = alternate(w_gate, w_up)
            grad_mlp = (mask * cotangent.astype(F32)).astype(BF)
            item, w_gu, grad_mlp = tie(item, w_gu, grad_mlp)
        if s == size - 1:
            for place, early in enumerate(pieces):
                pvg = project_vg(early, place, pvg)
            item, pqks, pvg, w_gu, w_down, grad_mlp = tie(
                item, pqks, pvg, w_gu, w_down, grad_mlp
            )
        elif s > 1:
            item, pqks = tie(item, pqks)
        pqks = project_qks(item, s, pqks)
        pieces.append(item)
    normed_pieces = pieces
    w_gu_other = opposite(w_gu)
    w_down_other = opposite(w_down)
    grad_out = [grad_mlp]
    for _ in range(1, group):
        grad_out.append(step(grad_out[-1], group))
    pvg = project_vg(item, size - 1, pvg)

    cq = lax.dynamic_slice_in_dim(conv_query, me * key_width, key_width, 1)
    ck = lax.dynamic_slice_in_dim(conv_key, me * key_width, key_width, 1)
    cv = lax.dynamic_slice_in_dim(conv_value, me * value_width, value_width, 1)
    log_local = lax.dynamic_slice_in_dim(decay_log, me * heads, heads, 0)
    bias_local = lax.dynamic_slice_in_dim(decay_bias, me * heads, heads, 0)
    mixed, t_kept, s_kept, f_kept = mixer_forward(
        pqks, pvg, cq, ck, cv, log_local, bias_local, gain_head
    )
    mixed, w_gu_other, w_down_other, *grad_out = tie(mixed, w_gu_other, w_down_other, *grad_out)
    wgu_full = [gather_weight(w_gu), gather_weight(w_gu_other)]
    wdown_full = [gather_weight(w_down), gather_weight(w_down_other)]

    def attn_part(s, dtype=F32, limit=VMEM_LIMIT):
        return rows_matmul(
            [(mixed, wo_full)], piece, nt=True, take=owner(s), dtype=dtype, limit=limit
        )

    total = attn_part(1, BF, WIDE_LIMIT)
    for s in range(2, size + 1):
        moved = step(total, size)
        own = attn_part(s % size)
        moved, own = tie(moved, own)
        total = (own + moved.astype(F32)).astype(BF)
    middle, normed_two = by_rows(middle_kernel, at, [own, moved, tokens], gain_mlp, [F32, BF])
    flat2 = lambda x: x.reshape(flat_piece, width)
    second = [normed_two]
    hidden, grad_gu = [[], []], [[], []]

    def keep_block(b, block):
        hidden[b].append(block[0].reshape(rows, piece, -1))
        grad_gu[b].append(block[1].reshape(rows, piece, -1))

    def mlp_part(s, dtype=F32):
        pairs = [(hidden[b][s], wdown_full[b]) for b in range(2)]
        return rows_matmul(pairs, piece, nt=True, dtype=dtype)

    def two_part(s, dtype=F32):
        pairs = [(grad_gu[b][s], wgu_full[b]) for b in range(2)]
        return rows_matmul(pairs, piece, nt=True, dtype=dtype)

    send, own_x, own_g = tie(normed_two, normed_two, grad_out[0])
    for s in range(1, group):
        moved = step(send, group)
        if s == 1:
            for b in range(2):
                keep_block(b, mlp_block(flat2(own_g), wdown_full[b], flat2(own_x), wgu_full[b]))
            own_two = two_part(0)
            moved, own_two, *held = tie(moved, own_two, *hidden[0], *hidden[1], *grad_gu[0], *grad_gu[1])
            hidden, grad_gu = [held[:1], held[1:2]], [held[2:3], held[3:]]
        second.append(moved)
        send = moved
    for s in range(1, group):
        for b in range(2):
            keep_block(
                b, mlp_block(flat2(grad_out[s]), wdown_full[b], flat2(second[s]), wgu_full[b])
            )
    first = [0] * group
    units = hidden[0][0].shape[2]

    def away_pair(b):
        return (
            outer_sum(second, grad_gu[b], first, 1 - core, data, 1408),
            outer_sum(grad_out, hidden[b], first, 1 - core, data, units),
        )

    def near_pair(b, parts):
        return (
            outer_sum(second, grad_gu[b], first, core, data, 1408, [cross(parts[:1])])[0],
            outer_sum(grad_out, hidden[b], first, core, data, units, [cross(parts[1:])])[0],
        )

    total = two_part(1, BF)
    total, *held = tie(total, *hidden[0], *hidden[1], *grad_gu[1])
    hidden, grad_gu[1] = [held[:group], held[group : 2 * group]], held[2 * group :]
    for s in range(2, group + 1):
        moved = step(total, group)
        if s == group:
            own = own_two
            own_mlp, send_mlp = mlp_part(0), mlp_part(1, BF)
            away_gu, away_down = away_pair(1)
            moved, own_mlp, send_mlp, *away = tie(
                moved, own_mlp, send_mlp, *away_gu, *away_down
            )
        else:
            own = two_part(s)
            total = (own + moved.astype(F32)).astype(BF)
    grad_middle, grad_attn, dgain_mlp = by_rows(
        middle_back_kernel, at, [own, moved, middle, cotangent], gain_mlp, [F32, BF], True
    )

    pair_gu, pair_down = [None, None], [None, None]
    mixed_buffer = jax.ShapeDtypeStruct((rows, length, value_width), F32)
    grad_mixed = mixed_buffer
    attn_pieces = [grad_attn]
    for s in range(1, size):
        send = attn_pieces[-1]
        if s == 1:
            send, *held = tie(send, *away, *hidden[0], *grad_gu[0])
            away, hidden[0], grad_gu[0] = held[:2], held[2 : 2 + group], held[2 + group :]
        elif s == 2:
            send, *away = tie(send, *away)
        item = step(send, size)
        if s == 1:
            pair_gu[1], pair_down[1] = near_pair(1, away)
            away_gu, away_down = away_pair(0)
            item, pair_gu[1], pair_down[1], *away = tie(
                item, pair_gu[1], pair_down[1], *away_gu, *away_down
            )
        elif s == 2:
            pair_gu[0], pair_down[0] = near_pair(0, away)
            item, pair_gu[0], pair_down[0] = tie(item, pair_gu[0], pair_down[0])
        if s == size - 1:
            for place, early in enumerate(attn_pieces):
                grad_mixed = rows_matmul(
                    [(early, wo_full)], piece, into=grad_mixed, put=owner(place)
                )
            wout_parts = [
                outer_sum(
                    attn_pieces, [mixed] * s, [owner(x) for x in range(s)], side, data, dtype=F32
                )[0]
                for side in (1 - core, core)
            ]
            item, grad_mixed, *wout_parts = tie(item, grad_mixed, *wout_parts)
        attn_pieces.append(item)
    grad_mixed = rows_matmul([(item, wo_full)], piece, into=grad_mixed, put=owner(size - 1))
    sums_gu = [None, scatter_weight(pair_gu[1])]
    sums_down = [None, scatter_weight(pair_down[1])]
    sums_gu[0] = scatter_weight(pair_gu[0])
    sums_down[0] = scatter_weight(pair_down[0])

    grad_mixed, send_mlp, send_gu, send_down = tie(grad_mixed, send_mlp, sums_gu[1], sums_down[1])
    moved = step(send_mlp, group)
    moved_gu, moved_down = opposite(send_gu), opposite(send_down)
    done = mixer_backward(
        grad_mixed, pqks, pvg, cq, ck, cv, log_local, bias_local, gain_head, t_kept, s_kept, f_kept
    )
    moved, moved_gu, moved_down, gqks, gvg, dcq, dck, dcv, dsm, dgain = tie(
        moved, moved_gu, moved_down, *done
    )
    for s in range(2, group):
        moved = step((mlp_part(s) + moved.astype(F32)).astype(BF), group)
    moved_mlp = moved

    def one_part(s, dtype=F32):
        return rows_matmul(
            [(gqks, w_qks), (gvg, w_vg)], piece, nt=True, take=owner(s),
            weigh=normed_pieces[s], dtype=dtype,
        )

    places = [owner(s) for s in range(size)]
    total, gain_sum = one_part(1, BF)
    for s in range(2, size + 1):
        if s == 3:
            total, attn_last, *last = tie(total, attn_pieces[-1], sums_down[0], sums_gu[0])
            sums_down[0], sums_gu[0] = last
        total, gqks, gvg = tie(total, gqks, gvg)
        if s == size:
            total, moved_mlp, *small = tie(
                total, moved_mlp, dcq, dck, dcv, dsm, dgain, dgain_mlp
            )
        moved = step(total, size)
        if s < size:
            own, gain_part = one_part(s)
            gain_sum = gain_sum + gain_part
        if s == 2:
            pair_vg = outer_halves(normed_pieces, [gvg] * size, places, 512, 4)
            moved, own, pair_vg = tie(moved, own, pair_vg)
        elif s == 3:
            pair_qks = outer_halves(normed_pieces, [gqks] * size, places, gqks.shape[2])
            pair_wout = outer_halves(
                [attn_last], [mixed], places[-1:], 512, 2, [wout_parts[:1]], [wout_parts[1:]]
            )
            moved, own, pair_qks, pair_wout, out_vg = tie(
                moved, own, pair_qks, pair_wout, scatter_weight(pair_vg)
            )
        if s < size:
            total = (own + moved.astype(F32)).astype(BF)
            continue
        own, gain_part = one_part(0)
        small = jnp.concatenate(
            [x[:4] for x in small] + [jnp.broadcast_to(gain_sum + gain_part, (4, width))],
            axis=1,
        )
        small = sum_over(small, "dp", data)
        out_wgate, out_wup = apart(sums_gu[0].astype(F32) + moved_gu.astype(F32))
        out_wdown = sums_down[0].astype(F32) + moved_down.astype(F32)
        mixed_rows = by_rows(result_kernel, at, [own_mlp, moved_mlp, middle], None, [BF])[0]
        moved, own, small, out_wgate, out_wup, out_wdown, mixed_rows = tie(
            moved, own, small, out_wgate, out_wup, out_wdown, mixed_rows
        )
    tokens_grad = by_rows(
        leave_kernel, at, [own, moved, tokens, grad_middle], gain_attn, [BF]
    )[0]
    out_vg = out_vg.astype(F32)
    out_wout = scatter_weight(pair_wout).astype(F32)
    out_qks = scatter_weight(pair_qks).astype(F32)

    taps_width = 2 * key_width + value_width
    own_width = taps_width + 128
    spread = lax.dynamic_update_slice_in_dim(
        jnp.zeros((4, size * own_width), F32), small[:, :own_width], me * own_width, 1
    )
    small = sum_over(jnp.concatenate([spread, small[:, own_width:]], axis=1), "head", size)
    by_head = [small[:, i * own_width : (i + 1) * own_width] for i in range(size)]
    taps = lambda start, stop: jnp.concatenate([x[:, start:stop] for x in by_head], axis=1)
    conv_sums = (
        taps(0, key_width),
        taps(key_width, 2 * key_width),
        taps(2 * key_width, taps_width),
    )
    decay_sums = [
        jnp.concatenate([x[i, taps_width : taps_width + heads] for x in by_head]) for i in range(2)
    ]
    gains = small[0, size * own_width :]
    gain_head_out = gains[:DV]
    gain_mlp_out = gains[DV : DV + width]
    gain_attn_out = gains[DV + width :] / gain_attn
    return (
        mixed_rows,
        tokens_grad,
        gain_attn_out,
        out_qks[:, :key_width],
        out_qks[:, key_width : 2 * key_width],
        out_vg[:, :value_width],
        out_qks[:, 2 * key_width : 2 * key_width + heads],
        out_qks[:, 2 * key_width + heads : 2 * key_width + 2 * heads],
        out_vg[:, value_width:],
        conv_sums[0],
        conv_sums[1],
        conv_sums[2],
        decay_sums[0],
        decay_sums[1],
        gain_head_out,
        out_wout,
        gain_mlp_out,
        out_wgate,
        out_wup,
        out_wdown,
    )

def solution(mesh):
    rows = P("dp", "head", None)
    weight = P("dp", "head")
    same = P()
    return jax.shard_map(
        per_device,
        mesh=mesh,
        in_specs=(
            rows, P("dp"), same, weight, weight, weight, weight, weight, weight, same, same, same,
            same, same, same, weight, same, weight, weight, weight, rows,
        ),
        out_specs=(
            rows, rows, same, weight, weight, weight, weight, weight, weight, same, same, same,
            same, same, same, weight, same, weight, weight, weight,
        ),
        check_vma=False,
    )
```

```python
import functools

import jax
import jax.numpy as jnp
from jax import lax
from jax.experimental import pallas as pl
from jax.experimental.pallas import tpu as pltpu
from jax.sharding import PartitionSpec as P

DK = 128
DV = 256
CHUNK = 128
STEP = 4
BACK_STEP = 2
NORM_EPS = 1e-06
BF = jnp.bfloat16
F32 = jnp.float32
NN = (((1,), (0,)), ((), ()))
NT = (((1,), (1,)), ((), ()))
TN = (((0,), (0,)), ((), ()))


def mm(a, b, dims=NN):
    return lax.dot_general(a.astype(BF), b.astype(BF), dims, preferred_element_type=F32)


def split(a):
    high = a.astype(BF)
    return high, (a - high.astype(F32)).astype(BF)


def mm3(a, b, dims=NN):
    ah, al = split(a)
    bh, bl = split(b)
    return mm(ah, bh, dims) + mm(ah, bl, dims) + mm(al, bh, dims)


def exact(a, b, dims=NN):
    return lax.dot_general(a, b, dims, precision=lax.Precision.HIGHEST, preferred_element_type=F32)


def iotas(n):
    return (
        lax.broadcasted_iota(jnp.int32, (n, n), 0),
        lax.broadcasted_iota(jnp.int32, (n, n), 1),
    )


def lower_inverses(lowers):
    n = lowers[0].shape[0]
    row, col = iotas(n)
    eye = (row == col).astype(F32)
    pair = (row // 2 == col // 2).astype(F32)
    inverses = [eye - low * pair for low in lowers]
    size = 2
    while size < n:
        corner = ((row // (2 * size)) == (col // (2 * size))) & ((row // size) != (col // size))
        corner = corner.astype(F32)
        half = [x.astype(BF) for x in inverses]
        inner = [mm(x, low * corner) for x, low in zip(half, lowers)]
        inverses = [x - mm(i, h) for x, i, h in zip(inverses, inner, half)]
        size = size * 2
    residual = [eye - x - mm3(low, x) for low, x in zip(lowers, inverses)]
    return [x + mm(x, r) for x, r in zip(inverses, residual)]


def sigmoid(x):
    return 1.0 / (1.0 + jnp.exp(-x))


def conv_of(buf, taps, sl, start=0):
    total = taps[0:1, sl] * buf[start + 5 : start + 5 + CHUNK, sl]
    for i in range(1, 4):
        total = total + taps[i : i + 1, sl] * buf[start + 5 + i : start + 5 + i + CHUNK, sl]
    return total


def softplus(x):
    return jnp.maximum(x, 0.0) + jnp.log1p(jnp.exp(-jnp.abs(x)))


def silu_slope(a):
    s = sigmoid(a)
    value = a * s
    return value, s + value * (1.0 - s)


def unit(a):
    r = lax.rsqrt(jnp.sum(a * a, axis=-1, keepdims=True) + NORM_EPS)
    return a * r, r


def mixer_forward_kernel(
    heads, pq, pk, pv, pg, ps, cq, ck, cv, rates, bias, gain,
    mixed, t_out, s_out, f_out, bq, bk, bv, state,
):
    step = pl.program_id(1)
    span = STEP * CHUNK

    @pl.when(step == 0)
    def _():
        state[...] = jnp.zeros_like(state)
        for b in (bq, bk, bv):
            b[0:8, :] = jnp.zeros((8, b.shape[1]), F32)

    @pl.when(step > 0)
    def _():
        for b in (bq, bk, bv):
            b[0:8, :] = b[span : span + 8, :]

    for b, p in ((bq, pq), (bk, pk), (bv, pv)):
        b[8 : span + 8, :] = p[0].astype(F32)
    row, col = iotas(CHUNK)
    hs = range(heads)
    both_at = [(j, h) for j in range(STEP) for h in hs]
    ks = [slice(h * DK, (h + 1) * DK) for h in hs]
    vs = [slice(h * DV, (h + 1) * DV) for h in hs]
    lines = [slice(j * CHUNK, (j + 1) * CHUNK) for j in range(STEP)]
    cum, cum_t, betas = [], [], []
    for j in range(STEP):
        small = ps[0, lines[j], :]
        g = rates[...] * softplus(small + bias[...])
        betas.append(sigmoid(small))
        cum.append(exact((row >= col).astype(F32), g))
        cum_t.append(cum[j].T)
    q, k, v, within, kbeta, gamma, rem, last = {}, {}, {}, {}, {}, {}, {}, {}
    for x in both_at:
        j, h = x
        a = conv_of(bq, cq, ks[h], j * CHUNK)
        q[x] = unit(a * sigmoid(a))[0]
        a = conv_of(bk, ck, ks[h], j * CHUNK)
        k[x] = unit(a * sigmoid(a))[0]
        a = conv_of(bv, cv, vs[h], j * CHUNK)
        v[x] = a * sigmoid(a)
        gc = cum[j][:, h : h + 1]
        within[x] = jnp.exp(jnp.where(row >= col, gc - cum_t[j][h : h + 1, :], -1e30))
        kbeta[x] = betas[j][:, heads + h : heads + h + 1]
        gamma[x] = jnp.exp(gc)
        tail = cum[j][CHUNK - 1 : CHUNK, h : h + 1]
        rem[x] = jnp.exp(tail - gc)
        last[x] = jnp.exp(tail)
    kb = {x: k[x].astype(BF) for x in both_at}
    lowers = [
        jnp.where(row > col, kbeta[x] * (mm(kb[x], kb[x], NT) * within[x]), 0.0) for x in both_at
    ]
    scores = {x: mm(q[x], kb[x], NT) * within[x] for x in both_at}
    inv = dict(zip(both_at, lower_inverses(lowers)))
    states = [state[h] for h in hs]
    for j in range(STEP):
        sb = [s.astype(BF) for s in states]
        both = [
            mm(jnp.concatenate([gamma[j, h] * k[j, h], gamma[j, h] * q[j, h]], axis=0), sb[h])
            for h in hs
        ]
        fb = [
            mm(inv[j, h], kbeta[j, h] * (v[j, h] - both[h][:CHUNK])).astype(BF) for h in hs
        ]
        out = [(both[h][CHUNK:] + mm(scores[j, h], fb[h])) * DK**-0.5 for h in hs]
        states = [
            last[j, h] * states[h] + mm(rem[j, h] * k[j, h], fb[h], TN) for h in hs
        ]
        for h in hs:
            t_out[0, j, h] = inv[j, h].astype(t_out.dtype)
            s_out[0, j, h] = sb[h]
            f_out[0, lines[j], vs[h]] = fb[h]
            o = out[h]
            r = lax.rsqrt(jnp.mean(o * o, axis=-1, keepdims=True) + NORM_EPS)
            p = pg[0, lines[j], vs[h]].astype(F32)
            mixed[0, lines[j], vs[h]] = (o * r * gain[...] * (p * sigmoid(p))).astype(BF)
    for h in hs:
        state[h] = states[h]


def mixer_backward_kernel(
    heads, dm, pq, pk, pv, pg, ps, tq, tk, tv, cq, ck, cv, rates, bias, gain, t_in, s_in, f_in,
    gqks, gvg, dcq, dck, dcv, dsm, dgain,
    bq, bk, bv, eq, ek, ev, dstate,
):
    row_at = pl.program_id(0)
    step = pl.program_id(1)
    chunk = pl.num_programs(1) - 1 - step
    span = BACK_STEP * CHUNK

    @pl.when((row_at == 0) & (step == 0))
    def _():
        for r in (dcq, dck, dcv, dsm, dgain):
            r[...] = jnp.zeros_like(r)

    @pl.when(step == 0)
    def _():
        dstate[...] = jnp.zeros_like(dstate)
        for b in (eq, ek, ev):
            b[span : span + 8, :] = jnp.zeros((8, b.shape[1]), F32)

    @pl.when(step > 0)
    def _():
        for b in (eq, ek, ev):
            b[span : span + 8, :] = b[0:8, :]

    has_before = (chunk > 0).astype(F32)
    for b, p, t in ((bq, pq, tq), (bk, pk, tk), (bv, pv, tv)):
        b[0:8, :] = t[0].astype(F32) * has_before
        b[8 : span + 8, :] = p[0].astype(F32)
    row, col = iotas(CHUNK)
    lane = col
    hs = range(heads)
    at = [(j, h) for j in range(BACK_STEP) for h in hs]
    ks = [slice(h * DK, (h + 1) * DK) for h in hs]
    vs = [slice(h * DV, (h + 1) * DV) for h in hs]
    lines = [slice(j * CHUNK, (j + 1) * CHUNK) for j in range(BACK_STEP)]
    scale = DK**-0.5
    small, shifted, g, betas, cum, cum_t = [], [], [], [], [], []
    for j in range(BACK_STEP):
        small.append(ps[0, lines[j], :])
        shifted.append(small[j] + bias[...])
        g.append(rates[...] * softplus(shifted[j]))
        betas.append(sigmoid(small[j]))
        cum.append(exact((row >= col).astype(F32), g[j]))
        cum_t.append(cum[j].T)
    q, k, v, rq, rk, kbeta, gamma, rem, last, within = {}, {}, {}, {}, {}, {}, {}, {}, {}, {}
    sq, sk, sv = {}, {}, {}
    for x in at:
        j, h = x
        a, sq[x] = silu_slope(conv_of(bq, cq, ks[h], j * CHUNK))
        q[x], rq[x] = unit(a)
        a, sk[x] = silu_slope(conv_of(bk, ck, ks[h], j * CHUNK))
        k[x], rk[x] = unit(a)
        v[x], sv[x] = silu_slope(conv_of(bv, cv, vs[h], j * CHUNK))
        gc = cum[j][:, h : h + 1]
        within[x] = jnp.exp(jnp.where(row >= col, gc - cum_t[j][h : h + 1, :], -1e30))
        kbeta[x] = betas[j][:, heads + h : heads + h + 1]
        gamma[x] = jnp.exp(gc)
        tail = cum[j][CHUNK - 1 : CHUNK, h : h + 1]
        rem[x] = jnp.exp(tail - gc)
        last[x] = jnp.exp(tail)
    qb = {x: q[x].astype(BF) for x in at}
    kb = {x: k[x].astype(BF) for x in at}
    sb = {x: s_in[0, x[0], x[1]] for x in at}
    fb = {x: f_in[0, lines[x[0]], vs[x[1]]] for x in at}
    tb = {x: t_in[0, x[0], x[1]] for x in at}
    gram = {x: mm(kb[x], kb[x], NT) * within[x] for x in at}
    scores = {x: mm(qb[x], kb[x], NT) * within[x] for x in at}
    gk_gq = {x: jnp.concatenate([gamma[x] * k[x], gamma[x] * q[x]], axis=0) for x in at}
    both = {x: mm(gk_gq[x], sb[x]) for x in at}
    x_in = {x: v[x] - both[x][:CHUNK] for x in at}
    out = {x: (both[x][CHUNK:] + mm(scores[x], fb[x])) * scale for x in at}
    head_dgain = jnp.zeros((1, DV), F32)
    dout = {}
    for x in at:
        j, h = x
        o = out[x]
        r = lax.rsqrt(jnp.mean(o * o, axis=-1, keepdims=True) + NORM_EPS)
        n = o * r
        p = pg[0, lines[j], vs[h]].astype(F32)
        s = sigmoid(p)
        d = dm[0, lines[j], vs[h]].astype(F32)
        y = n * gain[...]
        start = heads * DV + h * DV
        gvg[0, lines[j], start : start + DV] = (d * y * (s * (1.0 + p * (1.0 - s)))).astype(BF)
        dy = d * (p * s)
        head_dgain = head_dgain + jnp.sum(dy * n, axis=0, keepdims=True)
        dn = dy * gain[...]
        dout[x] = scale * r * (dn - n * jnp.mean(n * dn, axis=-1, keepdims=True))
    dgain[0:1, :] += head_dgain
    dob = {x: dout[x].astype(BF) for x in at}
    krem = {x: rem[x] * k[x] for x in at}
    dfresh_own = {x: mm(scores[x], dob[x], TN) for x in at}
    dscore = {x: mm(dob[x], fb[x], NT) for x in at}
    ds_next, dsb, dr, dx, dx_do = {}, {}, {}, {}, {}
    ds = [dstate[h] for h in hs]
    for j in reversed(range(BACK_STEP)):
        for h in hs:
            ds_next[j, h] = ds[h]
            dsb[j, h] = ds[h].astype(BF)
        dfresh = [dfresh_own[j, h] + mm(krem[j, h], dsb[j, h]) for h in hs]
        for h in hs:
            dr[j, h] = mm(tb[j, h], dfresh[h], TN)
        for h in hs:
            dx[j, h] = kbeta[j, h] * dr[j, h]
            dx_do[j, h] = jnp.concatenate([-dx[j, h], dout[j, h]], axis=0).astype(BF)
        ds = [last[j, h] * ds[h] + mm(gk_gq[j, h], dx_do[j, h], TN) for h in hs]
    for h in hs:
        dstate[h] = ds[h]
    dgk_gq = {x: mm(dx_do[x], sb[x], NT) for x in at}
    dkrem = {x: mm(fb[x], dsb[x], NT) for x in at}
    dlow = {x: jnp.where(row > col, -mm(dr[x], fb[x], NT), 0.0) for x in at}
    dcum = [jnp.zeros((CHUNK, CHUNK), F32) for _ in range(BACK_STEP)]
    dcum_rows = [jnp.zeros((CHUNK, CHUNK), F32) for _ in range(BACK_STEP)]
    dbeta = [jnp.zeros((CHUNK, CHUNK), F32) for _ in range(BACK_STEP)]
    for x in at:
        j, h = x
        m = dscore[x] * within[x]
        dgram = kbeta[x] * (dlow[x] * within[x])
        lg = dlow[x] * gram[x]
        e = dscore[x] * scores[x] + kbeta[x] * lg
        dq = gamma[x] * dgk_gq[x][CHUNK:] + mm(m, kb[x])
        mk = jnp.concatenate([m, dgram], axis=0)
        dk = (
            gamma[x] * dgk_gq[x][:CHUNK]
            + rem[x] * dkrem[x]
            + mm(mk, jnp.concatenate([qb[x], kb[x]], axis=0), TN)
            + mm(dgram, kb[x])
        )
        rem_part = jnp.sum(dkrem[x] * krem[x], axis=-1, keepdims=True)
        head_dcum = (
            jnp.sum(e, axis=-1, keepdims=True)
            + jnp.sum(
                dgk_gq[x][:CHUNK] * gk_gq[x][:CHUNK] + dgk_gq[x][CHUNK:] * gk_gq[x][CHUNK:],
                axis=-1, keepdims=True,
            )
            - rem_part
        )
        state_part = jnp.sum(
            jnp.sum(ds_next[x] * sb[x].astype(F32), axis=0, keepdims=True), axis=1, keepdims=True
        )
        end_part = jnp.sum(rem_part, axis=0, keepdims=True) + last[x] * state_part
        head_dcum = head_dcum + jnp.where(row[:, 0:1] == CHUNK - 1, end_part, 0.0)
        dcum[j] = dcum[j] + jnp.where(lane == h, head_dcum, 0.0)
        dcum_rows[j] = dcum_rows[j] + jnp.where(
            row == h, jnp.sum(e, axis=0, keepdims=True), 0.0
        )
        head_dbeta = jnp.sum(dr[x] * x_in[x], axis=-1, keepdims=True) + jnp.sum(
            lg, axis=-1, keepdims=True
        )
        dbeta[j] = dbeta[j] + jnp.where(lane == heads + h, head_dbeta, 0.0)
        da = rq[x] * (dq - q[x] * jnp.sum(q[x] * dq, axis=-1, keepdims=True))
        eq[lines[j], ks[h]] = da * sq[x]
        da = rk[x] * (dk - k[x] * jnp.sum(k[x] * dk, axis=-1, keepdims=True))
        ek[lines[j], ks[h]] = da * sk[x]
        ev[lines[j], vs[h]] = dx[x] * sv[x]
    for j in range(BACK_STEP):
        dg = exact((row >= col).astype(F32), dcum[j] - dcum_rows[j].T, TN)
        dshift = dg * rates[...] * sigmoid(shifted[j])
        dsm[0:1, :] += jnp.sum(dg * g[j], axis=0, keepdims=True)
        dsm[1:2, :] += jnp.sum(dshift, axis=0, keepdims=True)
        gqks[0, lines[j], 2 * heads * DK :] = (
            jnp.where(lane < heads, dshift, 0.0) + dbeta[j] * betas[j] * (1.0 - betas[j])
        ).astype(BF)
    for b, e, taps, dtaps, out_ref, start in (
        (bq, eq, cq, dcq, gqks, 0), (bk, ek, ck, dck, gqks, heads * DK), (bv, ev, cv, dcv, gvg, 0),
    ):
        for first in range(0, b.shape[1], DK):
            sl = slice(first, first + DK)
            own = e[0:span, sl]
            total = taps[3:4, sl] * own
            for i in range(3):
                total = total + taps[i : i + 1, sl] * e[3 - i : 3 - i + span, sl]
            out_ref[0, :, start + first : start + first + DK] = total.astype(BF)
            for i in range(4):
                dtaps[i : i + 1, sl] += jnp.sum(
                    own * b[5 + i : 5 + i + span, sl], axis=0, keepdims=True
                )


def whole_spec(shape):
    return pl.BlockSpec(shape, lambda r, c: (0,) * len(shape))


def lane_pad(vec, at):
    return jnp.zeros((1, 128), F32).at[0, at : at + vec.shape[0]].set(vec)


def mixer_forward(pqks, pvg, cq, ck, cv, log_rates, rate_bias, gain):
    rows, length, value_width = pvg.shape
    value_width = value_width // 2
    key_width = value_width * DK // DV
    heads = key_width // DK
    chunks = length // CHUNK
    span = STEP * CHUNK
    seq = lambda width, at=0: pl.BlockSpec((1, span, width), lambda r, c: (r, c, at))
    per = lambda a, b: pl.BlockSpec((1, STEP, heads, a, b), lambda r, c: (r, c, 0, 0, 0))
    return pl.pallas_call(
        functools.partial(mixer_forward_kernel, heads),
        grid=(rows, chunks // STEP),
        in_specs=[seq(key_width), seq(key_width, 1), seq(value_width), seq(value_width, 1),
                  seq(128, 2 * heads),
                  whole_spec((4, key_width)), whole_spec((4, key_width)), whole_spec((4, value_width)),
                  whole_spec((1, 128)), whole_spec((1, 128)), whole_spec((1, DV))],
        out_specs=[seq(value_width), per(CHUNK, CHUNK), per(DK, DV), seq(value_width)],
        out_shape=[
            jax.ShapeDtypeStruct((rows, length, value_width), BF),
            jax.ShapeDtypeStruct((rows, chunks, heads, CHUNK, CHUNK), BF),
            jax.ShapeDtypeStruct((rows, chunks, heads, DK, DV), BF),
            jax.ShapeDtypeStruct((rows, length, value_width), BF),
        ],
        scratch_shapes=[
            pltpu.VMEM((span + 8, key_width), F32),
            pltpu.VMEM((span + 8, key_width), F32),
            pltpu.VMEM((span + 8, value_width), F32),
            pltpu.VMEM((heads, DK, DV), F32),
        ],
        compiler_params=pltpu.CompilerParams(
            dimension_semantics=("arbitrary", "arbitrary"), vmem_limit_bytes=40 << 20
        ),
        cost_estimate=pl.CostEstimate(flops=0, bytes_accessed=int(rows * chunks * heads * 3007812.5), transcendentals=0),
        name="mixer_forward",
    )(pqks, pqks, pvg, pvg, pqks, cq, ck, cv, lane_pad(-jnp.exp(log_rates), 0),
      lane_pad(rate_bias, 0), gain.reshape(1, DV))


def mixer_backward(dm, pqks, pvg, cq, ck, cv, log_rates, rate_bias, gain, t_in, s_in, f_in):
    rows, length, value_width = dm.shape
    key_width = value_width * DK // DV
    heads = key_width // DK
    chunks = length // CHUNK
    span = BACK_STEP * CHUNK
    steps = chunks // BACK_STEP
    seq = lambda width, at=0: pl.BlockSpec(
        (1, span, width), lambda r, c: (r, steps - 1 - c, at)
    )
    before = lambda width, at=0: pl.BlockSpec(
        (1, 8, width),
        lambda r, c: (r, jnp.maximum((steps - 1 - c) * (span // 8) - 1, 0), at),
    )
    per = lambda a, b: pl.BlockSpec(
        (1, BACK_STEP, heads, a, b), lambda r, c: (r, steps - 1 - c, 0, 0, 0)
    )
    seq_shape = lambda width: jax.ShapeDtypeStruct((rows, length, width), BF)
    return pl.pallas_call(
        functools.partial(mixer_backward_kernel, heads),
        grid=(rows, steps),
        in_specs=[seq(value_width), seq(key_width), seq(key_width, 1), seq(value_width),
                  seq(value_width, 1), seq(128, 2 * heads),
                  before(key_width), before(key_width, 1), before(value_width),
                  whole_spec((4, key_width)), whole_spec((4, key_width)), whole_spec((4, value_width)),
                  whole_spec((1, 128)), whole_spec((1, 128)), whole_spec((1, DV)),
                  per(CHUNK, CHUNK), per(DK, DV), seq(value_width)],
        out_specs=[seq(2 * key_width + 128), seq(2 * value_width),
                   whole_spec((8, key_width)), whole_spec((8, key_width)), whole_spec((8, value_width)),
                   whole_spec((8, 128)), whole_spec((8, DV))],
        out_shape=[seq_shape(2 * key_width + 128), seq_shape(2 * value_width),
                   jax.ShapeDtypeStruct((8, key_width), F32),
                   jax.ShapeDtypeStruct((8, key_width), F32),
                   jax.ShapeDtypeStruct((8, value_width), F32),
                   jax.ShapeDtypeStruct((8, 128), F32),
                   jax.ShapeDtypeStruct((8, DV), F32)],
        scratch_shapes=[
            pltpu.VMEM((span + 8, key_width), F32),
            pltpu.VMEM((span + 8, key_width), F32),
            pltpu.VMEM((span + 8, value_width), F32),
            pltpu.VMEM((span + 8, key_width), F32),
            pltpu.VMEM((span + 8, key_width), F32),
            pltpu.VMEM((span + 8, value_width), F32),
            pltpu.VMEM((heads, DK, DV), F32),
        ],
        compiler_params=pltpu.CompilerParams(
            dimension_semantics=("arbitrary", "arbitrary"), vmem_limit_bytes=48 << 20
        ),
        cost_estimate=pl.CostEstimate(flops=0, bytes_accessed=int(rows * chunks * heads * 4921875.0), transcendentals=0),
        name="mixer_backward",
    )(dm, pqks, pqks, pvg, pvg, pqks, pqks, pqks, pvg, cq, ck, cv, lane_pad(-jnp.exp(log_rates), 0),
      lane_pad(rate_bias, 0), gain.reshape(1, DV), t_in, s_in, f_in)


FREE = pl.CostEstimate(flops=0, bytes_accessed=0, transcendentals=0)
VMEM_LIMIT = 44 << 20
WIDE_LIMIT = 58 << 20
SMALL_LIMIT = 16 << 20


def rows_kernel(count, nt, has_weigh, at, *refs):
    out = refs[-2] if has_weigh else refs[-1]
    total = None
    for i in range(count):
        part = lax.dot_general(
            refs[2 * i][0], refs[2 * i + 1][...], NT if nt else NN, preferred_element_type=F32
        )
        total = part if total is None else total + part
    if has_weigh:
        refs[-1][0, 0:1, :] = jnp.sum(
            total * refs[2 * count][0].astype(F32), axis=0, keepdims=True
        )
    out[0] = total.astype(out.dtype)


def rows_matmul(
    pairs, piece, nt=False, tile=512, take=0, weigh=None, into=None, put=0, dtype=BF, limit=WIDE_LIMIT
):
    rows = pairs[0][0].shape[0]
    width = pairs[0][1].shape[0 if nt else 1]
    tile = min(tile, width)
    at = jnp.stack([jnp.int32(take), jnp.int32(put)])
    specs, args = [], []
    for a, w in pairs:
        depth = a.shape[2]
        specs.append(pl.BlockSpec((1, piece, depth), lambda r, n, at: (r, at[0], 0)))
        if nt:
            specs.append(pl.BlockSpec((tile, depth), lambda r, n, at: (n, 0)))
        else:
            specs.append(pl.BlockSpec((depth, tile), lambda r, n, at: (0, n)))
        args.extend((a, w))
    if weigh is not None:
        specs.append(pl.BlockSpec((1, piece, tile), lambda r, n, at: (r, 0, n)))
        args.append(weigh)
    aliases = {}
    shape = (rows, piece, width)
    if into is not None:
        shape = into.shape
        dtype = into.dtype
        if not isinstance(into, jax.ShapeDtypeStruct):
            specs.append(pl.BlockSpec(memory_space=pl.ANY))
            args.append(into)
            aliases = {len(args): 0}
    out_specs = [pl.BlockSpec((1, piece, tile), lambda r, n, at: (r, at[1], n))]
    out_shape = [jax.ShapeDtypeStruct(shape, dtype)]
    if weigh is not None:
        out_specs.append(pl.BlockSpec((1, 8, tile), lambda r, n, at: (r, 0, n)))
        out_shape.append(jax.ShapeDtypeStruct((rows, 8, width), F32))
    out = pl.pallas_call(
        functools.partial(rows_kernel, len(pairs), nt, weigh is not None),
        grid_spec=pltpu.PrefetchScalarGridSpec(
            num_scalar_prefetch=1,
            grid=(rows, pl.cdiv(width, tile)),
            in_specs=specs,
            out_specs=out_specs,
        ),
        out_shape=out_shape,
        input_output_aliases=aliases,
        compiler_params=pltpu.CompilerParams(
            dimension_semantics=("arbitrary", "arbitrary"), vmem_limit_bytes=limit
        ),
        cost_estimate=FREE,
        name="rows_matmul",
    )(at, *args)
    return out[0] if weigh is None else (out[0], jnp.sum(out[1][:, 0:1], axis=0))


def outer_kernel(count, blocks, groups, parts, at, *refs):
    xs, gs = refs[:count], refs[count : 2 * count]
    extras = list(refs[2 * count : -1 - parts])
    outs, flipped = refs[-1 - parts : -1], refs[-1]
    rows, piece, width = xs[0].shape
    depth = rows * piece
    block = flipped.shape[0] // blocks

    @pl.when(pl.program_id(0) == 0)
    def _():
        for i, x in enumerate(xs):
            for k in range(blocks):
                start = pl.multiple_of((2 * k + at[0]) * block, block)
                part = x[:, :, pl.ds(start, block)].reshape(depth, block)
                flipped[k * block : (k + 1) * block, i * depth : (i + 1) * depth] = part.T

    total = None
    for i, g in enumerate(gs):
        part = lax.dot_general(
            flipped[:, i * depth : (i + 1) * depth],
            g[...].reshape(depth, g.shape[2]),
            NN,
            preferred_element_type=F32,
        )
        total = part if total is None else total + part
    for size in groups:
        held, extras = extras[:size], extras[size:]
        total = total + jnp.concatenate([x[...].astype(F32) for x in held], axis=0)
    lines = total.shape[0] // parts
    for i, out in enumerate(outs):
        out[...] = total[i * lines : (i + 1) * lines].astype(out.dtype)


def outer_sum(xs, gs, places, core, data, tile=512, adds=(), dtype=BF, parts=1):
    rows, piece, width = xs[0].shape
    columns = gs[0].shape[2]
    tile = min(tile, columns)
    at = jnp.stack([jnp.int32(core)] + [jnp.int32(x) for x in places])
    whole = pl.BlockSpec(
        (rows, piece, width), lambda n, at: (0, 0, 0), pipeline_mode=pl.Buffered(1)
    )
    specs = [whole] * len(xs)
    for i in range(len(gs)):
        specs.append(
            pl.BlockSpec((rows, piece, tile), lambda n, at, i=i: (0, at[1 + i], n))
        )
    args = [*xs, *gs]
    lines = lambda count: pl.BlockSpec((width // 2 // count, tile), lambda n, at: (0, n))
    for group in adds:
        specs.extend([lines(len(group))] * len(group))
        args.extend(group)
    return pl.pallas_call(
        functools.partial(outer_kernel, len(xs), data // 2, [len(x) for x in adds], parts),
        grid_spec=pltpu.PrefetchScalarGridSpec(
            num_scalar_prefetch=1,
            grid=(columns // tile,),
            in_specs=specs,
            out_specs=[lines(parts)] * parts,
            scratch_shapes=[pltpu.VMEM((width // 2, len(xs) * rows * piece), BF)],
        ),
        out_shape=[jax.ShapeDtypeStruct((width // 2 // parts, columns), dtype)] * parts,
        compiler_params=pltpu.CompilerParams(
            dimension_semantics=("arbitrary",), vmem_limit_bytes=VMEM_LIMIT
        ),
        cost_estimate=FREE,
        name="outer_sum",
    )(at, *args)


UNITS = 256


def lanes_of(units):
    return 128 if units % 128 == 0 else 64


def mlp_kernel(lanes, x, wgu, g, wd, hidden, grads):
    mlp_finish(lanes, lax.dot_general(x[...], wgu[...], NN, preferred_element_type=F32), g, wd, hidden, grads)


def mlp_finish(lanes, both, g, wd, hidden, grads):
    back = lax.dot_general(g[...], wd[...], NN, preferred_element_type=F32)
    for at in range(0, UNITS, lanes):
        first, second = 2 * at, 2 * at + lanes
        gate = both[:, first : first + lanes]
        up = both[:, second : second + lanes]
        own = back[:, at : at + lanes]
        sig = sigmoid(gate)
        act = gate * sig
        hidden[:, at : at + lanes] = (act * up).astype(BF)
        own_gate = own * up * (sig * (1.0 + gate * (1.0 - sig)))
        grads[:, first : first + lanes] = own_gate.astype(BF)
        grads[:, second : second + lanes] = (own * act).astype(BF)


def mlp_block(g, wd, x=None, wgu=None, both=None):
    piece, width = g.shape
    units = wd.shape[1]
    whole = pl.BlockSpec((piece, width), lambda n: (0, 0))
    part = lambda depth, size: pl.BlockSpec((depth, size), lambda n: (0, n))
    if both is None:
        kernel, args = mlp_kernel, (x, wgu, g, wd)
        specs = [whole, part(width, 2 * UNITS), whole, part(width, UNITS)]
    else:
        kernel, args = mlp_finish, (both, g, wd)
        specs = [part(piece, 2 * UNITS), whole, part(width, UNITS)]
    return pl.pallas_call(
        functools.partial(kernel, lanes_of(units)),
        grid=(pl.cdiv(units, UNITS),),
        in_specs=specs,
        out_specs=[part(piece, UNITS), part(piece, 2 * UNITS)],
        out_shape=[
            jax.ShapeDtypeStruct((piece, units), BF),
            jax.ShapeDtypeStruct((piece, 2 * units), BF),
        ],
        compiler_params=pltpu.CompilerParams(
            dimension_semantics=("arbitrary",), vmem_limit_bytes=WIDE_LIMIT
        ),
        cost_estimate=FREE,
        name="mlp_block",
    )(*args)


NORM_ROWS = 128


def row_stats(x):
    r = lax.rsqrt(jnp.mean(x * x, axis=-1, keepdims=True) + NORM_EPS)
    return x * r, r


def norm_grad(n, r, inner):
    return r * (inner - n * jnp.mean(n * inner, axis=-1, keepdims=True))


def valid_rows(at):
    start = at[0] + pl.program_id(1) * NORM_ROWS
    positions = start + lax.broadcasted_iota(jnp.int32, (NORM_ROWS, 1), 0)
    return (positions < at[1 + pl.program_id(0)]).astype(F32)


def enter_kernel(at, tokens, gain, normed):
    normed[0] = (row_stats(tokens[0].astype(F32))[0] * gain[...]).astype(BF)


def middle_kernel(at, own, moved, tokens, gain, middle, normed):
    total = own[0] + moved[0].astype(F32)
    x = tokens[0].astype(F32) + valid_rows(at) * total
    middle[0] = x
    normed[0] = (row_stats(x)[0] * gain[...]).astype(BF)


def middle_back_kernel(at, own, moved, middle, cot, gain, grad_middle, grad_attn, dgain):
    @pl.when((pl.program_id(0) == 0) & (pl.program_id(1) == 0))
    def _():
        dgain[...] = jnp.zeros_like(dgain)

    grad = own[0] + moved[0].astype(F32)
    n, r = row_stats(middle[0])
    dgain[0:1, :] += jnp.sum(grad * n, axis=0, keepdims=True)
    total = cot[0].astype(F32) + norm_grad(n, r, gain[...] * grad)
    grad_middle[0] = total
    grad_attn[0] = (valid_rows(at) * total).astype(BF)


def leave_kernel(at, own, moved, tokens, grad_middle, gain, out):
    grad = own[0] + moved[0].astype(F32)
    n, r = row_stats(tokens[0].astype(F32))
    out[0] = (grad_middle[0] + norm_grad(n, r, gain[...] * grad)).astype(BF)


def result_kernel(at, own, moved, middle, out):
    total = own[0] + moved[0].astype(F32)
    out[0] = (middle[0] + valid_rows(at) * total).astype(BF)


def by_rows(kernel, at, arrays, gain, out_types, with_sum=False, limit=SMALL_LIMIT, cost=FREE):
    rows, piece, width = arrays[0].shape
    block = pl.BlockSpec((1, NORM_ROWS, width), lambda r, t, at: (r, t, 0))
    out_shape = [jax.ShapeDtypeStruct((rows, piece, width), x) for x in out_types]
    out_specs = [block] * len(out_types)
    specs = [block] * len(arrays)
    args = list(arrays)
    if gain is not None:
        specs.append(pl.BlockSpec((1, width), lambda r, t, at: (0, 0)))
        args.append(gain.reshape(1, width))
    if with_sum:
        out_shape.append(jax.ShapeDtypeStruct((8, width), F32))
        out_specs.append(pl.BlockSpec((8, width), lambda r, t, at: (0, 0)))
    return pl.pallas_call(
        kernel,
        grid_spec=pltpu.PrefetchScalarGridSpec(
            num_scalar_prefetch=1,
            grid=(rows, piece // NORM_ROWS),
            in_specs=specs,
            out_specs=out_specs,
        ),
        out_shape=out_shape,
        compiler_params=pltpu.CompilerParams(
            dimension_semantics=("arbitrary", "arbitrary"), vmem_limit_bytes=limit
        ),
        cost_estimate=cost,
        name=kernel.__name__,
    )(at, *args)


def apart_kernel(lanes, gu, gu_moved, down, down_moved, gate, up, out):
    out[...] = down[...].astype(F32) + down_moved[...].astype(F32)
    for at in range(0, gate.shape[1], lanes):
        for first, half in ((2 * at, gate), (2 * at + lanes, up)):
            half[:, at : at + lanes] = gu[:, first : first + lanes].astype(F32) + gu_moved[
                :, first : first + lanes
            ].astype(F32)


def apart(gu, gu_moved, down, down_moved):
    shape = jax.ShapeDtypeStruct(down.shape, F32)
    return pl.pallas_call(
        functools.partial(apart_kernel, lanes_of(down.shape[1])),
        out_shape=[shape, shape, shape],
        compiler_params=pltpu.CompilerParams(vmem_limit_bytes=SMALL_LIMIT),
        cost_estimate=FREE,
        name="apart",
    )(gu, gu_moved, down, down_moved)


def ring(size, group):
    return [(i, i // group * group + (i + 1) % group) for i in range(size)]


def across(size):
    return [(i, (i + size // 2) % size) for i in range(size)]


def swap(size, bit):
    return [(i, i ^ bit) for i in range(size)]


def tie(*values):
    return lax.optimization_barrier(values)


def matmul(a, b):
    return lax.dot_general(a, b, NN, preferred_element_type=F32)


def sum_over(x, axis, size, bit=1):
    while bit < size:
        x = x + lax.ppermute(x, axis, swap(size, bit))
        bit = bit * 2
    return x


def alternate(gate, up):
    units = gate.shape[1]
    lanes = lanes_of(units)
    parts = [x[:, at : at + lanes] for at in range(0, units, lanes) for x in (gate, up)]
    return jnp.concatenate(parts, axis=1)


def per_device(
    tokens,
    lengths,
    gain_attn,
    w_query,
    w_key,
    w_value,
    w_decay,
    w_beta,
    w_gate_out,
    conv_query,
    conv_key,
    conv_value,
    decay_log,
    decay_bias,
    gain_head,
    w_out,
    gain_mlp,
    w_gate,
    w_up,
    w_down,
    cotangent,
):
    rows, piece, width = tokens.shape
    size = lax.axis_size("head")
    data = lax.axis_size("dp")
    me = lax.axis_index("head")
    core = lax.rem(lax.axis_index("dp"), 2)
    length = piece * size
    heads = w_decay.shape[1]
    key_width, value_width = heads * DK, heads * DV
    shape3 = (rows, piece, width)
    flat_piece = rows * piece
    group = size // 2
    at = jnp.concatenate([(me * piece).astype(jnp.int32)[None], lengths])
    positions = me * piece + jnp.arange(piece, dtype=jnp.int32)
    mask = (positions[None, :] < lengths[:, None]).astype(F32)[:, :, None]

    def owner(s):
        return lax.rem(me + size - s, size)

    def step(x, group):
        return lax.ppermute(x, "head", ring(size, group))

    def opposite(x):
        return lax.ppermute(x, "head", across(size))

    def gather_weight(w):
        return lax.all_gather(w, "dp", axis=0, tiled=True)

    def cross(parts):
        return [lax.ppermute(x, "dp", swap(data, 1)) for x in parts]

    def outer_halves(xs, gs, places, tile=512, parts=2, away=(), near=()):
        away = outer_sum(xs, gs, places, 1 - core, data, tile, away, parts=parts)
        return outer_sum(xs, gs, places, core, data, tile, [cross(away), *near])[0]

    def scatter_weight(total):
        places = [[i + c for i in range(0, data, 2)] for c in range(2)]
        return lax.psum_scatter(
            total, "dp", scatter_dimension=0, tiled=True, axis_index_groups=places
        )

    normed = by_rows(enter_kernel, at, [tokens], gain_attn, [BF])[0]
    small_pad = jnp.zeros((w_decay.shape[0], 128 - 2 * heads), BF)
    w_qks = gather_weight(jnp.concatenate([w_query, w_key, w_decay, w_beta, small_pad], axis=1))
    w_vg = gather_weight(jnp.concatenate([w_value, w_gate_out], axis=1))
    wo_full = gather_weight(w_out)

    qks_buffer = jax.ShapeDtypeStruct((rows, length, 2 * key_width + 128), F32)
    vg_buffer = jax.ShapeDtypeStruct((rows, length, 2 * value_width), F32)
    def project_qks(item, s, into):
        return rows_matmul([(item, w_qks)], piece, tile=into.shape[2], into=into, put=owner(s))

    def project_vg(item, s, into):
        return rows_matmul([(item, w_vg)], piece, into=into, put=owner(s))

    pqks = project_qks(normed, 0, qks_buffer)
    pvg = vg_buffer
    pieces = [normed]
    for s in range(1, size):
        send = pieces[-1]
        if s == 1:
            send, w_gate, w_up, cotangent = tie(send, w_gate, w_up, cotangent)
        item = step(send, size)
        if s == 1:
            w_gu = alternate(w_gate, w_up)
            grad_mlp = (mask * cotangent.astype(F32)).astype(BF)
            item, w_gu, grad_mlp = tie(item, w_gu, grad_mlp)
        if s == size - 1:
            for place, early in enumerate(pieces):
                pvg = project_vg(early, place, pvg)
            item, pqks, pvg, w_gu, w_down, grad_mlp = tie(
                item, pqks, pvg, w_gu, w_down, grad_mlp
            )
        elif s > 1:
            item, pqks = tie(item, pqks)
        pqks = project_qks(item, s, pqks)
        pieces.append(item)
    normed_pieces = pieces
    w_gu_other = opposite(w_gu)
    w_down_other = opposite(w_down)
    grad_out = [grad_mlp]
    for _ in range(1, group):
        grad_out.append(step(grad_out[-1], group))
    pvg = project_vg(item, size - 1, pvg)

    cq = lax.dynamic_slice_in_dim(conv_query, me * key_width, key_width, 1)
    ck = lax.dynamic_slice_in_dim(conv_key, me * key_width, key_width, 1)
    cv = lax.dynamic_slice_in_dim(conv_value, me * value_width, value_width, 1)
    log_local = lax.dynamic_slice_in_dim(decay_log, me * heads, heads, 0)
    bias_local = lax.dynamic_slice_in_dim(decay_bias, me * heads, heads, 0)
    mixed, t_kept, s_kept, f_kept = mixer_forward(
        pqks, pvg, cq, ck, cv, log_local, bias_local, gain_head
    )
    mixed, w_gu_other, w_down_other, *grad_out = tie(mixed, w_gu_other, w_down_other, *grad_out)
    wgu_full = [gather_weight(w_gu), gather_weight(w_gu_other)]
    wdown_full = [gather_weight(w_down), gather_weight(w_down_other)]

    def attn_part(s, dtype=F32, limit=VMEM_LIMIT):
        return rows_matmul(
            [(mixed, wo_full)], piece, nt=True, take=owner(s), dtype=dtype, limit=limit
        )

    total = attn_part(1, BF, WIDE_LIMIT)
    for s in range(2, size + 1):
        moved = step(total, size)
        own = attn_part(s % size)
        moved, own = tie(moved, own)
        total = (own + moved.astype(F32)).astype(BF)
    middle, normed_two = by_rows(middle_kernel, at, [own, moved, tokens], gain_mlp, [F32, BF])
    flat2 = lambda x: x.reshape(flat_piece, width)
    second = [normed_two]
    hidden, grad_gu = [[], []], [[], []]

    def keep_block(b, block):
        hidden[b].append(block[0].reshape(rows, piece, -1))
        grad_gu[b].append(block[1].reshape(rows, piece, -1))

    def mlp_part(s, dtype=F32):
        pairs = [(hidden[b][s], wdown_full[b]) for b in range(2)]
        return rows_matmul(pairs, piece, nt=True, dtype=dtype)

    def two_part(s, dtype=F32):
        pairs = [(grad_gu[b][s], wgu_full[b]) for b in range(2)]
        return rows_matmul(pairs, piece, nt=True, dtype=dtype)

    send, own_x, own_g = tie(normed_two, normed_two, grad_out[0])
    for s in range(1, group):
        moved = step(send, group)
        if s == 1:
            for b in range(2):
                keep_block(b, mlp_block(flat2(own_g), wdown_full[b], flat2(own_x), wgu_full[b]))
            own_two = two_part(0)
            moved, own_two, *held = tie(moved, own_two, *hidden[0], *hidden[1], *grad_gu[0], *grad_gu[1])
            hidden, grad_gu = [held[:1], held[1:2]], [held[2:3], held[3:]]
        second.append(moved)
        send = moved
    for s in range(1, group):
        for b in range(2):
            keep_block(
                b, mlp_block(flat2(grad_out[s]), wdown_full[b], flat2(second[s]), wgu_full[b])
            )
    first = [0] * group
    units = hidden[0][0].shape[2]

    def away_pair(b):
        return (
            outer_sum(second, grad_gu[b], first, 1 - core, data, 1408),
            outer_sum(grad_out, hidden[b], first, 1 - core, data, units),
        )

    def near_pair(b, parts):
        return (
            outer_sum(second, grad_gu[b], first, core, data, 1408, [cross(parts[:1])])[0],
            outer_sum(grad_out, hidden[b], first, core, data, units, [cross(parts[1:])])[0],
        )

    total = two_part(1, BF)
    total, *held = tie(total, *hidden[0], *hidden[1], *grad_gu[1])
    hidden, grad_gu[1] = [held[:group], held[group : 2 * group]], held[2 * group :]
    for s in range(2, group + 1):
        moved = step(total, group)
        if s == group:
            own = own_two
            own_mlp, send_mlp = mlp_part(0), mlp_part(1, BF)
            away_gu, away_down = away_pair(1)
            moved, own_mlp, send_mlp, *away = tie(
                moved, own_mlp, send_mlp, *away_gu, *away_down
            )
        else:
            own = two_part(s)
            total = (own + moved.astype(F32)).astype(BF)
    grad_middle, grad_attn, dgain_mlp = by_rows(
        middle_back_kernel, at, [own, moved, middle, cotangent], gain_mlp, [F32, BF], True, WIDE_LIMIT
    )

    pair_gu, pair_down = [None, None], [None, None]
    mixed_buffer = jax.ShapeDtypeStruct((rows, length, value_width), F32)
    grad_mixed = mixed_buffer
    attn_pieces = [grad_attn]
    for s in range(1, size):
        send = attn_pieces[-1]
        if s == 1:
            send, *held = tie(send, *away, *hidden[0], *grad_gu[0])
            away, hidden[0], grad_gu[0] = held[:2], held[2 : 2 + group], held[2 + group :]
        elif s == 2:
            send, *away = tie(send, *away)
        item = step(send, size)
        if s == 1:
            pair_gu[1], pair_down[1] = near_pair(1, away)
            away_gu, away_down = away_pair(0)
            item, pair_gu[1], pair_down[1], *away = tie(
                item, pair_gu[1], pair_down[1], *away_gu, *away_down
            )
        elif s == 2:
            pair_gu[0], pair_down[0] = near_pair(0, away)
            item, pair_gu[0], pair_down[0] = tie(item, pair_gu[0], pair_down[0])
        if s == size - 1:
            for place, early in enumerate(attn_pieces):
                grad_mixed = rows_matmul(
                    [(early, wo_full)], piece, into=grad_mixed, put=owner(place)
                )
            wout_parts = [
                outer_sum(
                    attn_pieces, [mixed] * s, [owner(x) for x in range(s)], side, data, dtype=F32
                )[0]
                for side in (1 - core, core)
            ]
            item, grad_mixed, *wout_parts = tie(item, grad_mixed, *wout_parts)
        attn_pieces.append(item)
    grad_mixed = rows_matmul(
        [(item, wo_full)], piece, into=grad_mixed, put=owner(size - 1), limit=VMEM_LIMIT
    )
    sums_gu = [None, scatter_weight(pair_gu[1])]
    sums_down = [None, scatter_weight(pair_down[1])]
    sums_gu[0] = scatter_weight(pair_gu[0])
    sums_down[0] = scatter_weight(pair_down[0])

    grad_mixed, send_mlp, send_gu, send_down = tie(grad_mixed, send_mlp, sums_gu[1], sums_down[1])
    moved = step(send_mlp, group)
    moved_gu, moved_down = opposite(send_gu), opposite(send_down)
    done = mixer_backward(
        grad_mixed, pqks, pvg, cq, ck, cv, log_local, bias_local, gain_head, t_kept, s_kept, f_kept
    )
    moved, moved_gu, moved_down, gqks, gvg, dcq, dck, dcv, dsm, dgain = tie(
        moved, moved_gu, moved_down, *done
    )
    for s in range(2, group):
        moved = step((mlp_part(s) + moved.astype(F32)).astype(BF), group)
    moved_mlp = moved

    def one_part(s, dtype=F32):
        return rows_matmul(
            [(gqks, w_qks), (gvg, w_vg)], piece, nt=True, take=owner(s),
            weigh=normed_pieces[s], dtype=dtype,
        )

    places = [owner(s) for s in range(size)]
    total, gain_sum = one_part(1, BF)
    for s in range(2, size + 1):
        if s == 3:
            total, attn_last, *last = tie(total, attn_pieces[-1], sums_down[0], sums_gu[0])
            sums_down[0], sums_gu[0] = last
        total, gqks, gvg = tie(total, gqks, gvg)
        if s == size:
            total, pair_qks, pair_wout = tie(total, pair_qks, pair_wout)
            pair_last = jnp.concatenate([pair_qks, pair_wout], axis=1)
            total, moved_mlp, sums_gu[0], sums_down[0], moved_gu, moved_down, *small = tie(
                total, moved_mlp, sums_gu[0], sums_down[0], moved_gu, moved_down,
                dcq, dck, dcv, dsm, dgain, dgain_mlp,
            )
        moved = step(total, size)
        if s < size:
            own, gain_part = one_part(s, BF)
            gain_sum = gain_sum + gain_part
        if s == 2:
            pair_vg = outer_halves(normed_pieces, [gvg] * size, places, 512, 4)
            moved, own, pair_vg = tie(moved, own, pair_vg)
        elif s == 3:
            pair_qks = outer_halves(normed_pieces, [gqks] * size, places, gqks.shape[2])
            pair_wout = outer_halves(
                [attn_last], [mixed], places[-1:], 512, 2, [wout_parts[:1]], [wout_parts[1:]]
            )
            moved, own, pair_qks, pair_wout, out_vg = tie(
                moved, own, pair_qks, pair_wout, scatter_weight(pair_vg)
            )
        if s < size:
            total = (own.astype(F32) + moved.astype(F32)).astype(BF)
            continue
        own, gain_part = one_part(0)
        small = jnp.concatenate(
            [x[:4] for x in small] + [jnp.broadcast_to(gain_sum + gain_part, (4, width))],
            axis=1,
        )
        small = sum_over(small, "dp", data)
        out_wgate, out_wup, out_wdown = apart(sums_gu[0], moved_gu, sums_down[0], moved_down)
        mixed_rows = by_rows(result_kernel, at, [own_mlp, moved_mlp, middle], None, [BF])[0]
        moved, own, small, out_wgate, out_wup, out_wdown, mixed_rows = tie(
            moved, own, small, out_wgate, out_wup, out_wdown, mixed_rows
        )
    leave_cost = pl.CostEstimate(flops=0, bytes_accessed=14 * tokens.size, transcendentals=0)
    tokens_grad = by_rows(
        leave_kernel, at, [own, moved, tokens, grad_middle], gain_attn, [BF], False, WIDE_LIMIT,
        leave_cost,
    )[0]
    out_vg = out_vg.astype(F32)
    out_last = scatter_weight(pair_last).astype(F32)
    out_qks, out_wout = out_last[:, : gqks.shape[2]], out_last[:, gqks.shape[2] :]

    taps_width = 2 * key_width + value_width
    own_width = taps_width + 128
    spread = lax.dynamic_update_slice_in_dim(
        jnp.zeros((4, size * own_width), F32), small[:, :own_width], me * own_width, 1
    )
    small = jnp.concatenate([spread, small[:, own_width:]], axis=1)
    crossed, tokens_grad = tie(lax.ppermute(small, "head", swap(size, 1)), tokens_grad)
    small = sum_over(small + crossed, "head", size, 2)
    by_head = [small[:, i * own_width : (i + 1) * own_width] for i in range(size)]
    taps = lambda start, stop: jnp.concatenate([x[:, start:stop] for x in by_head], axis=1)
    conv_sums = (
        taps(0, key_width),
        taps(key_width, 2 * key_width),
        taps(2 * key_width, taps_width),
    )
    decay_sums = [
        jnp.concatenate([x[i, taps_width : taps_width + heads] for x in by_head]) for i in range(2)
    ]
    gains = small[0, size * own_width :]
    gain_head_out = gains[:DV]
    gain_mlp_out = gains[DV : DV + width]
    gain_attn_out = gains[DV + width :] / gain_attn
    return (
        mixed_rows,
        tokens_grad,
        gain_attn_out,
        out_qks[:, :key_width],
        out_qks[:, key_width : 2 * key_width],
        out_vg[:, :value_width],
        out_qks[:, 2 * key_width : 2 * key_width + heads],
        out_qks[:, 2 * key_width + heads : 2 * key_width + 2 * heads],
        out_vg[:, value_width:],
        conv_sums[0],
        conv_sums[1],
        conv_sums[2],
        decay_sums[0],
        decay_sums[1],
        gain_head_out,
        out_wout,
        gain_mlp_out,
        out_wgate,
        out_wup,
        out_wdown,
    )

def solution(mesh):
    rows = P("dp", "head", None)
    weight = P("dp", "head")
    same = P()
    return jax.shard_map(
        per_device,
        mesh=mesh,
        in_specs=(
            rows, P("dp"), same, weight, weight, weight, weight, weight, weight, same, same, same,
            same, same, same, weight, same, weight, weight, weight, rows,
        ),
        out_specs=(
            rows, rows, same, weight, weight, weight, weight, weight, weight, same, same, same,
            same, same, same, weight, same, weight, weight, weight,
        ),
        check_vma=False,
    )
```

```python
import functools

import jax
import jax.numpy as jnp
from jax import lax
from jax.experimental import pallas as pl
from jax.experimental.pallas import tpu as pltpu
from jax.sharding import PartitionSpec as P

DK = 128
DV = 256
CHUNK = 128
STEP = 4
BACK_STEP = 2
NORM_EPS = 1e-06
BF = jnp.bfloat16
F32 = jnp.float32
NN = (((1,), (0,)), ((), ()))
NT = (((1,), (1,)), ((), ()))
TN = (((0,), (0,)), ((), ()))


def mm(a, b, dims=NN):
    return lax.dot_general(a.astype(BF), b.astype(BF), dims, preferred_element_type=F32)


def split(a):
    high = a.astype(BF)
    return high, (a - high.astype(F32)).astype(BF)


def mm3(a, b, dims=NN):
    ah, al = split(a)
    bh, bl = split(b)
    return mm(ah, bh, dims) + mm(ah, bl, dims) + mm(al, bh, dims)


def exact(a, b, dims=NN):
    return lax.dot_general(a, b, dims, precision=lax.Precision.HIGHEST, preferred_element_type=F32)


def iotas(n):
    return (
        lax.broadcasted_iota(jnp.int32, (n, n), 0),
        lax.broadcasted_iota(jnp.int32, (n, n), 1),
    )


def lower_inverses(lowers):
    n = lowers[0].shape[0]
    row, col = iotas(n)
    eye = (row == col).astype(F32)
    pair = (row // 2 == col // 2).astype(F32)
    inverses = [eye - low * pair for low in lowers]
    size = 2
    while size < n:
        corner = ((row // (2 * size)) == (col // (2 * size))) & ((row // size) != (col // size))
        corner = corner.astype(F32)
        half = [x.astype(BF) for x in inverses]
        inner = [mm(x, low * corner) for x, low in zip(half, lowers)]
        inverses = [x - mm(i, h) for x, i, h in zip(inverses, inner, half)]
        size = size * 2
    residual = [eye - x - mm3(low, x) for low, x in zip(lowers, inverses)]
    return [x + mm(x, r) for x, r in zip(inverses, residual)]


def sigmoid(x):
    return 1.0 / (1.0 + jnp.exp(-x))


def conv_of(buf, taps, sl, start=0):
    total = taps[0:1, sl] * buf[start + 5 : start + 5 + CHUNK, sl]
    for i in range(1, 4):
        total = total + taps[i : i + 1, sl] * buf[start + 5 + i : start + 5 + i + CHUNK, sl]
    return total


def softplus(x):
    return jnp.maximum(x, 0.0) + jnp.log1p(jnp.exp(-jnp.abs(x)))


def silu_slope(a):
    s = sigmoid(a)
    value = a * s
    return value, s + value * (1.0 - s)


def unit(a):
    r = lax.rsqrt(jnp.sum(a * a, axis=-1, keepdims=True) + NORM_EPS)
    return a * r, r


def mixer_forward_kernel(
    heads, pq, pk, pv, pg, ps, cq, ck, cv, rates, bias, gain,
    mixed, t_out, s_out, f_out, bq, bk, bv, state,
):
    step = pl.program_id(1)
    span = STEP * CHUNK

    @pl.when(step == 0)
    def _():
        state[...] = jnp.zeros_like(state)
        for b in (bq, bk, bv):
            b[0:8, :] = jnp.zeros((8, b.shape[1]), F32)

    @pl.when(step > 0)
    def _():
        for b in (bq, bk, bv):
            b[0:8, :] = b[span : span + 8, :]

    for b, p in ((bq, pq), (bk, pk), (bv, pv)):
        b[8 : span + 8, :] = p[0].astype(F32)
    row, col = iotas(CHUNK)
    hs = range(heads)
    both_at = [(j, h) for j in range(STEP) for h in hs]
    ks = [slice(h * DK, (h + 1) * DK) for h in hs]
    vs = [slice(h * DV, (h + 1) * DV) for h in hs]
    lines = [slice(j * CHUNK, (j + 1) * CHUNK) for j in range(STEP)]
    cum, cum_t, betas = [], [], []
    for j in range(STEP):
        small = ps[0, lines[j], :]
        g = rates[...] * softplus(small + bias[...])
        betas.append(sigmoid(small))
        cum.append(exact((row >= col).astype(F32), g))
        cum_t.append(cum[j].T)
    q, k, v, within, kbeta, gamma, rem, last = {}, {}, {}, {}, {}, {}, {}, {}
    for x in both_at:
        j, h = x
        a = conv_of(bq, cq, ks[h], j * CHUNK)
        q[x] = unit(a * sigmoid(a))[0]
        a = conv_of(bk, ck, ks[h], j * CHUNK)
        k[x] = unit(a * sigmoid(a))[0]
        a = conv_of(bv, cv, vs[h], j * CHUNK)
        v[x] = a * sigmoid(a)
        gc = cum[j][:, h : h + 1]
        within[x] = jnp.exp(jnp.where(row >= col, gc - cum_t[j][h : h + 1, :], -1e30))
        kbeta[x] = betas[j][:, heads + h : heads + h + 1]
        gamma[x] = jnp.exp(gc)
        tail = cum[j][CHUNK - 1 : CHUNK, h : h + 1]
        rem[x] = jnp.exp(tail - gc)
        last[x] = jnp.exp(tail)
    kb = {x: k[x].astype(BF) for x in both_at}
    lowers = [
        jnp.where(row > col, kbeta[x] * (mm(kb[x], kb[x], NT) * within[x]), 0.0) for x in both_at
    ]
    scores = {x: mm(q[x], kb[x], NT) * within[x] for x in both_at}
    inv = dict(zip(both_at, lower_inverses(lowers)))
    states = [state[h] for h in hs]
    for j in range(STEP):
        sb = [s.astype(BF) for s in states]
        both = [
            mm(jnp.concatenate([gamma[j, h] * k[j, h], gamma[j, h] * q[j, h]], axis=0), sb[h])
            for h in hs
        ]
        fb = [
            mm(inv[j, h], kbeta[j, h] * (v[j, h] - both[h][:CHUNK])).astype(BF) for h in hs
        ]
        out = [(both[h][CHUNK:] + mm(scores[j, h], fb[h])) * DK**-0.5 for h in hs]
        states = [
            last[j, h] * states[h] + mm(rem[j, h] * k[j, h], fb[h], TN) for h in hs
        ]
        for h in hs:
            t_out[0, j, h] = inv[j, h].astype(t_out.dtype)
            s_out[0, j, h] = sb[h]
            f_out[0, lines[j], vs[h]] = fb[h]
            o = out[h]
            r = lax.rsqrt(jnp.mean(o * o, axis=-1, keepdims=True) + NORM_EPS)
            p = pg[0, lines[j], vs[h]].astype(F32)
            mixed[0, lines[j], vs[h]] = (o * r * gain[...] * (p * sigmoid(p))).astype(BF)
    for h in hs:
        state[h] = states[h]


def mixer_backward_kernel(
    heads, dm, pq, pk, pv, pg, ps, tq, tk, tv, cq, ck, cv, rates, bias, gain, t_in, s_in, f_in,
    gqks, gvg, dcq, dck, dcv, dsm, dgain,
    bq, bk, bv, eq, ek, ev, dstate,
):
    row_at = pl.program_id(0)
    step = pl.program_id(1)
    chunk = pl.num_programs(1) - 1 - step
    span = BACK_STEP * CHUNK

    @pl.when((row_at == 0) & (step == 0))
    def _():
        for r in (dcq, dck, dcv, dsm, dgain):
            r[...] = jnp.zeros_like(r)

    @pl.when(step == 0)
    def _():
        dstate[...] = jnp.zeros_like(dstate)
        for b in (eq, ek, ev):
            b[span : span + 8, :] = jnp.zeros((8, b.shape[1]), F32)

    @pl.when(step > 0)
    def _():
        for b in (eq, ek, ev):
            b[span : span + 8, :] = b[0:8, :]

    has_before = (chunk > 0).astype(F32)
    for b, p, t in ((bq, pq, tq), (bk, pk, tk), (bv, pv, tv)):
        b[0:8, :] = t[0].astype(F32) * has_before
        b[8 : span + 8, :] = p[0].astype(F32)
    row, col = iotas(CHUNK)
    lane = col
    hs = range(heads)
    at = [(j, h) for j in range(BACK_STEP) for h in hs]
    ks = [slice(h * DK, (h + 1) * DK) for h in hs]
    vs = [slice(h * DV, (h + 1) * DV) for h in hs]
    lines = [slice(j * CHUNK, (j + 1) * CHUNK) for j in range(BACK_STEP)]
    scale = DK**-0.5
    small, shifted, g, betas, cum, cum_t = [], [], [], [], [], []
    for j in range(BACK_STEP):
        small.append(ps[0, lines[j], :])
        shifted.append(small[j] + bias[...])
        g.append(rates[...] * softplus(shifted[j]))
        betas.append(sigmoid(small[j]))
        cum.append(exact((row >= col).astype(F32), g[j]))
        cum_t.append(cum[j].T)
    q, k, v, rq, rk, kbeta, gamma, rem, last, within = {}, {}, {}, {}, {}, {}, {}, {}, {}, {}
    sq, sk, sv = {}, {}, {}
    for x in at:
        j, h = x
        a, sq[x] = silu_slope(conv_of(bq, cq, ks[h], j * CHUNK))
        q[x], rq[x] = unit(a)
        a, sk[x] = silu_slope(conv_of(bk, ck, ks[h], j * CHUNK))
        k[x], rk[x] = unit(a)
        v[x], sv[x] = silu_slope(conv_of(bv, cv, vs[h], j * CHUNK))
        gc = cum[j][:, h : h + 1]
        within[x] = jnp.exp(jnp.where(row >= col, gc - cum_t[j][h : h + 1, :], -1e30))
        kbeta[x] = betas[j][:, heads + h : heads + h + 1]
        gamma[x] = jnp.exp(gc)
        tail = cum[j][CHUNK - 1 : CHUNK, h : h + 1]
        rem[x] = jnp.exp(tail - gc)
        last[x] = jnp.exp(tail)
    qb = {x: q[x].astype(BF) for x in at}
    kb = {x: k[x].astype(BF) for x in at}
    sb = {x: s_in[0, x[0], x[1]] for x in at}
    fb = {x: f_in[0, lines[x[0]], vs[x[1]]] for x in at}
    tb = {x: t_in[0, x[0], x[1]] for x in at}
    gram = {x: mm(kb[x], kb[x], NT) * within[x] for x in at}
    scores = {x: mm(qb[x], kb[x], NT) * within[x] for x in at}
    gk_gq = {x: jnp.concatenate([gamma[x] * k[x], gamma[x] * q[x]], axis=0) for x in at}
    both = {x: mm(gk_gq[x], sb[x]) for x in at}
    x_in = {x: v[x] - both[x][:CHUNK] for x in at}
    out = {x: (both[x][CHUNK:] + mm(scores[x], fb[x])) * scale for x in at}
    head_dgain = jnp.zeros((1, DV), F32)
    dout = {}
    for x in at:
        j, h = x
        o = out[x]
        r = lax.rsqrt(jnp.mean(o * o, axis=-1, keepdims=True) + NORM_EPS)
        n = o * r
        p = pg[0, lines[j], vs[h]].astype(F32)
        s = sigmoid(p)
        d = dm[0, lines[j], vs[h]].astype(F32)
        y = n * gain[...]
        start = heads * DV + h * DV
        gvg[0, lines[j], start : start + DV] = (d * y * (s * (1.0 + p * (1.0 - s)))).astype(BF)
        dy = d * (p * s)
        head_dgain = head_dgain + jnp.sum(dy * n, axis=0, keepdims=True)
        dn = dy * gain[...]
        dout[x] = scale * r * (dn - n * jnp.mean(n * dn, axis=-1, keepdims=True))
    dgain[0:1, :] += head_dgain
    dob = {x: dout[x].astype(BF) for x in at}
    krem = {x: rem[x] * k[x] for x in at}
    dfresh_own = {x: mm(scores[x], dob[x], TN) for x in at}
    dscore = {x: mm(dob[x], fb[x], NT) for x in at}
    ds_next, dsb, dr, dx, dx_do = {}, {}, {}, {}, {}
    ds = [dstate[h] for h in hs]
    for j in reversed(range(BACK_STEP)):
        for h in hs:
            ds_next[j, h] = ds[h]
            dsb[j, h] = ds[h].astype(BF)
        dfresh = [dfresh_own[j, h] + mm(krem[j, h], dsb[j, h]) for h in hs]
        for h in hs:
            dr[j, h] = mm(tb[j, h], dfresh[h], TN)
        for h in hs:
            dx[j, h] = kbeta[j, h] * dr[j, h]
            dx_do[j, h] = jnp.concatenate([-dx[j, h], dout[j, h]], axis=0).astype(BF)
        ds = [last[j, h] * ds[h] + mm(gk_gq[j, h], dx_do[j, h], TN) for h in hs]
    for h in hs:
        dstate[h] = ds[h]
    dgk_gq = {x: mm(dx_do[x], sb[x], NT) for x in at}
    dkrem = {x: mm(fb[x], dsb[x], NT) for x in at}
    dlow = {x: jnp.where(row > col, -mm(dr[x], fb[x], NT), 0.0) for x in at}
    dcum = [jnp.zeros((CHUNK, CHUNK), F32) for _ in range(BACK_STEP)]
    dcum_rows = [jnp.zeros((CHUNK, CHUNK), F32) for _ in range(BACK_STEP)]
    dbeta = [jnp.zeros((CHUNK, CHUNK), F32) for _ in range(BACK_STEP)]
    for x in at:
        j, h = x
        m = dscore[x] * within[x]
        dgram = kbeta[x] * (dlow[x] * within[x])
        lg = dlow[x] * gram[x]
        e = dscore[x] * scores[x] + kbeta[x] * lg
        dq = gamma[x] * dgk_gq[x][CHUNK:] + mm(m, kb[x])
        mk = jnp.concatenate([m, dgram], axis=0)
        dk = (
            gamma[x] * dgk_gq[x][:CHUNK]
            + rem[x] * dkrem[x]
            + mm(mk, jnp.concatenate([qb[x], kb[x]], axis=0), TN)
            + mm(dgram, kb[x])
        )
        rem_part = jnp.sum(dkrem[x] * krem[x], axis=-1, keepdims=True)
        head_dcum = (
            jnp.sum(e, axis=-1, keepdims=True)
            + jnp.sum(
                dgk_gq[x][:CHUNK] * gk_gq[x][:CHUNK] + dgk_gq[x][CHUNK:] * gk_gq[x][CHUNK:],
                axis=-1, keepdims=True,
            )
            - rem_part
        )
        state_part = jnp.sum(
            jnp.sum(ds_next[x] * sb[x].astype(F32), axis=0, keepdims=True), axis=1, keepdims=True
        )
        end_part = jnp.sum(rem_part, axis=0, keepdims=True) + last[x] * state_part
        head_dcum = head_dcum + jnp.where(row[:, 0:1] == CHUNK - 1, end_part, 0.0)
        dcum[j] = dcum[j] + jnp.where(lane == h, head_dcum, 0.0)
        dcum_rows[j] = dcum_rows[j] + jnp.where(
            row == h, jnp.sum(e, axis=0, keepdims=True), 0.0
        )
        head_dbeta = jnp.sum(dr[x] * x_in[x], axis=-1, keepdims=True) + jnp.sum(
            lg, axis=-1, keepdims=True
        )
        dbeta[j] = dbeta[j] + jnp.where(lane == heads + h, head_dbeta, 0.0)
        da = rq[x] * (dq - q[x] * jnp.sum(q[x] * dq, axis=-1, keepdims=True))
        eq[lines[j], ks[h]] = da * sq[x]
        da = rk[x] * (dk - k[x] * jnp.sum(k[x] * dk, axis=-1, keepdims=True))
        ek[lines[j], ks[h]] = da * sk[x]
        ev[lines[j], vs[h]] = dx[x] * sv[x]
    for j in range(BACK_STEP):
        dg = exact((row >= col).astype(F32), dcum[j] - dcum_rows[j].T, TN)
        dshift = dg * rates[...] * sigmoid(shifted[j])
        dsm[0:1, :] += jnp.sum(dg * g[j], axis=0, keepdims=True)
        dsm[1:2, :] += jnp.sum(dshift, axis=0, keepdims=True)
        gqks[0, lines[j], 2 * heads * DK :] = (
            jnp.where(lane < heads, dshift, 0.0) + dbeta[j] * betas[j] * (1.0 - betas[j])
        ).astype(BF)
    for b, e, taps, dtaps, out_ref, start in (
        (bq, eq, cq, dcq, gqks, 0), (bk, ek, ck, dck, gqks, heads * DK), (bv, ev, cv, dcv, gvg, 0),
    ):
        for first in range(0, b.shape[1], DK):
            sl = slice(first, first + DK)
            own = e[0:span, sl]
            total = taps[3:4, sl] * own
            for i in range(3):
                total = total + taps[i : i + 1, sl] * e[3 - i : 3 - i + span, sl]
            out_ref[0, :, start + first : start + first + DK] = total.astype(BF)
            for i in range(4):
                dtaps[i : i + 1, sl] += jnp.sum(
                    own * b[5 + i : 5 + i + span, sl], axis=0, keepdims=True
                )


def whole_spec(shape):
    return pl.BlockSpec(shape, lambda r, c: (0,) * len(shape))


def lane_pad(vec, at):
    return jnp.zeros((1, 128), F32).at[0, at : at + vec.shape[0]].set(vec)


def mixer_forward(pqks, pvg, cq, ck, cv, log_rates, rate_bias, gain):
    rows, length, value_width = pvg.shape
    value_width = value_width // 2
    key_width = value_width * DK // DV
    heads = key_width // DK
    chunks = length // CHUNK
    span = STEP * CHUNK
    seq = lambda width, at=0: pl.BlockSpec((1, span, width), lambda r, c: (r, c, at))
    per = lambda a, b: pl.BlockSpec((1, STEP, heads, a, b), lambda r, c: (r, c, 0, 0, 0))
    return pl.pallas_call(
        functools.partial(mixer_forward_kernel, heads),
        grid=(rows, chunks // STEP),
        in_specs=[seq(key_width), seq(key_width, 1), seq(value_width), seq(value_width, 1),
                  seq(128, 2 * heads),
                  whole_spec((4, key_width)), whole_spec((4, key_width)), whole_spec((4, value_width)),
                  whole_spec((1, 128)), whole_spec((1, 128)), whole_spec((1, DV))],
        out_specs=[seq(value_width), per(CHUNK, CHUNK), per(DK, DV), seq(value_width)],
        out_shape=[
            jax.ShapeDtypeStruct((rows, length, value_width), BF),
            jax.ShapeDtypeStruct((rows, chunks, heads, CHUNK, CHUNK), BF),
            jax.ShapeDtypeStruct((rows, chunks, heads, DK, DV), BF),
            jax.ShapeDtypeStruct((rows, length, value_width), BF),
        ],
        scratch_shapes=[
            pltpu.VMEM((span + 8, key_width), F32),
            pltpu.VMEM((span + 8, key_width), F32),
            pltpu.VMEM((span + 8, value_width), F32),
            pltpu.VMEM((heads, DK, DV), F32),
        ],
        compiler_params=pltpu.CompilerParams(
            dimension_semantics=("arbitrary", "arbitrary"), vmem_limit_bytes=40 << 20
        ),
        cost_estimate=pl.CostEstimate(flops=0, bytes_accessed=int(rows * chunks * heads * 3007812.5), transcendentals=0),
        name="mixer_forward",
    )(pqks, pqks, pvg, pvg, pqks, cq, ck, cv, lane_pad(-jnp.exp(log_rates), 0),
      lane_pad(rate_bias, 0), gain.reshape(1, DV))


def mixer_backward(dm, pqks, pvg, cq, ck, cv, log_rates, rate_bias, gain, t_in, s_in, f_in):
    rows, length, value_width = dm.shape
    key_width = value_width * DK // DV
    heads = key_width // DK
    chunks = length // CHUNK
    span = BACK_STEP * CHUNK
    steps = chunks // BACK_STEP
    seq = lambda width, at=0: pl.BlockSpec(
        (1, span, width), lambda r, c: (r, steps - 1 - c, at)
    )
    before = lambda width, at=0: pl.BlockSpec(
        (1, 8, width),
        lambda r, c: (r, jnp.maximum((steps - 1 - c) * (span // 8) - 1, 0), at),
    )
    per = lambda a, b: pl.BlockSpec(
        (1, BACK_STEP, heads, a, b), lambda r, c: (r, steps - 1 - c, 0, 0, 0)
    )
    seq_shape = lambda width: jax.ShapeDtypeStruct((rows, length, width), BF)
    return pl.pallas_call(
        functools.partial(mixer_backward_kernel, heads),
        grid=(rows, steps),
        in_specs=[seq(value_width), seq(key_width), seq(key_width, 1), seq(value_width),
                  seq(value_width, 1), seq(128, 2 * heads),
                  before(key_width), before(key_width, 1), before(value_width),
                  whole_spec((4, key_width)), whole_spec((4, key_width)), whole_spec((4, value_width)),
                  whole_spec((1, 128)), whole_spec((1, 128)), whole_spec((1, DV)),
                  per(CHUNK, CHUNK), per(DK, DV), seq(value_width)],
        out_specs=[seq(2 * key_width + 128), seq(2 * value_width),
                   whole_spec((8, key_width)), whole_spec((8, key_width)), whole_spec((8, value_width)),
                   whole_spec((8, 128)), whole_spec((8, DV))],
        out_shape=[seq_shape(2 * key_width + 128), seq_shape(2 * value_width),
                   jax.ShapeDtypeStruct((8, key_width), F32),
                   jax.ShapeDtypeStruct((8, key_width), F32),
                   jax.ShapeDtypeStruct((8, value_width), F32),
                   jax.ShapeDtypeStruct((8, 128), F32),
                   jax.ShapeDtypeStruct((8, DV), F32)],
        scratch_shapes=[
            pltpu.VMEM((span + 8, key_width), F32),
            pltpu.VMEM((span + 8, key_width), F32),
            pltpu.VMEM((span + 8, value_width), F32),
            pltpu.VMEM((span + 8, key_width), F32),
            pltpu.VMEM((span + 8, key_width), F32),
            pltpu.VMEM((span + 8, value_width), F32),
            pltpu.VMEM((heads, DK, DV), F32),
        ],
        compiler_params=pltpu.CompilerParams(
            dimension_semantics=("arbitrary", "arbitrary"), vmem_limit_bytes=48 << 20
        ),
        cost_estimate=pl.CostEstimate(flops=0, bytes_accessed=int(rows * chunks * heads * 4921875.0), transcendentals=0),
        name="mixer_backward",
    )(dm, pqks, pqks, pvg, pvg, pqks, pqks, pqks, pvg, cq, ck, cv, lane_pad(-jnp.exp(log_rates), 0),
      lane_pad(rate_bias, 0), gain.reshape(1, DV), t_in, s_in, f_in)


FREE = pl.CostEstimate(flops=0, bytes_accessed=0, transcendentals=0)
VMEM_LIMIT = 44 << 20
WIDE_LIMIT = 58 << 20
SMALL_LIMIT = 16 << 20


def rows_kernel(count, nt, has_weigh, at, *refs):
    out = refs[-2] if has_weigh else refs[-1]
    total = None
    for i in range(count):
        part = lax.dot_general(
            refs[2 * i][0], refs[2 * i + 1][...], NT if nt else NN, preferred_element_type=F32
        )
        total = part if total is None else total + part
    if has_weigh:
        refs[-1][0, 0:1, :] = jnp.sum(
            total * refs[2 * count][0].astype(F32), axis=0, keepdims=True
        )
    out[0] = total.astype(out.dtype)


def rows_matmul(
    pairs, piece, nt=False, tile=512, take=0, weigh=None, into=None, put=0, dtype=BF, limit=WIDE_LIMIT
):
    rows = pairs[0][0].shape[0]
    width = pairs[0][1].shape[0 if nt else 1]
    tile = min(tile, width)
    at = jnp.stack([jnp.int32(take), jnp.int32(put)])
    specs, args = [], []
    for a, w in pairs:
        depth = a.shape[2]
        specs.append(pl.BlockSpec((1, piece, depth), lambda r, n, at: (r, at[0], 0)))
        if nt:
            specs.append(pl.BlockSpec((tile, depth), lambda r, n, at: (n, 0)))
        else:
            specs.append(pl.BlockSpec((depth, tile), lambda r, n, at: (0, n)))
        args.extend((a, w))
    if weigh is not None:
        specs.append(pl.BlockSpec((1, piece, tile), lambda r, n, at: (r, 0, n)))
        args.append(weigh)
    aliases = {}
    shape = (rows, piece, width)
    if into is not None:
        shape = into.shape
        dtype = into.dtype
        if not isinstance(into, jax.ShapeDtypeStruct):
            specs.append(pl.BlockSpec(memory_space=pl.ANY))
            args.append(into)
            aliases = {len(args): 0}
    out_specs = [pl.BlockSpec((1, piece, tile), lambda r, n, at: (r, at[1], n))]
    out_shape = [jax.ShapeDtypeStruct(shape, dtype)]
    if weigh is not None:
        out_specs.append(pl.BlockSpec((1, 8, tile), lambda r, n, at: (r, 0, n)))
        out_shape.append(jax.ShapeDtypeStruct((rows, 8, width), F32))
    out = pl.pallas_call(
        functools.partial(rows_kernel, len(pairs), nt, weigh is not None),
        grid_spec=pltpu.PrefetchScalarGridSpec(
            num_scalar_prefetch=1,
            grid=(rows, pl.cdiv(width, tile)),
            in_specs=specs,
            out_specs=out_specs,
        ),
        out_shape=out_shape,
        input_output_aliases=aliases,
        compiler_params=pltpu.CompilerParams(
            dimension_semantics=("arbitrary", "arbitrary"), vmem_limit_bytes=limit
        ),
        cost_estimate=FREE,
        name="rows_matmul",
    )(at, *args)
    return out[0] if weigh is None else (out[0], jnp.sum(out[1][:, 0:1], axis=0))


def outer_kernel(count, blocks, groups, parts, at, *refs):
    xs, gs = refs[:count], refs[count : 2 * count]
    extras = list(refs[2 * count : -1 - parts])
    outs, flipped = refs[-1 - parts : -1], refs[-1]
    rows, piece, width = xs[0].shape
    depth = rows * piece
    block = flipped.shape[0] // blocks

    @pl.when(pl.program_id(0) == 0)
    def _():
        for i, x in enumerate(xs):
            for k in range(blocks):
                start = pl.multiple_of((2 * k + at[0]) * block, block)
                part = x[:, :, pl.ds(start, block)].reshape(depth, block)
                flipped[k * block : (k + 1) * block, i * depth : (i + 1) * depth] = part.T

    total = None
    for i, g in enumerate(gs):
        part = lax.dot_general(
            flipped[:, i * depth : (i + 1) * depth],
            g[...].reshape(depth, g.shape[2]),
            NN,
            preferred_element_type=F32,
        )
        total = part if total is None else total + part
    for size in groups:
        held, extras = extras[:size], extras[size:]
        total = total + jnp.concatenate([x[...].astype(F32) for x in held], axis=0)
    lines = total.shape[0] // parts
    for i, out in enumerate(outs):
        out[...] = total[i * lines : (i + 1) * lines].astype(out.dtype)


def outer_sum(xs, gs, places, core, data, tile=512, adds=(), dtype=BF, parts=1):
    rows, piece, width = xs[0].shape
    columns = gs[0].shape[2]
    tile = min(tile, columns)
    at = jnp.stack([jnp.int32(core)] + [jnp.int32(x) for x in places])
    whole = pl.BlockSpec(
        (rows, piece, width), lambda n, at: (0, 0, 0), pipeline_mode=pl.Buffered(1)
    )
    specs = [whole] * len(xs)
    for i in range(len(gs)):
        specs.append(
            pl.BlockSpec((rows, piece, tile), lambda n, at, i=i: (0, at[1 + i], n))
        )
    args = [*xs, *gs]
    lines = lambda count: pl.BlockSpec((width // 2 // count, tile), lambda n, at: (0, n))
    for group in adds:
        specs.extend([lines(len(group))] * len(group))
        args.extend(group)
    return pl.pallas_call(
        functools.partial(outer_kernel, len(xs), data // 2, [len(x) for x in adds], parts),
        grid_spec=pltpu.PrefetchScalarGridSpec(
            num_scalar_prefetch=1,
            grid=(columns // tile,),
            in_specs=specs,
            out_specs=[lines(parts)] * parts,
            scratch_shapes=[pltpu.VMEM((width // 2, len(xs) * rows * piece), BF)],
        ),
        out_shape=[jax.ShapeDtypeStruct((width // 2 // parts, columns), dtype)] * parts,
        compiler_params=pltpu.CompilerParams(
            dimension_semantics=("arbitrary",), vmem_limit_bytes=VMEM_LIMIT
        ),
        cost_estimate=FREE,
        name="outer_sum",
    )(at, *args)


UNITS = 256


def lanes_of(units):
    return 128 if units % 128 == 0 else 64


def mlp_kernel(lanes, x, wgu, back, hidden, grads):
    both = lax.dot_general(x[...], wgu[...], NN, preferred_element_type=F32)
    for at in range(0, UNITS, lanes):
        first, second = 2 * at, 2 * at + lanes
        gate = both[:, first : first + lanes]
        up = both[:, second : second + lanes]
        own = back[:, at : at + lanes]
        sig = sigmoid(gate)
        act = gate * sig
        hidden[:, at : at + lanes] = (act * up).astype(BF)
        own_gate = own * up * (sig * (1.0 + gate * (1.0 - sig)))
        grads[:, first : first + lanes] = own_gate.astype(BF)
        grads[:, second : second + lanes] = (own * act).astype(BF)


def mlp_block(x, wgu, back):
    piece, width = x.shape
    units = back.shape[1]
    part = lambda depth, size: pl.BlockSpec((depth, size), lambda n: (0, n))
    return pl.pallas_call(
        functools.partial(mlp_kernel, lanes_of(units)),
        grid=(pl.cdiv(units, UNITS),),
        in_specs=[
            pl.BlockSpec((piece, width), lambda n: (0, 0)),
            part(width, 2 * UNITS),
            part(piece, UNITS),
        ],
        out_specs=[part(piece, UNITS), part(piece, 2 * UNITS)],
        out_shape=[
            jax.ShapeDtypeStruct((piece, units), BF),
            jax.ShapeDtypeStruct((piece, 2 * units), BF),
        ],
        compiler_params=pltpu.CompilerParams(
            dimension_semantics=("arbitrary",), vmem_limit_bytes=WIDE_LIMIT
        ),
        cost_estimate=FREE,
        name="mlp_block",
    )(x, wgu, back)


NORM_ROWS = 128


def row_stats(x):
    r = lax.rsqrt(jnp.mean(x * x, axis=-1, keepdims=True) + NORM_EPS)
    return x * r, r


def norm_grad(n, r, inner):
    return r * (inner - n * jnp.mean(n * inner, axis=-1, keepdims=True))


def valid_rows(at):
    start = at[0] + pl.program_id(1) * NORM_ROWS
    positions = start + lax.broadcasted_iota(jnp.int32, (NORM_ROWS, 1), 0)
    return (positions < at[1 + pl.program_id(0)]).astype(F32)


def enter_kernel(at, tokens, gain, normed):
    normed[0] = (row_stats(tokens[0].astype(F32))[0] * gain[...]).astype(BF)


def middle_kernel(at, own, moved, tokens, gain, middle, normed):
    total = own[0] + moved[0].astype(F32)
    x = tokens[0].astype(F32) + valid_rows(at) * total
    middle[0] = x
    normed[0] = (row_stats(x)[0] * gain[...]).astype(BF)


def middle_back_kernel(at, own, moved, middle, cot, gain, grad_middle, grad_attn, dgain):
    @pl.when((pl.program_id(0) == 0) & (pl.program_id(1) == 0))
    def _():
        dgain[...] = jnp.zeros_like(dgain)

    grad = own[0] + moved[0].astype(F32)
    n, r = row_stats(middle[0])
    dgain[0:1, :] += jnp.sum(grad * n, axis=0, keepdims=True)
    total = cot[0].astype(F32) + norm_grad(n, r, gain[...] * grad)
    grad_middle[0] = total
    grad_attn[0] = (valid_rows(at) * total).astype(BF)


def leave_kernel(at, own, moved, tokens, grad_middle, gain, out):
    grad = own[0] + moved[0].astype(F32)
    n, r = row_stats(tokens[0].astype(F32))
    out[0] = (grad_middle[0] + norm_grad(n, r, gain[...] * grad)).astype(BF)


def result_kernel(at, own, moved, middle, out):
    total = own[0] + moved[0].astype(F32)
    out[0] = (middle[0] + valid_rows(at) * total).astype(BF)


def by_rows(kernel, at, arrays, gain, out_types, with_sum=False, limit=SMALL_LIMIT, cost=FREE):
    rows, piece, width = arrays[0].shape
    block = pl.BlockSpec((1, NORM_ROWS, width), lambda r, t, at: (r, t, 0))
    out_shape = [jax.ShapeDtypeStruct((rows, piece, width), x) for x in out_types]
    out_specs = [block] * len(out_types)
    specs = [block] * len(arrays)
    args = list(arrays)
    if gain is not None:
        specs.append(pl.BlockSpec((1, width), lambda r, t, at: (0, 0)))
        args.append(gain.reshape(1, width))
    if with_sum:
        out_shape.append(jax.ShapeDtypeStruct((8, width), F32))
        out_specs.append(pl.BlockSpec((8, width), lambda r, t, at: (0, 0)))
    return pl.pallas_call(
        kernel,
        grid_spec=pltpu.PrefetchScalarGridSpec(
            num_scalar_prefetch=1,
            grid=(rows, piece // NORM_ROWS),
            in_specs=specs,
            out_specs=out_specs,
        ),
        out_shape=out_shape,
        compiler_params=pltpu.CompilerParams(
            dimension_semantics=("arbitrary", "arbitrary"), vmem_limit_bytes=limit
        ),
        cost_estimate=cost,
        name=kernel.__name__,
    )(at, *args)


def apart_kernel(lanes, gu, gu_moved, down, down_moved, gate, up, out):
    out[...] = down[...].astype(F32) + down_moved[...].astype(F32)
    for at in range(0, gate.shape[1], lanes):
        for first, half in ((2 * at, gate), (2 * at + lanes, up)):
            half[:, at : at + lanes] = gu[:, first : first + lanes].astype(F32) + gu_moved[
                :, first : first + lanes
            ].astype(F32)


def apart(gu, gu_moved, down, down_moved):
    shape = jax.ShapeDtypeStruct(down.shape, F32)
    return pl.pallas_call(
        functools.partial(apart_kernel, lanes_of(down.shape[1])),
        out_shape=[shape, shape, shape],
        compiler_params=pltpu.CompilerParams(vmem_limit_bytes=SMALL_LIMIT),
        cost_estimate=FREE,
        name="apart",
    )(gu, gu_moved, down, down_moved)


def ring(size, group):
    return [(i, i // group * group + (i + 1) % group) for i in range(size)]


def across(size):
    return [(i, (i + size // 2) % size) for i in range(size)]


def swap(size, bit):
    return [(i, i ^ bit) for i in range(size)]


def tie(*values):
    return lax.optimization_barrier(values)


def matmul(a, b):
    return lax.dot_general(a, b, NN, preferred_element_type=F32)


def sum_over(x, axis, size):
    bit = 1
    while bit < size:
        x = x + lax.ppermute(x, axis, swap(size, bit))
        bit = bit * 2
    return x


def alternate(gate, up):
    units = gate.shape[1]
    lanes = lanes_of(units)
    parts = [x[:, at : at + lanes] for at in range(0, units, lanes) for x in (gate, up)]
    return jnp.concatenate(parts, axis=1)


def per_device(
    tokens,
    lengths,
    gain_attn,
    w_query,
    w_key,
    w_value,
    w_decay,
    w_beta,
    w_gate_out,
    conv_query,
    conv_key,
    conv_value,
    decay_log,
    decay_bias,
    gain_head,
    w_out,
    gain_mlp,
    w_gate,
    w_up,
    w_down,
    cotangent,
):
    rows, piece, width = tokens.shape
    size = lax.axis_size("head")
    data = lax.axis_size("dp")
    me = lax.axis_index("head")
    core = lax.rem(lax.axis_index("dp"), 2)
    length = piece * size
    heads = w_decay.shape[1]
    key_width, value_width = heads * DK, heads * DV
    shape3 = (rows, piece, width)
    flat_piece = rows * piece
    group = size // 2
    at = jnp.concatenate([(me * piece).astype(jnp.int32)[None], lengths])
    positions = me * piece + jnp.arange(piece, dtype=jnp.int32)
    mask = (positions[None, :] < lengths[:, None]).astype(F32)[:, :, None]

    def owner(s):
        return lax.rem(me + size - s, size)

    def step(x, group):
        return lax.ppermute(x, "head", ring(size, group))

    def opposite(x):
        return lax.ppermute(x, "head", across(size))

    def gather_weight(w):
        return lax.all_gather(w, "dp", axis=0, tiled=True)

    def cross(parts):
        return [lax.ppermute(x, "dp", swap(data, 1)) for x in parts]

    def outer_halves(xs, gs, places, tile=512, parts=2, away=(), near=()):
        away = outer_sum(xs, gs, places, 1 - core, data, tile, away, parts=parts)
        return outer_sum(xs, gs, places, core, data, tile, [cross(away), *near])[0]

    def scatter_weight(total):
        places = [[i + c for i in range(0, data, 2)] for c in range(2)]
        return lax.psum_scatter(
            total, "dp", scatter_dimension=0, tiled=True, axis_index_groups=places
        )

    normed = by_rows(enter_kernel, at, [tokens], gain_attn, [BF])[0]
    normed, w_query = tie(normed, w_query)
    small_pad = jnp.zeros((w_decay.shape[0], 128 - 2 * heads), BF)
    w_qks = gather_weight(jnp.concatenate([w_query, w_key, w_decay, w_beta, small_pad], axis=1))
    w_vg = gather_weight(jnp.concatenate([w_value, w_gate_out], axis=1))
    wo_full = gather_weight(w_out)

    qks_buffer = jax.ShapeDtypeStruct((rows, length, 2 * key_width + 128), F32)
    vg_buffer = jax.ShapeDtypeStruct((rows, length, 2 * value_width), F32)
    def project_qks(item, s, into):
        return rows_matmul([(item, w_qks)], piece, tile=into.shape[2], into=into, put=owner(s))

    def project_vg(item, s, into):
        return rows_matmul([(item, w_vg)], piece, into=into, put=owner(s))

    pqks = project_qks(normed, 0, qks_buffer)
    pvg = vg_buffer
    pieces = [normed]
    for s in range(1, size):
        send = pieces[-1]
        if s == 1:
            send, w_gate, w_up, cotangent = tie(send, w_gate, w_up, cotangent)
        item = step(send, size)
        if s == 1:
            w_gu = alternate(w_gate, w_up)
            grad_mlp = (mask * cotangent.astype(F32)).astype(BF)
            item, w_gu, grad_mlp = tie(item, w_gu, grad_mlp)
        if s == size - 1:
            for place, early in enumerate(pieces):
                pvg = project_vg(early, place, pvg)
            item, pqks, pvg, w_gu, w_down, grad_mlp = tie(
                item, pqks, pvg, w_gu, w_down, grad_mlp
            )
        elif s > 1:
            item, pqks = tie(item, pqks)
        pqks = project_qks(item, s, pqks)
        pieces.append(item)
    normed_pieces = pieces
    w_gu_other = opposite(w_gu)
    w_down_other = opposite(w_down)
    grad_out = [grad_mlp]
    for _ in range(1, group):
        grad_out.append(step(grad_out[-1], group))
    pvg = project_vg(item, size - 1, pvg)

    cq = lax.dynamic_slice_in_dim(conv_query, me * key_width, key_width, 1)
    ck = lax.dynamic_slice_in_dim(conv_key, me * key_width, key_width, 1)
    cv = lax.dynamic_slice_in_dim(conv_value, me * value_width, value_width, 1)
    log_local = lax.dynamic_slice_in_dim(decay_log, me * heads, heads, 0)
    bias_local = lax.dynamic_slice_in_dim(decay_bias, me * heads, heads, 0)
    mixed, t_kept, s_kept, f_kept = mixer_forward(
        pqks, pvg, cq, ck, cv, log_local, bias_local, gain_head
    )
    mixed, w_gu_other, w_down_other, *grad_out = tie(mixed, w_gu_other, w_down_other, *grad_out)
    wgu_full = [gather_weight(w_gu), gather_weight(w_gu_other)]
    wdown_full = [gather_weight(w_down), gather_weight(w_down_other)]

    def attn_part(s, dtype=F32, limit=VMEM_LIMIT):
        return rows_matmul(
            [(mixed, wo_full)], piece, nt=True, take=owner(s), dtype=dtype, limit=limit
        )

    def back_parts(b):
        return [
            rows_matmul([(g, wdown_full[b])], piece, tile=768, dtype=F32, limit=VMEM_LIMIT)
            for g in grad_out
        ]

    back = [None, None]
    total = attn_part(1, BF, WIDE_LIMIT)
    for s in range(2, size + 1):
        moved = step(total, size)
        own = attn_part(s % size)
        if s == size - 1:
            moved, own, wgu_full[0], *back[0] = tie(moved, own, wgu_full[0], *back_parts(0))
        elif s == size:
            moved, own, *back[1] = tie(moved, own, *back_parts(1))
        else:
            moved, own = tie(moved, own)
        total = (own + moved.astype(F32)).astype(BF)
    middle, normed_two = by_rows(middle_kernel, at, [own, moved, tokens], gain_mlp, [F32, BF])
    flat2 = lambda x: x.reshape(flat_piece, width)
    flat_units = lambda x: x.reshape(flat_piece, x.shape[2])
    second = [normed_two]
    hidden, grad_gu = [[], []], [[], []]

    def keep_block(b, block):
        hidden[b].append(block[0].reshape(rows, piece, -1))
        grad_gu[b].append(block[1].reshape(rows, piece, -1))

    def mlp_part(s, dtype=F32):
        pairs = [(hidden[b][s], wdown_full[b]) for b in range(2)]
        return rows_matmul(pairs, piece, nt=True, dtype=dtype)

    def two_part(s, dtype=F32):
        pairs = [(grad_gu[b][s], wgu_full[b]) for b in range(2)]
        return rows_matmul(pairs, piece, nt=True, dtype=dtype)

    send, own_x = tie(normed_two, normed_two)
    for s in range(1, group):
        moved = step(send, group)
        if s == 1:
            for b in range(2):
                keep_block(b, mlp_block(flat2(own_x), wgu_full[b], flat_units(back[b][0])))
            own_two = two_part(0)
            moved, own_two, *held = tie(moved, own_two, *hidden[0], *hidden[1], *grad_gu[0], *grad_gu[1])
            hidden, grad_gu = [held[:1], held[1:2]], [held[2:3], held[3:]]
        second.append(moved)
        send = moved
    for s in range(1, group):
        for b in range(2):
            keep_block(b, mlp_block(flat2(second[s]), wgu_full[b], flat_units(back[b][s])))
    first = [0] * group
    units = hidden[0][0].shape[2]

    def away_pair(b):
        return (
            outer_sum(second, grad_gu[b], first, 1 - core, data, 1408),
            outer_sum(grad_out, hidden[b], first, 1 - core, data, units),
        )

    def near_pair(b, parts):
        return (
            outer_sum(second, grad_gu[b], first, core, data, 1408, [cross(parts[:1])])[0],
            outer_sum(grad_out, hidden[b], first, core, data, units, [cross(parts[1:])])[0],
        )

    total = two_part(1, BF)
    total, *held = tie(total, *hidden[0], *hidden[1], *grad_gu[1])
    hidden, grad_gu[1] = [held[:group], held[group : 2 * group]], held[2 * group :]
    for s in range(2, group + 1):
        moved = step(total, group)
        if s == group:
            own = own_two
            own_mlp, send_mlp = mlp_part(0), mlp_part(1, BF)
            away_gu, away_down = away_pair(1)
            moved, own_mlp, send_mlp, *away = tie(
                moved, own_mlp, send_mlp, *away_gu, *away_down
            )
        else:
            own = two_part(s)
            total = (own + moved.astype(F32)).astype(BF)
    grad_middle, grad_attn, dgain_mlp = by_rows(
        middle_back_kernel, at, [own, moved, middle, cotangent], gain_mlp, [F32, BF], True, WIDE_LIMIT
    )

    pair_gu, pair_down = [None, None], [None, None]
    mixed_buffer = jax.ShapeDtypeStruct((rows, length, value_width), F32)
    grad_mixed = mixed_buffer
    attn_pieces = [grad_attn]
    for s in range(1, size):
        send = attn_pieces[-1]
        if s == 1:
            send, *held = tie(send, *away, *hidden[0], *grad_gu[0])
            away, hidden[0], grad_gu[0] = held[:2], held[2 : 2 + group], held[2 + group :]
        elif s == 2:
            send, *away = tie(send, *away)
        item = step(send, size)
        if s == 1:
            pair_gu[1], pair_down[1] = near_pair(1, away)
            away_gu, away_down = away_pair(0)
            item, pair_gu[1], pair_down[1], *away = tie(
                item, pair_gu[1], pair_down[1], *away_gu, *away_down
            )
        elif s == 2:
            pair_gu[0], pair_down[0] = near_pair(0, away)
            item, pair_gu[0], pair_down[0] = tie(item, pair_gu[0], pair_down[0])
        if s == size - 1:
            for place, early in enumerate(attn_pieces):
                grad_mixed = rows_matmul(
                    [(early, wo_full)], piece, into=grad_mixed, put=owner(place)
                )
            wout_parts = [
                outer_sum(
                    attn_pieces, [mixed] * s, [owner(x) for x in range(s)], side, data, dtype=F32
                )[0]
                for side in (1 - core, core)
            ]
            item, grad_mixed, *wout_parts = tie(item, grad_mixed, *wout_parts)
        attn_pieces.append(item)
    grad_mixed = rows_matmul(
        [(item, wo_full)], piece, into=grad_mixed, put=owner(size - 1), limit=VMEM_LIMIT
    )
    sums_gu = [None, scatter_weight(pair_gu[1])]
    sums_down = [None, scatter_weight(pair_down[1])]
    sums_gu[0] = scatter_weight(pair_gu[0])
    sums_down[0] = scatter_weight(pair_down[0])

    grad_mixed, send_mlp, send_gu, send_down = tie(grad_mixed, send_mlp, sums_gu[1], sums_down[1])
    moved = step(send_mlp, group)
    moved_gu, moved_down = opposite(send_gu), opposite(send_down)
    done = mixer_backward(
        grad_mixed, pqks, pvg, cq, ck, cv, log_local, bias_local, gain_head, t_kept, s_kept, f_kept
    )
    moved, moved_gu, moved_down, gqks, gvg, dcq, dck, dcv, dsm, dgain = tie(
        moved, moved_gu, moved_down, *done
    )
    for s in range(2, group):
        moved = step((mlp_part(s) + moved.astype(F32)).astype(BF), group)
    moved_mlp = moved

    def one_part(s, dtype=F32):
        return rows_matmul(
            [(gqks, w_qks), (gvg, w_vg)], piece, nt=True, take=owner(s),
            weigh=normed_pieces[s], dtype=dtype,
        )

    places = [owner(s) for s in range(size)]
    total, gain_sum = one_part(1, BF)
    for s in range(2, size + 1):
        if s == 3:
            total, attn_last, *last = tie(total, attn_pieces[-1], sums_down[0], sums_gu[0])
            sums_down[0], sums_gu[0] = last
        total, gqks, gvg = tie(total, gqks, gvg)
        if s == size:
            total, pair_qks, pair_wout = tie(total, pair_qks, pair_wout)
            pair_last = jnp.concatenate([pair_qks, pair_wout], axis=1)
            total, moved_mlp, sums_gu[0], sums_down[0], moved_gu, moved_down, *small = tie(
                total, moved_mlp, sums_gu[0], sums_down[0], moved_gu, moved_down,
                dcq, dck, dcv, dsm, dgain, dgain_mlp,
            )
        moved = step(total, size)
        if s < size:
            own, gain_part = one_part(s, BF)
            gain_sum = gain_sum + gain_part
        if s == 2:
            pair_vg = outer_halves(normed_pieces, [gvg] * size, places, 512, 4)
            moved, own, pair_vg = tie(moved, own, pair_vg)
        elif s == 3:
            pair_qks = outer_halves(normed_pieces, [gqks] * size, places, gqks.shape[2])
            pair_wout = outer_halves(
                [attn_last], [mixed], places[-1:], 512, 2, [wout_parts[:1]], [wout_parts[1:]]
            )
            moved, own, pair_qks, pair_wout, out_vg = tie(
                moved, own, pair_qks, pair_wout, scatter_weight(pair_vg)
            )
        if s < size:
            total = (own.astype(F32) + moved.astype(F32)).astype(BF)
            continue
        own, gain_part = one_part(0)
        small = jnp.concatenate(
            [x[:4] for x in small] + [jnp.broadcast_to(gain_sum + gain_part, (4, width))],
            axis=1,
        )
        small = sum_over(small, "dp", data)
        out_wgate, out_wup, out_wdown = apart(sums_gu[0], moved_gu, sums_down[0], moved_down)
        mixed_rows = by_rows(result_kernel, at, [own_mlp, moved_mlp, middle], None, [BF])[0]
        moved, own, small, out_wgate, out_wup, out_wdown, mixed_rows = tie(
            moved, own, small, out_wgate, out_wup, out_wdown, mixed_rows
        )
    leave_cost = pl.CostEstimate(flops=0, bytes_accessed=14 * tokens.size, transcendentals=0)
    tokens_grad = by_rows(
        leave_kernel, at, [own, moved, tokens, grad_middle], gain_attn, [BF], False, WIDE_LIMIT,
        leave_cost,
    )[0]
    out_vg = out_vg.astype(F32)
    out_last = scatter_weight(pair_last).astype(F32)
    out_qks, out_wout = out_last[:, : gqks.shape[2]], out_last[:, gqks.shape[2] :]

    taps_width = 2 * key_width + value_width
    own_width = taps_width + 128
    spread, line = small[:, :own_width], small[0:1, own_width:]
    bit = 1
    while bit < size:
        above = (me // bit) % 2 == 1
        crossed = lax.ppermute(spread, "head", swap(size, bit))
        line_crossed = lax.ppermute(line, "head", swap(size, bit))
        if bit == 1:
            crossed, line_crossed, tokens_grad = tie(crossed, line_crossed, tokens_grad)
        low = jnp.where(above, crossed, spread)
        high = jnp.where(above, spread, crossed)
        spread = jnp.concatenate([low, high], axis=1)
        line = line + line_crossed
        bit = bit * 2
    by_head = [spread[:, i * own_width : (i + 1) * own_width] for i in range(size)]
    taps = lambda start, stop: jnp.concatenate([x[:, start:stop] for x in by_head], axis=1)
    conv_sums = (
        taps(0, key_width),
        taps(key_width, 2 * key_width),
        taps(2 * key_width, taps_width),
    )
    decay_sums = [
        jnp.concatenate([x[i, taps_width : taps_width + heads] for x in by_head]) for i in range(2)
    ]
    gains = line[0]
    gain_head_out = gains[:DV]
    gain_mlp_out = gains[DV : DV + width]
    gain_attn_out = gains[DV + width :] / gain_attn
    return (
        mixed_rows,
        tokens_grad,
        gain_attn_out,
        out_qks[:, :key_width],
        out_qks[:, key_width : 2 * key_width],
        out_vg[:, :value_width],
        out_qks[:, 2 * key_width : 2 * key_width + heads],
        out_qks[:, 2 * key_width + heads : 2 * key_width + 2 * heads],
        out_vg[:, value_width:],
        conv_sums[0],
        conv_sums[1],
        conv_sums[2],
        decay_sums[0],
        decay_sums[1],
        gain_head_out,
        out_wout,
        gain_mlp_out,
        out_wgate,
        out_wup,
        out_wdown,
    )

def solution(mesh):
    rows = P("dp", "head", None)
    weight = P("dp", "head")
    same = P()
    return jax.shard_map(
        per_device,
        mesh=mesh,
        in_specs=(
            rows, P("dp"), same, weight, weight, weight, weight, weight, weight, same, same, same,
            same, same, same, weight, same, weight, weight, weight, rows,
        ),
        out_specs=(
            rows, rows, same, weight, weight, weight, weight, weight, weight, same, same, same,
            same, same, same, weight, same, weight, weight, weight,
        ),
        check_vma=False,
    )
```

```python
import functools

import jax
import jax.numpy as jnp
from jax import lax
from jax.experimental import pallas as pl
from jax.experimental.pallas import tpu as pltpu
from jax.sharding import PartitionSpec as P

DK = 128
DV = 256
CHUNK = 128
STEP = 4
BACK_STEP = 2
NORM_EPS = 1e-06
BF = jnp.bfloat16
F32 = jnp.float32
NN = (((1,), (0,)), ((), ()))
NT = (((1,), (1,)), ((), ()))
TN = (((0,), (0,)), ((), ()))


def mm(a, b, dims=NN):
    return lax.dot_general(a.astype(BF), b.astype(BF), dims, preferred_element_type=F32)


def split(a):
    high = a.astype(BF)
    return high, (a - high.astype(F32)).astype(BF)


def mm3(a, b, dims=NN):
    ah, al = split(a)
    bh, bl = split(b)
    return mm(ah, bh, dims) + mm(ah, bl, dims) + mm(al, bh, dims)


def exact(a, b, dims=NN):
    return lax.dot_general(a, b, dims, precision=lax.Precision.HIGHEST, preferred_element_type=F32)


def iotas(n):
    return (
        lax.broadcasted_iota(jnp.int32, (n, n), 0),
        lax.broadcasted_iota(jnp.int32, (n, n), 1),
    )


def lower_inverses(lowers):
    n = lowers[0].shape[0]
    row, col = iotas(n)
    eye = (row == col).astype(F32)
    pair = (row // 2 == col // 2).astype(F32)
    inverses = [eye - low * pair for low in lowers]
    size = 2
    while size < n:
        corner = ((row // (2 * size)) == (col // (2 * size))) & ((row // size) != (col // size))
        corner = corner.astype(F32)
        half = [x.astype(BF) for x in inverses]
        inner = [mm(x, low * corner) for x, low in zip(half, lowers)]
        inverses = [x - mm(i, h) for x, i, h in zip(inverses, inner, half)]
        size = size * 2
    residual = [eye - x - mm3(low, x) for low, x in zip(lowers, inverses)]
    return [x + mm(x, r) for x, r in zip(inverses, residual)]


def sigmoid(x):
    return 1.0 / (1.0 + jnp.exp(-x))


def conv_of(buf, taps, sl, start=0):
    total = taps[0:1, sl] * buf[start + 5 : start + 5 + CHUNK, sl]
    for i in range(1, 4):
        total = total + taps[i : i + 1, sl] * buf[start + 5 + i : start + 5 + i + CHUNK, sl]
    return total


def softplus(x):
    return jnp.maximum(x, 0.0) + jnp.log1p(jnp.exp(-jnp.abs(x)))


def silu_slope(a):
    s = sigmoid(a)
    value = a * s
    return value, s + value * (1.0 - s)


def unit(a):
    r = lax.rsqrt(jnp.sum(a * a, axis=-1, keepdims=True) + NORM_EPS)
    return a * r, r


def mixer_forward_kernel(
    heads, pq, pk, pv, pg, ps, cq, ck, cv, rates, bias, gain,
    mixed, t_out, s_out, f_out, bq, bk, bv, state,
):
    step = pl.program_id(1)
    span = STEP * CHUNK

    @pl.when(step == 0)
    def _():
        state[...] = jnp.zeros_like(state)
        for b in (bq, bk, bv):
            b[0:8, :] = jnp.zeros((8, b.shape[1]), F32)

    @pl.when(step > 0)
    def _():
        for b in (bq, bk, bv):
            b[0:8, :] = b[span : span + 8, :]

    for b, p in ((bq, pq), (bk, pk), (bv, pv)):
        b[8 : span + 8, :] = p[0].astype(F32)
    row, col = iotas(CHUNK)
    hs = range(heads)
    both_at = [(j, h) for j in range(STEP) for h in hs]
    ks = [slice(h * DK, (h + 1) * DK) for h in hs]
    vs = [slice(h * DV, (h + 1) * DV) for h in hs]
    lines = [slice(j * CHUNK, (j + 1) * CHUNK) for j in range(STEP)]
    cum, cum_t, betas = [], [], []
    for j in range(STEP):
        small = ps[0, lines[j], :]
        g = rates[...] * softplus(small + bias[...])
        betas.append(sigmoid(small))
        cum.append(exact((row >= col).astype(F32), g))
        cum_t.append(cum[j].T)
    q, k, v, within, kbeta, gamma, rem, last = {}, {}, {}, {}, {}, {}, {}, {}
    for x in both_at:
        j, h = x
        a = conv_of(bq, cq, ks[h], j * CHUNK)
        q[x] = unit(a * sigmoid(a))[0]
        a = conv_of(bk, ck, ks[h], j * CHUNK)
        k[x] = unit(a * sigmoid(a))[0]
        a = conv_of(bv, cv, vs[h], j * CHUNK)
        v[x] = a * sigmoid(a)
        gc = cum[j][:, h : h + 1]
        within[x] = jnp.exp(jnp.where(row >= col, gc - cum_t[j][h : h + 1, :], -1e30))
        kbeta[x] = betas[j][:, heads + h : heads + h + 1]
        gamma[x] = jnp.exp(gc)
        tail = cum[j][CHUNK - 1 : CHUNK, h : h + 1]
        rem[x] = jnp.exp(tail - gc)
        last[x] = jnp.exp(tail)
    kb = {x: k[x].astype(BF) for x in both_at}
    lowers = [
        jnp.where(row > col, kbeta[x] * (mm(kb[x], kb[x], NT) * within[x]), 0.0) for x in both_at
    ]
    scores = {x: mm(q[x], kb[x], NT) * within[x] for x in both_at}
    inv = dict(zip(both_at, lower_inverses(lowers)))
    states = [state[h] for h in hs]
    for j in range(STEP):
        sb = [s.astype(BF) for s in states]
        both = [
            mm(jnp.concatenate([gamma[j, h] * k[j, h], gamma[j, h] * q[j, h]], axis=0), sb[h])
            for h in hs
        ]
        fb = [
            mm(inv[j, h], kbeta[j, h] * (v[j, h] - both[h][:CHUNK])).astype(BF) for h in hs
        ]
        out = [(both[h][CHUNK:] + mm(scores[j, h], fb[h])) * DK**-0.5 for h in hs]
        states = [
            last[j, h] * states[h] + mm(rem[j, h] * k[j, h], fb[h], TN) for h in hs
        ]
        for h in hs:
            t_out[0, j, h] = inv[j, h].astype(t_out.dtype)
            s_out[0, j, h] = sb[h]
            f_out[0, lines[j], vs[h]] = fb[h]
            o = out[h]
            r = lax.rsqrt(jnp.mean(o * o, axis=-1, keepdims=True) + NORM_EPS)
            p = pg[0, lines[j], vs[h]].astype(F32)
            mixed[0, lines[j], vs[h]] = (o * r * gain[...] * (p * sigmoid(p))).astype(BF)
    for h in hs:
        state[h] = states[h]


def mixer_backward_kernel(
    heads, dm, pq, pk, pv, pg, ps, tq, tk, tv, cq, ck, cv, rates, bias, gain, t_in, s_in, f_in,
    gqks, gvg, dcq, dck, dcv, dsm, dgain,
    bq, bk, bv, eq, ek, ev, dstate,
):
    row_at = pl.program_id(0)
    step = pl.program_id(1)
    chunk = pl.num_programs(1) - 1 - step
    span = BACK_STEP * CHUNK

    @pl.when((row_at == 0) & (step == 0))
    def _():
        for r in (dcq, dck, dcv, dsm, dgain):
            r[...] = jnp.zeros_like(r)

    @pl.when(step == 0)
    def _():
        dstate[...] = jnp.zeros_like(dstate)
        for b in (eq, ek, ev):
            b[span : span + 8, :] = jnp.zeros((8, b.shape[1]), F32)

    @pl.when(step > 0)
    def _():
        for b in (eq, ek, ev):
            b[span : span + 8, :] = b[0:8, :]

    has_before = (chunk > 0).astype(F32)
    for b, p, t in ((bq, pq, tq), (bk, pk, tk), (bv, pv, tv)):
        b[0:8, :] = t[0].astype(F32) * has_before
        b[8 : span + 8, :] = p[0].astype(F32)
    row, col = iotas(CHUNK)
    lane = col
    hs = range(heads)
    at = [(j, h) for j in range(BACK_STEP) for h in hs]
    ks = [slice(h * DK, (h + 1) * DK) for h in hs]
    vs = [slice(h * DV, (h + 1) * DV) for h in hs]
    lines = [slice(j * CHUNK, (j + 1) * CHUNK) for j in range(BACK_STEP)]
    scale = DK**-0.5
    small, shifted, g, betas, cum, cum_t = [], [], [], [], [], []
    for j in range(BACK_STEP):
        small.append(ps[0, lines[j], :])
        shifted.append(small[j] + bias[...])
        g.append(rates[...] * softplus(shifted[j]))
        betas.append(sigmoid(small[j]))
        cum.append(exact((row >= col).astype(F32), g[j]))
        cum_t.append(cum[j].T)
    q, k, v, rq, rk, kbeta, gamma, rem, last, within = {}, {}, {}, {}, {}, {}, {}, {}, {}, {}
    sq, sk, sv = {}, {}, {}
    for x in at:
        j, h = x
        a, sq[x] = silu_slope(conv_of(bq, cq, ks[h], j * CHUNK))
        q[x], rq[x] = unit(a)
        a, sk[x] = silu_slope(conv_of(bk, ck, ks[h], j * CHUNK))
        k[x], rk[x] = unit(a)
        v[x], sv[x] = silu_slope(conv_of(bv, cv, vs[h], j * CHUNK))
        gc = cum[j][:, h : h + 1]
        within[x] = jnp.exp(jnp.where(row >= col, gc - cum_t[j][h : h + 1, :], -1e30))
        kbeta[x] = betas[j][:, heads + h : heads + h + 1]
        gamma[x] = jnp.exp(gc)
        tail = cum[j][CHUNK - 1 : CHUNK, h : h + 1]
        rem[x] = jnp.exp(tail - gc)
        last[x] = jnp.exp(tail)
    qb = {x: q[x].astype(BF) for x in at}
    kb = {x: k[x].astype(BF) for x in at}
    sb = {x: s_in[0, x[0], x[1]] for x in at}
    fb = {x: f_in[0, lines[x[0]], vs[x[1]]] for x in at}
    tb = {x: t_in[0, x[0], x[1]] for x in at}
    gram = {x: mm(kb[x], kb[x], NT) * within[x] for x in at}
    scores = {x: mm(qb[x], kb[x], NT) * within[x] for x in at}
    gk_gq = {x: jnp.concatenate([gamma[x] * k[x], gamma[x] * q[x]], axis=0) for x in at}
    both = {x: mm(gk_gq[x], sb[x]) for x in at}
    x_in = {x: v[x] - both[x][:CHUNK] for x in at}
    out = {x: (both[x][CHUNK:] + mm(scores[x], fb[x])) * scale for x in at}
    head_dgain = jnp.zeros((1, DV), F32)
    dout = {}
    for x in at:
        j, h = x
        o = out[x]
        r = lax.rsqrt(jnp.mean(o * o, axis=-1, keepdims=True) + NORM_EPS)
        n = o * r
        p = pg[0, lines[j], vs[h]].astype(F32)
        s = sigmoid(p)
        d = dm[0, lines[j], vs[h]].astype(F32)
        y = n * gain[...]
        start = heads * DV + h * DV
        gvg[0, lines[j], start : start + DV] = (d * y * (s * (1.0 + p * (1.0 - s)))).astype(BF)
        dy = d * (p * s)
        head_dgain = head_dgain + jnp.sum(dy * n, axis=0, keepdims=True)
        dn = dy * gain[...]
        dout[x] = scale * r * (dn - n * jnp.mean(n * dn, axis=-1, keepdims=True))
    dgain[0:1, :] += head_dgain
    dob = {x: dout[x].astype(BF) for x in at}
    krem = {x: rem[x] * k[x] for x in at}
    dfresh_own = {x: mm(scores[x], dob[x], TN) for x in at}
    dscore = {x: mm(dob[x], fb[x], NT) for x in at}
    ds_next, dsb, dr, dx, dx_do = {}, {}, {}, {}, {}
    ds = [dstate[h] for h in hs]
    for j in reversed(range(BACK_STEP)):
        for h in hs:
            ds_next[j, h] = ds[h]
            dsb[j, h] = ds[h].astype(BF)
        dfresh = [dfresh_own[j, h] + mm(krem[j, h], dsb[j, h]) for h in hs]
        for h in hs:
            dr[j, h] = mm(tb[j, h], dfresh[h], TN)
        for h in hs:
            dx[j, h] = kbeta[j, h] * dr[j, h]
            dx_do[j, h] = jnp.concatenate([-dx[j, h], dout[j, h]], axis=0).astype(BF)
        ds = [last[j, h] * ds[h] + mm(gk_gq[j, h], dx_do[j, h], TN) for h in hs]
    for h in hs:
        dstate[h] = ds[h]
    dgk_gq = {x: mm(dx_do[x], sb[x], NT) for x in at}
    dkrem = {x: mm(fb[x], dsb[x], NT) for x in at}
    dlow = {x: jnp.where(row > col, -mm(dr[x], fb[x], NT), 0.0) for x in at}
    dcum = [jnp.zeros((CHUNK, CHUNK), F32) for _ in range(BACK_STEP)]
    dcum_rows = [jnp.zeros((CHUNK, CHUNK), F32) for _ in range(BACK_STEP)]
    dbeta = [jnp.zeros((CHUNK, CHUNK), F32) for _ in range(BACK_STEP)]
    for x in at:
        j, h = x
        m = dscore[x] * within[x]
        dgram = kbeta[x] * (dlow[x] * within[x])
        lg = dlow[x] * gram[x]
        e = dscore[x] * scores[x] + kbeta[x] * lg
        dq = gamma[x] * dgk_gq[x][CHUNK:] + mm(m, kb[x])
        mk = jnp.concatenate([m, dgram], axis=0)
        dk = (
            gamma[x] * dgk_gq[x][:CHUNK]
            + rem[x] * dkrem[x]
            + mm(mk, jnp.concatenate([qb[x], kb[x]], axis=0), TN)
            + mm(dgram, kb[x])
        )
        rem_part = jnp.sum(dkrem[x] * krem[x], axis=-1, keepdims=True)
        head_dcum = (
            jnp.sum(e, axis=-1, keepdims=True)
            + jnp.sum(
                dgk_gq[x][:CHUNK] * gk_gq[x][:CHUNK] + dgk_gq[x][CHUNK:] * gk_gq[x][CHUNK:],
                axis=-1, keepdims=True,
            )
            - rem_part
        )
        state_part = jnp.sum(
            jnp.sum(ds_next[x] * sb[x].astype(F32), axis=0, keepdims=True), axis=1, keepdims=True
        )
        end_part = jnp.sum(rem_part, axis=0, keepdims=True) + last[x] * state_part
        head_dcum = head_dcum + jnp.where(row[:, 0:1] == CHUNK - 1, end_part, 0.0)
        dcum[j] = dcum[j] + jnp.where(lane == h, head_dcum, 0.0)
        dcum_rows[j] = dcum_rows[j] + jnp.where(
            row == h, jnp.sum(e, axis=0, keepdims=True), 0.0
        )
        head_dbeta = jnp.sum(dr[x] * x_in[x], axis=-1, keepdims=True) + jnp.sum(
            lg, axis=-1, keepdims=True
        )
        dbeta[j] = dbeta[j] + jnp.where(lane == heads + h, head_dbeta, 0.0)
        da = rq[x] * (dq - q[x] * jnp.sum(q[x] * dq, axis=-1, keepdims=True))
        eq[lines[j], ks[h]] = da * sq[x]
        da = rk[x] * (dk - k[x] * jnp.sum(k[x] * dk, axis=-1, keepdims=True))
        ek[lines[j], ks[h]] = da * sk[x]
        ev[lines[j], vs[h]] = dx[x] * sv[x]
    for j in range(BACK_STEP):
        dg = exact((row >= col).astype(F32), dcum[j] - dcum_rows[j].T, TN)
        dshift = dg * rates[...] * sigmoid(shifted[j])
        dsm[0:1, :] += jnp.sum(dg * g[j], axis=0, keepdims=True)
        dsm[1:2, :] += jnp.sum(dshift, axis=0, keepdims=True)
        gqks[0, lines[j], 2 * heads * DK :] = (
            jnp.where(lane < heads, dshift, 0.0) + dbeta[j] * betas[j] * (1.0 - betas[j])
        ).astype(BF)
    for b, e, taps, dtaps, out_ref, start in (
        (bq, eq, cq, dcq, gqks, 0), (bk, ek, ck, dck, gqks, heads * DK), (bv, ev, cv, dcv, gvg, 0),
    ):
        for first in range(0, b.shape[1], DK):
            sl = slice(first, first + DK)
            own = e[0:span, sl]
            total = taps[3:4, sl] * own
            for i in range(3):
                total = total + taps[i : i + 1, sl] * e[3 - i : 3 - i + span, sl]
            out_ref[0, :, start + first : start + first + DK] = total.astype(BF)
            for i in range(4):
                dtaps[i : i + 1, sl] += jnp.sum(
                    own * b[5 + i : 5 + i + span, sl], axis=0, keepdims=True
                )


def whole_spec(shape):
    return pl.BlockSpec(shape, lambda r, c: (0,) * len(shape))


def lane_pad(vec, at):
    return jnp.zeros((1, 128), F32).at[0, at : at + vec.shape[0]].set(vec)


def mixer_forward(pqks, pvg, cq, ck, cv, log_rates, rate_bias, gain):
    rows, length, value_width = pvg.shape
    value_width = value_width // 2
    key_width = value_width * DK // DV
    heads = key_width // DK
    chunks = length // CHUNK
    span = STEP * CHUNK
    seq = lambda width, at=0: pl.BlockSpec((1, span, width), lambda r, c: (r, c, at))
    per = lambda a, b: pl.BlockSpec((1, STEP, heads, a, b), lambda r, c: (r, c, 0, 0, 0))
    return pl.pallas_call(
        functools.partial(mixer_forward_kernel, heads),
        grid=(rows, chunks // STEP),
        in_specs=[seq(key_width), seq(key_width, 1), seq(value_width), seq(value_width, 1),
                  seq(128, 2 * heads),
                  whole_spec((4, key_width)), whole_spec((4, key_width)), whole_spec((4, value_width)),
                  whole_spec((1, 128)), whole_spec((1, 128)), whole_spec((1, DV))],
        out_specs=[seq(value_width), per(CHUNK, CHUNK), per(DK, DV), seq(value_width)],
        out_shape=[
            jax.ShapeDtypeStruct((rows, length, value_width), BF),
            jax.ShapeDtypeStruct((rows, chunks, heads, CHUNK, CHUNK), BF),
            jax.ShapeDtypeStruct((rows, chunks, heads, DK, DV), BF),
            jax.ShapeDtypeStruct((rows, length, value_width), BF),
        ],
        scratch_shapes=[
            pltpu.VMEM((span + 8, key_width), F32),
            pltpu.VMEM((span + 8, key_width), F32),
            pltpu.VMEM((span + 8, value_width), F32),
            pltpu.VMEM((heads, DK, DV), F32),
        ],
        compiler_params=pltpu.CompilerParams(
            dimension_semantics=("arbitrary", "arbitrary"), vmem_limit_bytes=40 << 20
        ),
        cost_estimate=pl.CostEstimate(flops=0, bytes_accessed=int(rows * chunks * heads * 3007812.5), transcendentals=0),
        name="mixer_forward",
    )(pqks, pqks, pvg, pvg, pqks, cq, ck, cv, lane_pad(-jnp.exp(log_rates), 0),
      lane_pad(rate_bias, 0), gain.reshape(1, DV))


def mixer_backward(dm, pqks, pvg, cq, ck, cv, log_rates, rate_bias, gain, t_in, s_in, f_in):
    rows, length, value_width = dm.shape
    key_width = value_width * DK // DV
    heads = key_width // DK
    chunks = length // CHUNK
    span = BACK_STEP * CHUNK
    steps = chunks // BACK_STEP
    seq = lambda width, at=0: pl.BlockSpec(
        (1, span, width), lambda r, c: (r, steps - 1 - c, at)
    )
    before = lambda width, at=0: pl.BlockSpec(
        (1, 8, width),
        lambda r, c: (r, jnp.maximum((steps - 1 - c) * (span // 8) - 1, 0), at),
    )
    per = lambda a, b: pl.BlockSpec(
        (1, BACK_STEP, heads, a, b), lambda r, c: (r, steps - 1 - c, 0, 0, 0)
    )
    seq_shape = lambda width: jax.ShapeDtypeStruct((rows, length, width), BF)
    return pl.pallas_call(
        functools.partial(mixer_backward_kernel, heads),
        grid=(rows, steps),
        in_specs=[seq(value_width), seq(key_width), seq(key_width, 1), seq(value_width),
                  seq(value_width, 1), seq(128, 2 * heads),
                  before(key_width), before(key_width, 1), before(value_width),
                  whole_spec((4, key_width)), whole_spec((4, key_width)), whole_spec((4, value_width)),
                  whole_spec((1, 128)), whole_spec((1, 128)), whole_spec((1, DV)),
                  per(CHUNK, CHUNK), per(DK, DV), seq(value_width)],
        out_specs=[seq(2 * key_width + 128), seq(2 * value_width),
                   whole_spec((8, key_width)), whole_spec((8, key_width)), whole_spec((8, value_width)),
                   whole_spec((8, 128)), whole_spec((8, DV))],
        out_shape=[seq_shape(2 * key_width + 128), seq_shape(2 * value_width),
                   jax.ShapeDtypeStruct((8, key_width), F32),
                   jax.ShapeDtypeStruct((8, key_width), F32),
                   jax.ShapeDtypeStruct((8, value_width), F32),
                   jax.ShapeDtypeStruct((8, 128), F32),
                   jax.ShapeDtypeStruct((8, DV), F32)],
        scratch_shapes=[
            pltpu.VMEM((span + 8, key_width), F32),
            pltpu.VMEM((span + 8, key_width), F32),
            pltpu.VMEM((span + 8, value_width), F32),
            pltpu.VMEM((span + 8, key_width), F32),
            pltpu.VMEM((span + 8, key_width), F32),
            pltpu.VMEM((span + 8, value_width), F32),
            pltpu.VMEM((heads, DK, DV), F32),
        ],
        compiler_params=pltpu.CompilerParams(
            dimension_semantics=("arbitrary", "arbitrary"), vmem_limit_bytes=48 << 20
        ),
        cost_estimate=pl.CostEstimate(flops=0, bytes_accessed=int(rows * chunks * heads * 4921875.0), transcendentals=0),
        name="mixer_backward",
    )(dm, pqks, pqks, pvg, pvg, pqks, pqks, pqks, pvg, cq, ck, cv, lane_pad(-jnp.exp(log_rates), 0),
      lane_pad(rate_bias, 0), gain.reshape(1, DV), t_in, s_in, f_in)


FREE = pl.CostEstimate(flops=0, bytes_accessed=0, transcendentals=0)
VMEM_LIMIT = 44 << 20
WIDE_LIMIT = 58 << 20
SMALL_LIMIT = 16 << 20


def rows_kernel(count, nt, has_weigh, at, *refs):
    out = refs[-2] if has_weigh else refs[-1]
    total = None
    for i in range(count):
        part = lax.dot_general(
            refs[2 * i][0], refs[2 * i + 1][...], NT if nt else NN, preferred_element_type=F32
        )
        total = part if total is None else total + part
    if has_weigh:
        refs[-1][0, 0:1, :] = jnp.sum(
            total * refs[2 * count][0].astype(F32), axis=0, keepdims=True
        )
    out[0] = total.astype(out.dtype)


def rows_matmul(
    pairs, piece, nt=False, tile=512, take=0, weigh=None, into=None, put=0, dtype=BF, limit=WIDE_LIMIT
):
    rows = pairs[0][0].shape[0]
    width = pairs[0][1].shape[0 if nt else 1]
    tile = min(tile, width)
    at = jnp.stack([jnp.int32(take), jnp.int32(put)])
    specs, args = [], []
    for a, w in pairs:
        depth = a.shape[2]
        specs.append(pl.BlockSpec((1, piece, depth), lambda r, n, at: (r, at[0], 0)))
        if nt:
            specs.append(pl.BlockSpec((tile, depth), lambda r, n, at: (n, 0)))
        else:
            specs.append(pl.BlockSpec((depth, tile), lambda r, n, at: (0, n)))
        args.extend((a, w))
    if weigh is not None:
        specs.append(pl.BlockSpec((1, piece, tile), lambda r, n, at: (r, 0, n)))
        args.append(weigh)
    aliases = {}
    shape = (rows, piece, width)
    if into is not None:
        shape = into.shape
        dtype = into.dtype
        if not isinstance(into, jax.ShapeDtypeStruct):
            specs.append(pl.BlockSpec(memory_space=pl.ANY))
            args.append(into)
            aliases = {len(args): 0}
    out_specs = [pl.BlockSpec((1, piece, tile), lambda r, n, at: (r, at[1], n))]
    out_shape = [jax.ShapeDtypeStruct(shape, dtype)]
    if weigh is not None:
        out_specs.append(pl.BlockSpec((1, 8, tile), lambda r, n, at: (r, 0, n)))
        out_shape.append(jax.ShapeDtypeStruct((rows, 8, width), F32))
    out = pl.pallas_call(
        functools.partial(rows_kernel, len(pairs), nt, weigh is not None),
        grid_spec=pltpu.PrefetchScalarGridSpec(
            num_scalar_prefetch=1,
            grid=(rows, pl.cdiv(width, tile)),
            in_specs=specs,
            out_specs=out_specs,
        ),
        out_shape=out_shape,
        input_output_aliases=aliases,
        compiler_params=pltpu.CompilerParams(
            dimension_semantics=("arbitrary", "arbitrary"), vmem_limit_bytes=limit
        ),
        cost_estimate=FREE,
        name="rows_matmul",
    )(at, *args)
    return out[0] if weigh is None else (out[0], jnp.sum(out[1][:, 0:1], axis=0))


def outer_kernel(count, blocks, groups, parts, at, *refs):
    xs, gs = refs[:count], refs[count : 2 * count]
    extras = list(refs[2 * count : -1 - parts])
    outs, flipped = refs[-1 - parts : -1], refs[-1]
    rows, piece, width = xs[0].shape
    depth = rows * piece
    block = flipped.shape[0] // blocks

    @pl.when(pl.program_id(0) == 0)
    def _():
        for i, x in enumerate(xs):
            for k in range(blocks):
                start = pl.multiple_of((2 * k + at[0]) * block, block)
                part = x[:, :, pl.ds(start, block)].reshape(depth, block)
                flipped[k * block : (k + 1) * block, i * depth : (i + 1) * depth] = part.T

    total = None
    for i, g in enumerate(gs):
        part = lax.dot_general(
            flipped[:, i * depth : (i + 1) * depth],
            g[...].reshape(depth, g.shape[2]),
            NN,
            preferred_element_type=F32,
        )
        total = part if total is None else total + part
    for size in groups:
        held, extras = extras[:size], extras[size:]
        total = total + jnp.concatenate([x[...].astype(F32) for x in held], axis=0)
    lines = total.shape[0] // parts
    for i, out in enumerate(outs):
        out[...] = total[i * lines : (i + 1) * lines].astype(out.dtype)


def outer_sum(xs, gs, places, core, data, tile=512, adds=(), dtype=BF, parts=1):
    rows, piece, width = xs[0].shape
    columns = gs[0].shape[2]
    tile = min(tile, columns)
    at = jnp.stack([jnp.int32(core)] + [jnp.int32(x) for x in places])
    whole = pl.BlockSpec(
        (rows, piece, width), lambda n, at: (0, 0, 0), pipeline_mode=pl.Buffered(1)
    )
    specs = [whole] * len(xs)
    for i in range(len(gs)):
        specs.append(
            pl.BlockSpec((rows, piece, tile), lambda n, at, i=i: (0, at[1 + i], n))
        )
    args = [*xs, *gs]
    lines = lambda count: pl.BlockSpec((width // 2 // count, tile), lambda n, at: (0, n))
    for group in adds:
        specs.extend([lines(len(group))] * len(group))
        args.extend(group)
    return pl.pallas_call(
        functools.partial(outer_kernel, len(xs), data // 2, [len(x) for x in adds], parts),
        grid_spec=pltpu.PrefetchScalarGridSpec(
            num_scalar_prefetch=1,
            grid=(columns // tile,),
            in_specs=specs,
            out_specs=[lines(parts)] * parts,
            scratch_shapes=[pltpu.VMEM((width // 2, len(xs) * rows * piece), BF)],
        ),
        out_shape=[jax.ShapeDtypeStruct((width // 2 // parts, columns), dtype)] * parts,
        compiler_params=pltpu.CompilerParams(
            dimension_semantics=("arbitrary",), vmem_limit_bytes=VMEM_LIMIT
        ),
        cost_estimate=FREE,
        name="outer_sum",
    )(at, *args)


UNITS = 512


def lanes_of(units):
    return 128 if units % 128 == 0 else 64


def mlp_kernel(lanes, x, wgu, back, hidden, grads):
    both = lax.dot_general(x[...], wgu[...], NN, preferred_element_type=F32)
    for at in range(0, UNITS, lanes):
        first, second = 2 * at, 2 * at + lanes
        gate = both[:, first : first + lanes]
        up = both[:, second : second + lanes]
        own = back[:, at : at + lanes]
        sig = sigmoid(gate)
        act = gate * sig
        hidden[:, at : at + lanes] = (act * up).astype(BF)
        own_gate = own * up * (sig * (1.0 + gate * (1.0 - sig)))
        grads[:, first : first + lanes] = own_gate.astype(BF)
        grads[:, second : second + lanes] = (own * act).astype(BF)


def mlp_block(x, wgu, back):
    piece, width = x.shape
    units = back.shape[1]
    part = lambda depth, size: pl.BlockSpec((depth, size), lambda n: (0, n))
    return pl.pallas_call(
        functools.partial(mlp_kernel, lanes_of(units)),
        grid=(pl.cdiv(units, UNITS),),
        in_specs=[
            pl.BlockSpec((piece, width), lambda n: (0, 0)),
            part(width, 2 * UNITS),
            part(piece, UNITS),
        ],
        out_specs=[part(piece, UNITS), part(piece, 2 * UNITS)],
        out_shape=[
            jax.ShapeDtypeStruct((piece, units), BF),
            jax.ShapeDtypeStruct((piece, 2 * units), BF),
        ],
        compiler_params=pltpu.CompilerParams(
            dimension_semantics=("arbitrary",), vmem_limit_bytes=WIDE_LIMIT
        ),
        cost_estimate=FREE,
        name="mlp_block",
    )(x, wgu, back)


NORM_ROWS = 128


def row_stats(x):
    r = lax.rsqrt(jnp.mean(x * x, axis=-1, keepdims=True) + NORM_EPS)
    return x * r, r


def norm_grad(n, r, inner):
    return r * (inner - n * jnp.mean(n * inner, axis=-1, keepdims=True))


def valid_rows(at):
    start = at[0] + pl.program_id(1) * NORM_ROWS
    positions = start + lax.broadcasted_iota(jnp.int32, (NORM_ROWS, 1), 0)
    return (positions < at[1 + pl.program_id(0)]).astype(F32)


def enter_kernel(at, tokens, gain, normed):
    normed[0] = (row_stats(tokens[0].astype(F32))[0] * gain[...]).astype(BF)


def middle_kernel(at, own, moved, tokens, gain, middle, normed):
    total = own[0] + moved[0].astype(F32)
    x = tokens[0].astype(F32) + valid_rows(at) * total
    middle[0] = x
    normed[0] = (row_stats(x)[0] * gain[...]).astype(BF)


def middle_back_kernel(at, own, moved, middle, cot, gain, grad_middle, grad_attn, dgain):
    @pl.when((pl.program_id(0) == 0) & (pl.program_id(1) == 0))
    def _():
        dgain[...] = jnp.zeros_like(dgain)

    grad = own[0] + moved[0].astype(F32)
    n, r = row_stats(middle[0])
    dgain[0:1, :] += jnp.sum(grad * n, axis=0, keepdims=True)
    total = cot[0].astype(F32) + norm_grad(n, r, gain[...] * grad)
    grad_middle[0] = total
    grad_attn[0] = (valid_rows(at) * total).astype(BF)


def leave_kernel(at, own, moved, tokens, grad_middle, gain, out):
    grad = own[0] + moved[0].astype(F32)
    n, r = row_stats(tokens[0].astype(F32))
    out[0] = (grad_middle[0] + norm_grad(n, r, gain[...] * grad)).astype(BF)


def result_kernel(at, own, moved, middle, out):
    total = own[0] + moved[0].astype(F32)
    out[0] = (middle[0] + valid_rows(at) * total).astype(BF)


def by_rows(kernel, at, arrays, gain, out_types, with_sum=False, limit=SMALL_LIMIT, cost=FREE):
    rows, piece, width = arrays[0].shape
    block = pl.BlockSpec((1, NORM_ROWS, width), lambda r, t, at: (r, t, 0))
    out_shape = [jax.ShapeDtypeStruct((rows, piece, width), x) for x in out_types]
    out_specs = [block] * len(out_types)
    specs = [block] * len(arrays)
    args = list(arrays)
    if gain is not None:
        specs.append(pl.BlockSpec((1, width), lambda r, t, at: (0, 0)))
        args.append(gain.reshape(1, width))
    if with_sum:
        out_shape.append(jax.ShapeDtypeStruct((8, width), F32))
        out_specs.append(pl.BlockSpec((8, width), lambda r, t, at: (0, 0)))
    return pl.pallas_call(
        kernel,
        grid_spec=pltpu.PrefetchScalarGridSpec(
            num_scalar_prefetch=1,
            grid=(rows, piece // NORM_ROWS),
            in_specs=specs,
            out_specs=out_specs,
        ),
        out_shape=out_shape,
        compiler_params=pltpu.CompilerParams(
            dimension_semantics=("arbitrary", "arbitrary"), vmem_limit_bytes=limit
        ),
        cost_estimate=cost,
        name=kernel.__name__,
    )(at, *args)


def apart_kernel(lanes, gu, gu_moved, down, down_moved, gate, up, out):
    out[...] = down[...].astype(F32) + down_moved[...].astype(F32)
    for at in range(0, gate.shape[1], lanes):
        for first, half in ((2 * at, gate), (2 * at + lanes, up)):
            half[:, at : at + lanes] = gu[:, first : first + lanes].astype(F32) + gu_moved[
                :, first : first + lanes
            ].astype(F32)


def apart(gu, gu_moved, down, down_moved):
    shape = jax.ShapeDtypeStruct(down.shape, F32)
    return pl.pallas_call(
        functools.partial(apart_kernel, lanes_of(down.shape[1])),
        out_shape=[shape, shape, shape],
        compiler_params=pltpu.CompilerParams(vmem_limit_bytes=SMALL_LIMIT),
        cost_estimate=FREE,
        name="apart",
    )(gu, gu_moved, down, down_moved)


def ring(size, group):
    return [(i, i // group * group + (i + 1) % group) for i in range(size)]


def across(size):
    return [(i, (i + size // 2) % size) for i in range(size)]


def swap(size, bit):
    return [(i, i ^ bit) for i in range(size)]


def tie(*values):
    return lax.optimization_barrier(values)


def matmul(a, b):
    return lax.dot_general(a, b, NN, preferred_element_type=F32)


def sum_over(x, axis, size):
    bit = 1
    while bit < size:
        x = x + lax.ppermute(x, axis, swap(size, bit))
        bit = bit * 2
    return x


def alternate(gate, up):
    units = gate.shape[1]
    lanes = lanes_of(units)
    parts = [x[:, at : at + lanes] for at in range(0, units, lanes) for x in (gate, up)]
    return jnp.concatenate(parts, axis=1)


def per_device(
    tokens,
    lengths,
    gain_attn,
    w_query,
    w_key,
    w_value,
    w_decay,
    w_beta,
    w_gate_out,
    conv_query,
    conv_key,
    conv_value,
    decay_log,
    decay_bias,
    gain_head,
    w_out,
    gain_mlp,
    w_gate,
    w_up,
    w_down,
    cotangent,
):
    rows, piece, width = tokens.shape
    size = lax.axis_size("head")
    data = lax.axis_size("dp")
    me = lax.axis_index("head")
    core = lax.rem(lax.axis_index("dp"), 2)
    length = piece * size
    heads = w_decay.shape[1]
    key_width, value_width = heads * DK, heads * DV
    shape3 = (rows, piece, width)
    flat_piece = rows * piece
    group = size // 2
    at = jnp.concatenate([(me * piece).astype(jnp.int32)[None], lengths])
    positions = me * piece + jnp.arange(piece, dtype=jnp.int32)
    mask = (positions[None, :] < lengths[:, None]).astype(F32)[:, :, None]

    def owner(s):
        return lax.rem(me + size - s, size)

    def step(x, group):
        return lax.ppermute(x, "head", ring(size, group))

    def opposite(x):
        return lax.ppermute(x, "head", across(size))

    def gather_weight(w):
        return lax.all_gather(w, "dp", axis=0, tiled=True)

    def cross(parts):
        return [lax.ppermute(x, "dp", swap(data, 1)) for x in parts]

    def outer_halves(xs, gs, places, tile=512, parts=2, away=(), near=()):
        away = outer_sum(xs, gs, places, 1 - core, data, tile, away, parts=parts)
        return outer_sum(xs, gs, places, core, data, tile, [cross(away), *near])[0]

    def scatter_weight(total):
        places = [[i + c for i in range(0, data, 2)] for c in range(2)]
        return lax.psum_scatter(
            total, "dp", scatter_dimension=0, tiled=True, axis_index_groups=places
        )

    normed = by_rows(enter_kernel, at, [tokens], gain_attn, [BF])[0]
    normed, w_query = tie(normed, w_query)
    small_pad = jnp.zeros((w_decay.shape[0], 128 - 2 * heads), BF)
    w_qks = gather_weight(jnp.concatenate([w_query, w_key, w_decay, w_beta, small_pad], axis=1))
    w_vg = gather_weight(jnp.concatenate([w_value, w_gate_out], axis=1))
    wo_full = gather_weight(w_out)

    qks_buffer = jax.ShapeDtypeStruct((rows, length, 2 * key_width + 128), F32)
    vg_buffer = jax.ShapeDtypeStruct((rows, length, 2 * value_width), F32)
    def project_qks(item, s, into):
        return rows_matmul([(item, w_qks)], piece, tile=into.shape[2], into=into, put=owner(s))

    def project_vg(item, s, into):
        return rows_matmul([(item, w_vg)], piece, into=into, put=owner(s))

    pqks = project_qks(normed, 0, qks_buffer)
    pvg = vg_buffer
    pieces = [normed]
    for s in range(1, size):
        send = pieces[-1]
        if s == 1:
            send, w_gate, w_up, cotangent = tie(send, w_gate, w_up, cotangent)
        item = step(send, size)
        if s == 1:
            w_gu = alternate(w_gate, w_up)
            grad_mlp = (mask * cotangent.astype(F32)).astype(BF)
            item, w_gu, grad_mlp = tie(item, w_gu, grad_mlp)
        if s == size - 1:
            for place, early in enumerate(pieces):
                pvg = project_vg(early, place, pvg)
            item, pqks, pvg, w_gu, w_down, grad_mlp = tie(
                item, pqks, pvg, w_gu, w_down, grad_mlp
            )
        elif s > 1:
            item, pqks = tie(item, pqks)
        pqks = project_qks(item, s, pqks)
        pieces.append(item)
    normed_pieces = pieces
    w_gu_other = opposite(w_gu)
    w_down_other = opposite(w_down)
    grad_out = [grad_mlp]
    for _ in range(1, group):
        grad_out.append(step(grad_out[-1], group))
    pvg = project_vg(item, size - 1, pvg)

    cq = lax.dynamic_slice_in_dim(conv_query, me * key_width, key_width, 1)
    ck = lax.dynamic_slice_in_dim(conv_key, me * key_width, key_width, 1)
    cv = lax.dynamic_slice_in_dim(conv_value, me * value_width, value_width, 1)
    log_local = lax.dynamic_slice_in_dim(decay_log, me * heads, heads, 0)
    bias_local = lax.dynamic_slice_in_dim(decay_bias, me * heads, heads, 0)
    mixed, t_kept, s_kept, f_kept = mixer_forward(
        pqks, pvg, cq, ck, cv, log_local, bias_local, gain_head
    )
    mixed, w_gu_other, w_down_other, *grad_out = tie(mixed, w_gu_other, w_down_other, *grad_out)
    wgu_full = [gather_weight(w_gu), gather_weight(w_gu_other)]
    wdown_full = [gather_weight(w_down), gather_weight(w_down_other)]

    def attn_part(s, dtype=F32, limit=VMEM_LIMIT):
        return rows_matmul(
            [(mixed, wo_full)], piece, nt=True, take=owner(s), dtype=dtype, limit=limit
        )

    def back_parts(b):
        return [
            rows_matmul([(g, wdown_full[b])], piece, tile=768, dtype=F32, limit=VMEM_LIMIT)
            for g in grad_out
        ]

    back = [None, None]
    total = attn_part(1, BF, WIDE_LIMIT)
    for s in range(2, size + 1):
        moved = step(total, size)
        own = attn_part(s % size)
        if s == size - 1:
            moved, own, wgu_full[0], *back[0] = tie(moved, own, wgu_full[0], *back_parts(0))
        elif s == size:
            moved, own, *back[1] = tie(moved, own, *back_parts(1))
        else:
            moved, own = tie(moved, own)
        total = (own + moved.astype(F32)).astype(BF)
    middle, normed_two = by_rows(middle_kernel, at, [own, moved, tokens], gain_mlp, [F32, BF])
    flat2 = lambda x: x.reshape(flat_piece, width)
    flat_units = lambda x: x.reshape(flat_piece, x.shape[2])
    second = [normed_two]
    hidden, grad_gu = [[], []], [[], []]

    def keep_block(b, block):
        hidden[b].append(block[0].reshape(rows, piece, -1))
        grad_gu[b].append(block[1].reshape(rows, piece, -1))

    def mlp_part(s, dtype=F32):
        pairs = [(hidden[b][s], wdown_full[b]) for b in range(2)]
        return rows_matmul(pairs, piece, nt=True, dtype=dtype)

    def two_part(s, dtype=F32):
        pairs = [(grad_gu[b][s], wgu_full[b]) for b in range(2)]
        return rows_matmul(pairs, piece, nt=True, dtype=dtype)

    send, own_x = tie(normed_two, normed_two)
    for s in range(1, group):
        moved = step(send, group)
        if s == 1:
            for b in range(2):
                keep_block(b, mlp_block(flat2(own_x), wgu_full[b], flat_units(back[b][0])))
            own_two = two_part(0)
            moved, own_two, *held = tie(moved, own_two, *hidden[0], *hidden[1], *grad_gu[0], *grad_gu[1])
            hidden, grad_gu = [held[:1], held[1:2]], [held[2:3], held[3:]]
        second.append(moved)
        send = moved
    for s in range(1, group):
        for b in range(2):
            keep_block(b, mlp_block(flat2(second[s]), wgu_full[b], flat_units(back[b][s])))
    first = [0] * group
    units = hidden[0][0].shape[2]

    def away_pair(b):
        return (
            outer_sum(second, grad_gu[b], first, 1 - core, data, 1408),
            outer_sum(grad_out, hidden[b], first, 1 - core, data, units),
        )

    def near_pair(b, parts):
        return (
            outer_sum(second, grad_gu[b], first, core, data, 1408, [cross(parts[:1])])[0],
            outer_sum(grad_out, hidden[b], first, core, data, units, [cross(parts[1:])])[0],
        )

    total = two_part(1, BF)
    total, *held = tie(total, *hidden[0], *hidden[1], *grad_gu[1])
    hidden, grad_gu[1] = [held[:group], held[group : 2 * group]], held[2 * group :]
    for s in range(2, group + 1):
        moved = step(total, group)
        if s == group:
            own = own_two
            own_mlp, send_mlp = mlp_part(0), mlp_part(1, BF)
            away_gu, away_down = away_pair(1)
            moved, own_mlp, send_mlp, *away = tie(
                moved, own_mlp, send_mlp, *away_gu, *away_down
            )
        else:
            own = two_part(s)
            total = (own + moved.astype(F32)).astype(BF)
    grad_middle, grad_attn, dgain_mlp = by_rows(
        middle_back_kernel, at, [own, moved, middle, cotangent], gain_mlp, [F32, BF], True, WIDE_LIMIT
    )

    pair_gu, pair_down = [None, None], [None, None]
    mixed_buffer = jax.ShapeDtypeStruct((rows, length, value_width), F32)
    grad_mixed = mixed_buffer
    attn_pieces = [grad_attn]
    for s in range(1, size):
        send = attn_pieces[-1]
        if s == 1:
            send, *held = tie(send, *away, *hidden[0], *grad_gu[0])
            away, hidden[0], grad_gu[0] = held[:2], held[2 : 2 + group], held[2 + group :]
        elif s == 2:
            send, *away = tie(send, *away)
        item = step(send, size)
        if s == 1:
            pair_gu[1], pair_down[1] = near_pair(1, away)
            away_gu, away_down = away_pair(0)
            item, pair_gu[1], pair_down[1], *away = tie(
                item, pair_gu[1], pair_down[1], *away_gu, *away_down
            )
        elif s == 2:
            pair_gu[0], pair_down[0] = near_pair(0, away)
            item, pair_gu[0], pair_down[0] = tie(item, pair_gu[0], pair_down[0])
        if s == size - 1:
            for place, early in enumerate(attn_pieces):
                grad_mixed = rows_matmul(
                    [(early, wo_full)], piece, into=grad_mixed, put=owner(place)
                )
            wout_parts = [
                outer_sum(
                    attn_pieces, [mixed] * s, [owner(x) for x in range(s)], side, data, dtype=F32
                )[0]
                for side in (1 - core, core)
            ]
            item, grad_mixed, *wout_parts = tie(item, grad_mixed, *wout_parts)
        attn_pieces.append(item)
    grad_mixed = rows_matmul(
        [(item, wo_full)], piece, into=grad_mixed, put=owner(size - 1), limit=VMEM_LIMIT
    )
    sums_gu = [None, scatter_weight(pair_gu[1])]
    sums_down = [None, scatter_weight(pair_down[1])]
    sums_gu[0] = scatter_weight(pair_gu[0])
    sums_down[0] = scatter_weight(pair_down[0])

    grad_mixed, send_mlp, send_gu, send_down = tie(grad_mixed, send_mlp, sums_gu[1], sums_down[1])
    moved = step(send_mlp, group)
    moved_gu, moved_down = opposite(send_gu), opposite(send_down)
    done = mixer_backward(
        grad_mixed, pqks, pvg, cq, ck, cv, log_local, bias_local, gain_head, t_kept, s_kept, f_kept
    )
    moved, moved_gu, moved_down, gqks, gvg, dcq, dck, dcv, dsm, dgain = tie(
        moved, moved_gu, moved_down, *done
    )
    for s in range(2, group):
        moved = step((mlp_part(s) + moved.astype(F32)).astype(BF), group)
    moved_mlp = moved

    def one_part(s, dtype=F32):
        return rows_matmul(
            [(gqks, w_qks), (gvg, w_vg)], piece, nt=True, take=owner(s),
            weigh=normed_pieces[s], dtype=dtype,
        )

    places = [owner(s) for s in range(size)]
    total, gain_sum = one_part(1, BF)
    for s in range(2, size + 1):
        if s == 3:
            total, attn_last, *last = tie(total, attn_pieces[-1], sums_down[0], sums_gu[0])
            sums_down[0], sums_gu[0] = last
        total, gqks, gvg = tie(total, gqks, gvg)
        if s == size:
            total, pair_qks, pair_wout = tie(total, pair_qks, pair_wout)
            pair_last = jnp.concatenate([pair_qks, pair_wout], axis=1)
            total, moved_mlp, sums_gu[0], sums_down[0], moved_gu, moved_down, *small = tie(
                total, moved_mlp, sums_gu[0], sums_down[0], moved_gu, moved_down,
                dcq, dck, dcv, dsm, dgain, dgain_mlp,
            )
        moved = step(total, size)
        if s < size:
            own, gain_part = one_part(s, BF)
            gain_sum = gain_sum + gain_part
        if s == 2:
            pair_vg = outer_halves(normed_pieces, [gvg] * size, places, 512, 4)
            moved, own, pair_vg = tie(moved, own, pair_vg)
        elif s == 3:
            pair_qks = outer_halves(normed_pieces, [gqks] * size, places, gqks.shape[2])
            pair_wout = outer_halves(
                [attn_last], [mixed], places[-1:], 512, 2, [wout_parts[:1]], [wout_parts[1:]]
            )
            moved, own, pair_qks, pair_wout, out_vg = tie(
                moved, own, pair_qks, pair_wout, scatter_weight(pair_vg)
            )
        if s < size:
            total = (own.astype(F32) + moved.astype(F32)).astype(BF)
            continue
        own, gain_part = one_part(0)
        small = jnp.concatenate(
            [x[:4] for x in small] + [jnp.broadcast_to(gain_sum + gain_part, (4, width))],
            axis=1,
        )
        small = sum_over(small, "dp", data)
        out_wgate, out_wup, out_wdown = apart(sums_gu[0], moved_gu, sums_down[0], moved_down)
        mixed_rows = by_rows(result_kernel, at, [own_mlp, moved_mlp, middle], None, [BF])[0]
        moved, own, small, out_wgate, out_wup, out_wdown, mixed_rows = tie(
            moved, own, small, out_wgate, out_wup, out_wdown, mixed_rows
        )
    leave_cost = pl.CostEstimate(flops=0, bytes_accessed=14 * tokens.size, transcendentals=0)
    tokens_grad = by_rows(
        leave_kernel, at, [own, moved, tokens, grad_middle], gain_attn, [BF], False, WIDE_LIMIT,
        leave_cost,
    )[0]
    out_vg = out_vg.astype(F32)
    out_last = scatter_weight(pair_last).astype(F32)
    out_qks, out_wout = out_last[:, : gqks.shape[2]], out_last[:, gqks.shape[2] :]

    taps_width = 2 * key_width + value_width
    own_width = taps_width + 128
    spread, line = small[:, :own_width], small[0:1, own_width:]
    bit = 1
    while bit < size:
        above = (me // bit) % 2 == 1
        crossed = lax.ppermute(spread, "head", swap(size, bit))
        line_crossed = lax.ppermute(line, "head", swap(size, bit))
        if bit == 1:
            crossed, line_crossed, tokens_grad = tie(crossed, line_crossed, tokens_grad)
        low = jnp.where(above, crossed, spread)
        high = jnp.where(above, spread, crossed)
        spread = jnp.concatenate([low, high], axis=1)
        line = line + line_crossed
        bit = bit * 2
    by_head = [spread[:, i * own_width : (i + 1) * own_width] for i in range(size)]
    taps = lambda start, stop: jnp.concatenate([x[:, start:stop] for x in by_head], axis=1)
    conv_sums = (
        taps(0, key_width),
        taps(key_width, 2 * key_width),
        taps(2 * key_width, taps_width),
    )
    decay_sums = [
        jnp.concatenate([x[i, taps_width : taps_width + heads] for x in by_head]) for i in range(2)
    ]
    gains = line[0]
    gain_head_out = gains[:DV]
    gain_mlp_out = gains[DV : DV + width]
    gain_attn_out = gains[DV + width :] / gain_attn
    return (
        mixed_rows,
        tokens_grad,
        gain_attn_out,
        out_qks[:, :key_width],
        out_qks[:, key_width : 2 * key_width],
        out_vg[:, :value_width],
        out_qks[:, 2 * key_width : 2 * key_width + heads],
        out_qks[:, 2 * key_width + heads : 2 * key_width + 2 * heads],
        out_vg[:, value_width:],
        conv_sums[0],
        conv_sums[1],
        conv_sums[2],
        decay_sums[0],
        decay_sums[1],
        gain_head_out,
        out_wout,
        gain_mlp_out,
        out_wgate,
        out_wup,
        out_wdown,
    )

def solution(mesh):
    rows = P("dp", "head", None)
    weight = P("dp", "head")
    same = P()
    return jax.shard_map(
        per_device,
        mesh=mesh,
        in_specs=(
            rows, P("dp"), same, weight, weight, weight, weight, weight, weight, same, same, same,
            same, same, same, weight, same, weight, weight, weight, rows,
        ),
        out_specs=(
            rows, rows, same, weight, weight, weight, weight, weight, weight, same, same, same,
            same, same, same, weight, same, weight, weight, weight,
        ),
        check_vma=False,
    )
```
